256 devices in a mesh: grp: 4 (over x), seq: 64 (over y, z, core).
Axes of the slice: x: 4, y: 4, z: 8, core: 2. Of those that a mesh axis runs over, the one named last changes fastest.
Arguments:
- tokens: bfloat16 [32768, 8192], P(('grp', 'seq')), may hold values from -6 to 6
- cotangent: bfloat16 [32768, 1024], P(('grp', 'seq')), may hold values from -6 to 6
- frozen_weight: bfloat16 [8192, 1024], P('seq'), may hold values from -0.0625 to 0.0625
- adapters: bfloat16 [64, 9216, 64], P('grp', 'seq'), may hold values from -0.5 to 0.5
- tile_job: int32 [256, 1], replicated, may hold values from 0 to 63
- job_slot: int32 [64], replicated, may hold values from 0 to 63, each once
Outputs:
- keys: bfloat16 [32768, 1024], P(('grp', 'seq'))
- token_gradient: bfloat16 [32768, 8192], P(('grp', 'seq'))
- grad_adapters: float32 [64, 9216, 64], P('grp', 'seq')
The draws below stay inside these ranges and needn't reach their ends.
All inputs are finite; a program needn't handle non-finite values.
Results may differ from the reference program's by a relative error of at most 0.0029.
Values may be sent and summed in bfloat16 or wider, within the bound.
No kernel may reach another device: no remote copies, remote signals or barrier semaphores. Data moves between devices by JAX's collectives and lax.ppermute only.
A program may use at most 128 MiB of HBM per device.

```python
import jax
import jax.numpy as jnp
from jax import lax

D = 8192
KV = 1024
R = 64
TILE_ROWS = 128
JOBS = 64
TOKENS = 32768
TILES = 256


def draw_adapters(key, part):
    key = jax.random.fold_in(key, 7)
    shape = (JOBS, D + KV, R)
    rowpos = jnp.arange(D + KV)[None, :, None]
    spread = jnp.where(rowpos < D, D ** (-0.5), R ** (-0.5)).astype(jnp.float32)
    values = jax.random.truncated_normal(key, -4.0, 4.0, shape, jnp.float32)
    return jnp.clip(values * spread, -0.5, 0.5).astype(jnp.bfloat16)


def level_of(stream_key, dims, cuts, smallest, high):
    def one(dim, blocks):
        steps = jax.random.uniform(jax.random.fold_in(jax.random.fold_in(stream_key, 6), dim), (blocks,), jnp.float32, smallest / len(cuts), high / len(cuts))
        return jnp.repeat(jnp.exp(steps), dims[dim] // blocks).reshape((-1,) + (1,) * (len(dims) - dim - 1))

    gain = one(*cuts[0])
    for cut in cuts[1:]:
        gain = gain * one(*cut)
    return gain


def picks_of(stream_key, rows, count, top, lift):
    order = jax.random.permutation(jax.random.fold_in(stream_key, 1), count)
    boost = order
    for power in range(3):
        boost = boost * boost // count
    boost = boost * lift // count
    tickets = jax.random.randint(jax.random.fold_in(stream_key, 2), (rows, count), 0, 4096) + boost
    fixed_rows = jax.random.permutation(jax.random.fold_in(stream_key, 3), rows)[jnp.arange(count) % rows]
    tickets = jnp.where(jnp.arange(rows)[:, None] == fixed_rows[None, :], 1 << 14, tickets)
    merit = tickets * count + jnp.arange(count)
    return lax.top_k(merit.astype(jnp.int32), top)[1].astype(jnp.int32)


def bell_draw(stream_key, extent, width, limit, split=(), kind=jnp.bfloat16):
    factor_of = level_of(stream_key, extent, split, -0.22, 0.18) if split else 1.0
    entries = jax.random.normal(stream_key, extent, jnp.float32) * width * factor_of
    return jnp.minimum(jnp.maximum(entries, -limit), limit).astype(kind)


def setup_inputs(seed: int = 0) -> dict:
    seeds = jax.random.split(jax.random.key(seed), 7)
    tokens = bell_draw(seeds[0], (TOKENS, D), 1.0, 6.0, ((0, 256),))
    cotangent = bell_draw(seeds[1], (TOKENS, KV), 1.0, 6.0, ((0, 256),))
    frozen_weight = bell_draw(seeds[2], (D, KV), D ** -0.5, 0.0625, ((0, 64),))
    adapters = draw_adapters(jax.random.fold_in(seeds[6], 71), 0)
    tile_job = picks_of(seeds[4], TILES, JOBS, 1, 256)
    job_slot = jax.random.permutation(seeds[5], JOBS).astype(jnp.int32)
    return {"tokens": tokens, "cotangent": cotangent, "frozen_weight": frozen_weight, "adapters": adapters, "tile_job": tile_job, "job_slot": job_slot}


adapter_scale = 0.5


def reference(tokens, cotangent, frozen_weight, adapters, tile_job, job_slot):
    jobs = tile_job[:, 0]
    table = jnp.arange(JOBS, dtype=jnp.int32)
    slots = jnp.sum(jnp.where(jobs[:, None] == table[None, :], job_slot[None, :], 0), axis=1).astype(jnp.int32)
    token_tiles = tokens.reshape(TILES, TILE_ROWS, D)
    cot_tiles = cotangent.reshape(TILES, TILE_ROWS, KV)

    def step(grads, item):
        token_rows, output_gradients, slot = item
        adapter = lax.dynamic_index_in_dim(adapters, slot, 0, keepdims=False)
        down_weight = adapter[:D]
        up_weight = adapter[D:]
        base_weight = jnp.dot(token_rows, frozen_weight, preferred_element_type=jnp.float32)
        hidden_width = jnp.dot(token_rows, down_weight, preferred_element_type=jnp.float32).astype(jnp.bfloat16)
        adapter_weights = jnp.dot(hidden_width, up_weight.T, preferred_element_type=jnp.float32)
        keys = (base_weight + adapter_scale * adapter_weights).astype(jnp.bfloat16)
        backward_pass = jnp.dot(output_gradients, up_weight, preferred_element_type=jnp.float32).astype(jnp.bfloat16)
        input_gradient = jnp.dot(output_gradients, frozen_weight.T, preferred_element_type=jnp.float32)
        input_gradient = input_gradient + adapter_scale * jnp.dot(backward_pass, down_weight.T, preferred_element_type=jnp.float32)
        adapter_term = jnp.concatenate([adapter_scale * jnp.dot(token_rows.T, backward_pass, preferred_element_type=jnp.float32),
                                adapter_scale * jnp.dot(output_gradients.T, hidden_width, preferred_element_type=jnp.float32)], axis=0)
        current = lax.dynamic_index_in_dim(grads, slot, 0, keepdims=False)
        grads = lax.dynamic_update_index_in_dim(grads, current + adapter_term, slot, 0)
        return grads, (keys, input_gradient.astype(jnp.bfloat16))

    start = jnp.zeros((JOBS, D + KV, R), jnp.float32)
    grads, (keys, input_gradient) = lax.scan(step, start, (token_tiles, cot_tiles, slots))
    return keys.reshape(TOKENS, KV), input_gradient.reshape(TOKENS, D), grads
```

```python
import functools

import jax
import jax.numpy as jnp
from jax import lax
from jax.experimental import pallas as pl
from jax.experimental.pallas import tpu as pltpu
from jax.sharding import PartitionSpec as P

TILE_ROWS = 128
LANES = 128
adapter_scale = 0.5
f32 = jnp.float32
bf16 = jnp.bfloat16
NT = (((1,), (1,)), ((), ()))
TN = (((0,), (0,)), ((), ()))


def params(vmem_mib=32):
    return pltpu.CompilerParams(vmem_limit_bytes=vmem_mib * 1024 * 1024)


def pack_kernel(a_ref, o_ref):
    slots, rank, width = a_ref.shape
    tail = width - LANES
    for s in range(slots):
        o_ref[s, :rank, :] = a_ref[s, :, :LANES]
        rest = a_ref[s, :, LANES:].astype(f32)
        pieces = [rest[8 * b : 8 * b + 8, :] for b in range(LANES // tail)]
        o_ref[s, rank:, :] = jnp.concatenate(pieces, axis=1).astype(o_ref.dtype)


def pick_kernel(group_ref, job_ref, slot_ref, a_ref, o_ref):
    tiles = o_ref.shape[0]

    def step(t, carry):
        o_ref[t] = a_ref[slot_ref[job_ref[group_ref[0] * tiles + t]]]
        return carry

    lax.fori_loop(0, tiles, step, 0)


def sum_kernel(group_ref, job_ref, slot_ref, x_ref, o_ref):
    tiles = x_ref.shape[0]
    o_ref[...] = jnp.zeros_like(o_ref)

    def step(t, carry):
        s = slot_ref[job_ref[group_ref[0] * tiles + t]]
        o_ref[s] = o_ref[s] + x_ref[t].astype(f32)
        return carry

    lax.fori_loop(0, tiles, step, 0)


def unpack_kernel(x_ref, o_ref):
    slots, rank, width = o_ref.shape
    tail = width - LANES
    for s in range(slots):
        o_ref[s, :, :LANES] = x_ref[s, :rank, :]
        rest = x_ref[s, rank:, :]
        for b in range(LANES // tail):
            o_ref[s, 8 * b : 8 * b + 8, LANES:] = rest[:, tail * b : tail * (b + 1)]


def tile_kernel(x_ref, tok_ref, cot_ref, terms_ref, at_ref, hid_ref, back_ref, t_ref):
    shards, _, _ = x_ref.shape
    rank = at_ref.shape[0]
    depth = tok_ref.shape[1]
    tail = at_ref.shape[1] // shards - LANES
    per = LANES // tail
    group = per * (LANES + tail)
    lane = lax.broadcasted_iota(jnp.int32, (rank, LANES), 1)
    lane8 = lax.broadcasted_iota(jnp.int32, (8, LANES), 1)

    def unpack(a, carry):
        before = None
        for j in range(per + 1):
            if j < per:
                block = x_ref[a * per + j].astype(f32)
                main = block[:rank]
                now = main if j == 0 else pltpu.roll(main, tail * j, axis=1)
            else:
                now = None
            if before is None:
                out = now
            else:
                out = jnp.where(lane >= tail * (j - 1), rest, before)
                if now is not None:
                    out = jnp.where(lane >= tail * j, now, out)
            start = pl.multiple_of(a * group + LANES * j, LANES)
            at_ref[:, pl.ds(start, LANES)] = out.astype(at_ref.dtype)
            before = now
            if j < per:
                packed = block[rank:]
                rest = jnp.concatenate(
                    [
                        packed if b == j else pltpu.roll(packed, tail * ((j - b) % per), axis=1)
                        for b in range(per)
                    ],
                    axis=0,
                )
        return carry

    lax.fori_loop(0, shards // per, unpack, 0)

    tok = tok_ref[...]
    cot = cot_ref[...]
    hidden = lax.dot_general(
        tok, at_ref[:, :depth], NT, preferred_element_type=f32
    ).astype(bf16)
    back = lax.dot_general(cot, at_ref[:, depth:], NT, preferred_element_type=f32).astype(bf16)
    hid_ref[...] = hidden
    back_ref[...] = back
    t_ref[:, :depth] = adapter_scale * lax.dot_general(
        back, tok, TN, preferred_element_type=f32
    )
    t_ref[:, depth:] = adapter_scale * lax.dot_general(
        hidden, cot, TN, preferred_element_type=f32
    )

    def pack(a, carry):
        cols = [
            t_ref[:, pl.ds(pl.multiple_of(a * group + LANES * j, LANES), LANES)]
            for j in range(per + 1)
        ]
        for j in range(per):
            main = jnp.where(lane >= tail * j, cols[j], cols[j + 1])
            if j:
                main = pltpu.roll(main, LANES - tail * j, axis=1)
            packed = jnp.zeros((8, LANES), f32)
            for b in range(per):
                piece = cols[j + 1][8 * b : 8 * b + 8]
                if b != j:
                    piece = pltpu.roll(piece, tail * ((b - j) % per), axis=1)
                packed = jnp.where(lane8 // tail == b, piece, packed)
            terms_ref[a * per + j] = jnp.concatenate([main, packed], axis=0).astype(
                terms_ref.dtype
            )
        return carry

    lax.fori_loop(0, shards // per, pack, 0)


def main_kernel(tok_ref, cot_ref, w_ref, at_ref, up_ref, hid_ref, back_ref, keys_ref, grad_ref, acc_ref):
    step = pl.program_id(0)

    @pl.when(step == 0)
    def _():
        acc_ref[...] = adapter_scale * jnp.dot(
            hid_ref[...], up_ref[...], preferred_element_type=f32
        )

    acc_ref[...] += jnp.dot(tok_ref[...], w_ref[...], preferred_element_type=f32)
    grad = lax.dot_general(cot_ref[...], w_ref[...], NT, preferred_element_type=f32)
    grad += adapter_scale * jnp.dot(back_ref[...], at_ref[...], preferred_element_type=f32)
    grad_ref[...] = grad.astype(grad_ref.dtype)

    @pl.when(step == pl.num_programs(0) - 1)
    def _():
        keys_ref[...] = acc_ref[...].astype(keys_ref.dtype)


def whole(memory=pltpu.VMEM):
    return pl.BlockSpec(memory_space=memory)


def on_device(tokens, cotangent, frozen_weight, adapters, tile_job, job_slot):
    rows, depth = tokens.shape
    key_columns = cotangent.shape[1]
    slot_count, row_count, rank = adapters.shape
    total_jobs = job_slot.shape[0]
    groups = lax.axis_size("grp")
    shards = lax.axis_size("seq")
    packed_rows = row_count * rank // LANES
    width = depth + key_columns
    group = lax.axis_index("grp").reshape(1).astype(jnp.int32)
    jobs = tile_job.reshape(-1)

    weight = lax.all_gather(frozen_weight, "seq", axis=0, tiled=True)

    own = pl.pallas_call(
        pack_kernel,
        out_shape=jax.ShapeDtypeStruct((slot_count, packed_rows, LANES), bf16),
        in_specs=[whole()],
        out_specs=whole(),
        compiler_params=params(),
        name="pack",
    )(jnp.swapaxes(adapters, 1, 2))
    every = lax.all_gather(own, "grp", axis=0, tiled=True)
    smem = whole(pltpu.SMEM)
    outgoing = pl.pallas_call(
        pick_kernel,
        out_shape=jax.ShapeDtypeStruct((shards, packed_rows, LANES), bf16),
        in_specs=[smem, smem, smem, whole()],
        out_specs=whole(),
        compiler_params=params(),
        name="pick",
    )(group, jobs, job_slot, every)
    arrived = lax.all_to_all(outgoing, "seq", split_axis=0, concat_axis=0, tiled=True)
    terms, adapter, hidden, back = pl.pallas_call(
        tile_kernel,
        out_shape=(
            jax.ShapeDtypeStruct((shards, packed_rows, LANES), bf16),
            jax.ShapeDtypeStruct((rank, width), bf16),
            jax.ShapeDtypeStruct((rows, rank), bf16),
            jax.ShapeDtypeStruct((rows, rank), bf16),
        ),
        in_specs=[whole()] * 3,
        out_specs=(whole(),) * 4,
        scratch_shapes=[pltpu.VMEM((rank, width), f32)],
        compiler_params=params(),
        name="tile",
    )(arrived, tokens, cotangent)
    incoming = lax.all_to_all(terms, "seq", split_axis=0, concat_axis=0, tiled=True)
    sums = pl.pallas_call(
        sum_kernel,
        out_shape=jax.ShapeDtypeStruct((total_jobs, packed_rows, LANES), f32),
        in_specs=[smem, smem, smem, whole()],
        out_specs=whole(),
        compiler_params=params(),
        name="sum",
    )(group, jobs, job_slot, incoming)
    owned = lax.psum_scatter(sums, "grp", scatter_dimension=0, tiled=True)
    grads = pl.pallas_call(
        unpack_kernel,
        out_shape=jax.ShapeDtypeStruct((slot_count, rank, row_count), f32),
        in_specs=[whole()],
        out_specs=whole(),
        compiler_params=params(),
        name="unpack",
    )(owned)

    block = 512
    steps = depth // block
    keys, token_gradient = pl.pallas_call(
        main_kernel,
        grid=(steps,),
        out_shape=(
            jax.ShapeDtypeStruct((rows, key_columns), bf16),
            jax.ShapeDtypeStruct((rows, depth), bf16),
        ),
        in_specs=[
            pl.BlockSpec((rows, block), lambda i: (0, i)),
            pl.BlockSpec((rows, key_columns), lambda i: (0, 0)),
            pl.BlockSpec((block, key_columns), lambda i: (i, 0)),
            pl.BlockSpec((rank, block), lambda i: (0, i)),
            pl.BlockSpec((rank, key_columns), lambda i: (0, depth // key_columns)),
            pl.BlockSpec((rows, rank), lambda i: (0, 0)),
            pl.BlockSpec((rows, rank), lambda i: (0, 0)),
        ],
        out_specs=(
            pl.BlockSpec((rows, key_columns), lambda i: (0, 0)),
            pl.BlockSpec((rows, block), lambda i: (0, i)),
        ),
        scratch_shapes=[pltpu.VMEM((rows, key_columns), f32)],
        compiler_params=params(),
        cost_estimate=pl.CostEstimate(
            flops=4 * rows * depth * key_columns,
            bytes_accessed=2 * depth * key_columns + 4 * rows * width,
            transcendentals=0,
        ),
        name="base",
    )(tokens, cotangent, weight, adapter, adapter, hidden, back)
    return keys, token_gradient, jnp.swapaxes(grads, 1, 2)


def solution(mesh):
    placed = (
        P(("grp", "seq"), None),
        P(("grp", "seq"), None),
        P("seq", None),
        P("grp", "seq", None),
        P(),
        P(),
    )
    return jax.shard_map(
        on_device,
        mesh=mesh,
        in_specs=placed,
        out_specs=(P(("grp", "seq"), None), P(("grp", "seq"), None), P("grp", "seq", None)),
        check_vma=False,
    )
```

```python
import functools

import jax
import jax.numpy as jnp
from jax import lax
from jax.experimental import pallas as pl
from jax.experimental.pallas import tpu as pltpu
from jax.sharding import PartitionSpec as P

TILE_ROWS = 128
LANES = 128
adapter_scale = 0.5
f32 = jnp.float32
bf16 = jnp.bfloat16
NT = (((1,), (1,)), ((), ()))
TN = (((0,), (0,)), ((), ()))


def params(vmem_mib=32):
    return pltpu.CompilerParams(vmem_limit_bytes=vmem_mib * 1024 * 1024)


def pack_kernel(a_ref, o_ref):
    slots, rank, width = a_ref.shape
    tail = width - LANES
    for s in range(slots):
        o_ref[s, :rank, :] = a_ref[s, :, :LANES]
        rest = a_ref[s, :, LANES:].astype(f32)
        pieces = [rest[8 * b : 8 * b + 8, :] for b in range(LANES // tail)]
        o_ref[s, rank:, :] = jnp.concatenate(pieces, axis=1).astype(o_ref.dtype)


def pick_kernel(group_ref, job_ref, slot_ref, a_ref, o_ref):
    tiles = o_ref.shape[0]

    def step(t, carry):
        o_ref[t] = a_ref[slot_ref[job_ref[group_ref[0] * tiles + t]]]
        return carry

    lax.fori_loop(0, tiles, step, 0)


def sum_kernel(group_ref, job_ref, slot_ref, x_ref, o_ref):
    tiles = x_ref.shape[0]
    o_ref[...] = jnp.zeros_like(o_ref)

    def step(t, carry):
        s = slot_ref[job_ref[group_ref[0] * tiles + t]]
        o_ref[s] = o_ref[s] + x_ref[t].astype(f32)
        return carry

    lax.fori_loop(0, tiles, step, 0)


def unpack_kernel(x_ref, o_ref):
    slots, rank, width = o_ref.shape
    tail = width - LANES
    for s in range(slots):
        o_ref[s, :, :LANES] = x_ref[s, :rank, :]
        rest = x_ref[s, rank:, :]
        for b in range(LANES // tail):
            o_ref[s, 8 * b : 8 * b + 8, LANES:] = rest[:, tail * b : tail * (b + 1)]


def tile_kernel(x_ref, tok_ref, cot_ref, terms_ref, at_ref, hid_ref, back_ref, t_ref):
    shards, _, _ = x_ref.shape
    rank = at_ref.shape[0]
    depth = tok_ref.shape[1]
    tail = at_ref.shape[1] // shards - LANES
    per = LANES // tail
    group = per * (LANES + tail)
    lane = lax.broadcasted_iota(jnp.int32, (rank, LANES), 1)
    lane8 = lax.broadcasted_iota(jnp.int32, (8, LANES), 1)

    def unpack(a, carry):
        before = None
        for j in range(per + 1):
            if j < per:
                block = x_ref[a * per + j].astype(f32)
                main = block[:rank]
                now = main if j == 0 else pltpu.roll(main, tail * j, axis=1)
            else:
                now = None
            if before is None:
                out = now
            else:
                out = jnp.where(lane >= tail * (j - 1), rest, before)
                if now is not None:
                    out = jnp.where(lane >= tail * j, now, out)
            start = pl.multiple_of(a * group + LANES * j, LANES)
            at_ref[:, pl.ds(start, LANES)] = out.astype(at_ref.dtype)
            before = now
            if j < per:
                packed = block[rank:]
                rest = jnp.concatenate(
                    [
                        packed if b == j else pltpu.roll(packed, tail * ((j - b) % per), axis=1)
                        for b in range(per)
                    ],
                    axis=0,
                )
        return carry

    lax.fori_loop(0, shards // per, unpack, 0)

    tok = tok_ref[...]
    cot = cot_ref[...]
    hidden = lax.dot_general(
        tok, at_ref[:, :depth], NT, preferred_element_type=f32
    ).astype(bf16)
    back = lax.dot_general(cot, at_ref[:, depth:], NT, preferred_element_type=f32).astype(bf16)
    hid_ref[...] = hidden
    back_ref[...] = back
    t_ref[:, :depth] = adapter_scale * lax.dot_general(
        back, tok, TN, preferred_element_type=f32
    )
    t_ref[:, depth:] = adapter_scale * lax.dot_general(
        hidden, cot, TN, preferred_element_type=f32
    )

    def pack(a, carry):
        cols = [
            t_ref[:, pl.ds(pl.multiple_of(a * group + LANES * j, LANES), LANES)]
            for j in range(per + 1)
        ]
        for j in range(per):
            main = jnp.where(lane >= tail * j, cols[j], cols[j + 1])
            if j:
                main = pltpu.roll(main, LANES - tail * j, axis=1)
            packed = jnp.zeros((8, LANES), f32)
            for b in range(per):
                piece = cols[j + 1][8 * b : 8 * b + 8]
                if b != j:
                    piece = pltpu.roll(piece, tail * ((b - j) % per), axis=1)
                packed = jnp.where(lane8 // tail == b, piece, packed)
            terms_ref[a * per + j] = jnp.concatenate([main, packed], axis=0).astype(
                terms_ref.dtype
            )
        return carry

    lax.fori_loop(0, shards // per, pack, 0)


def main_kernel(tok_ref, cot_ref, w_ref, at_ref, up_ref, hid_ref, back_ref, keys_ref, grad_ref, acc_ref):
    step = pl.program_id(0)

    @pl.when(step == 0)
    def _():
        acc_ref[...] = adapter_scale * jnp.dot(
            hid_ref[...], up_ref[...], preferred_element_type=f32
        )

    acc_ref[...] += jnp.dot(tok_ref[...], w_ref[...], preferred_element_type=f32)
    grad = lax.dot_general(cot_ref[...], w_ref[...], NT, preferred_element_type=f32)
    grad += adapter_scale * jnp.dot(back_ref[...], at_ref[...], preferred_element_type=f32)
    grad_ref[...] = grad.astype(grad_ref.dtype)

    @pl.when(step == pl.num_programs(0) - 1)
    def _():
        keys_ref[...] = acc_ref[...].astype(keys_ref.dtype)


def whole(memory=pltpu.VMEM):
    return pl.BlockSpec(memory_space=memory)


def on_device(tokens, cotangent, frozen_weight, adapters, tile_job, job_slot):
    rows, depth = tokens.shape
    key_columns = cotangent.shape[1]
    slot_count, row_count, rank = adapters.shape
    total_jobs = job_slot.shape[0]
    groups = lax.axis_size("grp")
    shards = lax.axis_size("seq")
    packed_rows = row_count * rank // LANES
    width = depth + key_columns
    group = lax.axis_index("grp").reshape(1).astype(jnp.int32)
    jobs = tile_job.reshape(-1)

    weight = lax.all_gather(frozen_weight, "seq", axis=0, tiled=True)

    own = pl.pallas_call(
        pack_kernel,
        out_shape=jax.ShapeDtypeStruct((slot_count, packed_rows, LANES), bf16),
        in_specs=[whole()],
        out_specs=whole(),
        compiler_params=params(),
        name="pack",
    )(jnp.swapaxes(adapters, 1, 2))
    every = lax.all_gather(own, "grp", axis=0, tiled=True)
    smem = whole(pltpu.SMEM)
    outgoing = pl.pallas_call(
        pick_kernel,
        out_shape=jax.ShapeDtypeStruct((shards, packed_rows, LANES), bf16),
        in_specs=[smem, smem, smem, whole()],
        out_specs=whole(),
        compiler_params=params(),
        name="pick",
    )(group, jobs, job_slot, every)
    arrived = lax.all_to_all(outgoing, "seq", split_axis=0, concat_axis=0, tiled=True)
    terms, adapter, hidden, back = pl.pallas_call(
        tile_kernel,
        out_shape=(
            jax.ShapeDtypeStruct((shards, packed_rows, LANES), bf16),
            jax.ShapeDtypeStruct((rank, width), bf16),
            jax.ShapeDtypeStruct((rows, rank), bf16),
            jax.ShapeDtypeStruct((rows, rank), bf16),
        ),
        in_specs=[whole()] * 3,
        out_specs=(whole(),) * 4,
        scratch_shapes=[pltpu.VMEM((rank, width), f32)],
        compiler_params=params(),
        name="tile",
    )(arrived, tokens, cotangent)
    incoming = lax.all_to_all(terms, "seq", split_axis=0, concat_axis=0, tiled=True)
    incoming, weight = lax.optimization_barrier((incoming, weight))
    sums = pl.pallas_call(
        sum_kernel,
        out_shape=jax.ShapeDtypeStruct((total_jobs, packed_rows, LANES), f32),
        in_specs=[smem, smem, smem, whole()],
        out_specs=whole(),
        compiler_params=params(),
        name="sum",
    )(group, jobs, job_slot, incoming)
    owned = lax.psum_scatter(sums, "grp", scatter_dimension=0, tiled=True)
    grads = pl.pallas_call(
        unpack_kernel,
        out_shape=jax.ShapeDtypeStruct((slot_count, rank, row_count), f32),
        in_specs=[whole()],
        out_specs=whole(),
        compiler_params=params(),
        name="unpack",
    )(owned)

    block = 512
    steps = depth // block
    keys, token_gradient = pl.pallas_call(
        main_kernel,
        grid=(steps,),
        out_shape=(
            jax.ShapeDtypeStruct((rows, key_columns), bf16),
            jax.ShapeDtypeStruct((rows, depth), bf16),
        ),
        in_specs=[
            pl.BlockSpec((rows, block), lambda i: (0, i)),
            pl.BlockSpec((rows, key_columns), lambda i: (0, 0)),
            pl.BlockSpec((block, key_columns), lambda i: (i, 0)),
            pl.BlockSpec((rank, block), lambda i: (0, i)),
            pl.BlockSpec((rank, key_columns), lambda i: (0, depth // key_columns)),
            pl.BlockSpec((rows, rank), lambda i: (0, 0)),
            pl.BlockSpec((rows, rank), lambda i: (0, 0)),
        ],
        out_specs=(
            pl.BlockSpec((rows, key_columns), lambda i: (0, 0)),
            pl.BlockSpec((rows, block), lambda i: (0, i)),
        ),
        scratch_shapes=[pltpu.VMEM((rows, key_columns), f32)],
        compiler_params=params(56),
        cost_estimate=pl.CostEstimate(
            flops=4 * rows * depth * key_columns,
            bytes_accessed=2 * depth * key_columns + 4 * rows * width,
            transcendentals=0,
        ),
        name="base",
    )(tokens, cotangent, weight, adapter, adapter, hidden, back)
    return keys, token_gradient, jnp.swapaxes(grads, 1, 2)


def solution(mesh):
    placed = (
        P(("grp", "seq"), None),
        P(("grp", "seq"), None),
        P("seq", None),
        P("grp", "seq", None),
        P(),
        P(),
    )
    return jax.shard_map(
        on_device,
        mesh=mesh,
        in_specs=placed,
        out_specs=(P(("grp", "seq"), None), P(("grp", "seq"), None), P("grp", "seq", None)),
        check_vma=False,
    )
```

```python
import jax
import jax.numpy as jnp
from jax import lax
from jax.experimental import pallas as pl
from jax.experimental.pallas import tpu as pltpu
from jax.sharding import PartitionSpec as P

TILE_ROWS = 128
LANES = 128
adapter_scale = 0.5
f32 = jnp.float32
bf16 = jnp.bfloat16
NT = (((1,), (1,)), ((), ()))
TN = (((0,), (0,)), ((), ()))


def params(vmem_mib=32):
    return pltpu.CompilerParams(vmem_limit_bytes=vmem_mib * 1024 * 1024)


def pack_kernel(a_ref, o_ref):
    slots, rank, width = a_ref.shape
    tail = width - LANES
    for s in range(slots):
        o_ref[s, :rank, :] = a_ref[s, :, :LANES]
        rest = a_ref[s, :, LANES:].astype(f32)
        pieces = [rest[8 * b : 8 * b + 8, :] for b in range(LANES // tail)]
        o_ref[s, rank:, :] = jnp.concatenate(pieces, axis=1).astype(o_ref.dtype)


def pick_kernel(group_ref, job_ref, slot_ref, a0_ref, a1_ref, a2_ref, a3_ref, o_ref):
    tiles = o_ref.shape[0]
    sources = (a0_ref, a1_ref, a2_ref, a3_ref)
    count = a0_ref.shape[0]
    me = group_ref[0]

    def step(t, carry):
        s = slot_ref[job_ref[me * tiles + t]]
        away = lax.rem(s // count - me + len(sources), len(sources))
        for k, source in enumerate(sources):

            @pl.when(away == k)
            def _():
                o_ref[t] = source[lax.rem(s, count)]

        return carry

    lax.fori_loop(0, tiles, step, 0)


def sum_kernel(group_ref, job_ref, slot_ref, x_ref, o0_ref, o1_ref, o2_ref, o3_ref):
    tiles = x_ref.shape[0]
    sinks = (o0_ref, o1_ref, o2_ref, o3_ref)
    count = o0_ref.shape[0]
    me = group_ref[0]
    for sink in sinks:
        sink[...] = jnp.zeros_like(sink)

    def step(t, carry):
        s = slot_ref[job_ref[me * tiles + t]]
        away = lax.rem(s // count - me + len(sinks), len(sinks))
        at = lax.rem(s, count)
        for k, sink in enumerate(sinks):

            @pl.when(away == k)
            def _():
                sink[at] = sink[at] + x_ref[t].astype(f32)

        return carry

    lax.fori_loop(0, tiles, step, 0)


def unpack_kernel(x0_ref, x1_ref, x2_ref, x3_ref, o_ref):
    slots, rank, width = o_ref.shape
    tail = width - LANES
    for s in range(slots):
        total = (x0_ref[s] + x1_ref[s]) + (x2_ref[s] + x3_ref[s])
        o_ref[s, :, :LANES] = total[:rank]
        rest = total[rank:]
        for b in range(LANES // tail):
            o_ref[s, 8 * b : 8 * b + 8, LANES:] = rest[:, tail * b : tail * (b + 1)]


def tile_kernel(x_ref, tok_ref, cot_ref, terms_ref, at_ref, hid_ref, back_ref, t_ref):
    shards, _, _ = x_ref.shape
    rank = at_ref.shape[0]
    depth = tok_ref.shape[1]
    tail = at_ref.shape[1] // shards - LANES
    per = LANES // tail
    group = per * (LANES + tail)
    lane = lax.broadcasted_iota(jnp.int32, (rank, LANES), 1)
    lane8 = lax.broadcasted_iota(jnp.int32, (8, LANES), 1)

    def unpack(a, carry):
        before = None
        for j in range(per + 1):
            if j < per:
                block = x_ref[a * per + j].astype(f32)
                main = block[:rank]
                now = main if j == 0 else pltpu.roll(main, tail * j, axis=1)
            else:
                now = None
            if before is None:
                out = now
            else:
                out = jnp.where(lane >= tail * (j - 1), rest, before)
                if now is not None:
                    out = jnp.where(lane >= tail * j, now, out)
            start = pl.multiple_of(a * group + LANES * j, LANES)
            at_ref[:, pl.ds(start, LANES)] = out.astype(at_ref.dtype)
            before = now
            if j < per:
                packed = block[rank:]
                rest = jnp.concatenate(
                    [
                        packed if b == j else pltpu.roll(packed, tail * ((j - b) % per), axis=1)
                        for b in range(per)
                    ],
                    axis=0,
                )
        return carry

    lax.fori_loop(0, shards // per, unpack, 0)

    tok = tok_ref[...]
    cot = cot_ref[...]
    hidden = lax.dot_general(
        tok, at_ref[:, :depth], NT, preferred_element_type=f32
    ).astype(bf16)
    back = lax.dot_general(cot, at_ref[:, depth:], NT, preferred_element_type=f32).astype(bf16)
    hid_ref[...] = hidden
    back_ref[...] = back
    t_ref[:, :depth] = adapter_scale * lax.dot_general(
        back, tok, TN, preferred_element_type=f32
    )
    t_ref[:, depth:] = adapter_scale * lax.dot_general(
        hidden, cot, TN, preferred_element_type=f32
    )

    def pack(a, carry):
        cols = [
            t_ref[:, pl.ds(pl.multiple_of(a * group + LANES * j, LANES), LANES)]
            for j in range(per + 1)
        ]
        for j in range(per):
            main = jnp.where(lane >= tail * j, cols[j], cols[j + 1])
            if j:
                main = pltpu.roll(main, LANES - tail * j, axis=1)
            packed = jnp.zeros((8, LANES), f32)
            for b in range(per):
                piece = cols[j + 1][8 * b : 8 * b + 8]
                if b != j:
                    piece = pltpu.roll(piece, tail * ((b - j) % per), axis=1)
                packed = jnp.where(lane8 // tail == b, piece, packed)
            terms_ref[a * per + j] = jnp.concatenate([main, packed], axis=0).astype(
                terms_ref.dtype
            )
        return carry

    lax.fori_loop(0, shards // per, pack, 0)


def main_kernel(tok_ref, cot_ref, w_ref, at_ref, up_ref, hid_ref, back_ref, keys_ref, grad_ref, acc_ref):
    step = pl.program_id(0)

    @pl.when(step == 0)
    def _():
        acc_ref[...] = adapter_scale * jnp.dot(
            hid_ref[...], up_ref[...], preferred_element_type=f32
        )

    acc_ref[...] += jnp.dot(tok_ref[...], w_ref[...], preferred_element_type=f32)
    grad = lax.dot_general(cot_ref[...], w_ref[...], NT, preferred_element_type=f32)
    grad += adapter_scale * jnp.dot(back_ref[...], at_ref[...], preferred_element_type=f32)
    grad_ref[...] = grad.astype(grad_ref.dtype)

    @pl.when(step == pl.num_programs(0) - 1)
    def _():
        keys_ref[...] = acc_ref[...].astype(keys_ref.dtype)


def shift(x, by, groups):
    return lax.ppermute(x, "grp", [(i, (i + by) % groups) for i in range(groups)])


def whole(memory=pltpu.VMEM):
    return pl.BlockSpec(memory_space=memory)


def on_device(tokens, cotangent, frozen_weight, adapters, tile_job, job_slot):
    rows, depth = tokens.shape
    key_columns = cotangent.shape[1]
    slot_count, row_count, rank = adapters.shape
    groups = lax.axis_size("grp")
    shards = lax.axis_size("seq")
    packed_rows = row_count * rank // LANES
    width = depth + key_columns
    group = lax.axis_index("grp").reshape(1).astype(jnp.int32)
    jobs = tile_job.reshape(-1)

    weight = lax.all_gather(frozen_weight, "seq", axis=0, tiled=True)

    own = pl.pallas_call(
        pack_kernel,
        out_shape=jax.ShapeDtypeStruct((slot_count, packed_rows, LANES), bf16),
        in_specs=[whole()],
        out_specs=whole(),
        compiler_params=params(),
        name="pack",
    )(jnp.swapaxes(adapters, 1, 2))
    every = (own,) + tuple(shift(own, -k, groups) for k in range(1, groups))
    smem = whole(pltpu.SMEM)
    outgoing = pl.pallas_call(
        pick_kernel,
        out_shape=jax.ShapeDtypeStruct((shards, packed_rows, LANES), bf16),
        in_specs=[smem, smem, smem] + [whole()] * groups,
        out_specs=whole(),
        compiler_params=params(),
        name="pick",
    )(group, jobs, job_slot, *every)
    arrived = lax.all_to_all(outgoing, "seq", split_axis=0, concat_axis=0, tiled=True)
    terms, adapter, hidden, back = pl.pallas_call(
        tile_kernel,
        out_shape=(
            jax.ShapeDtypeStruct((shards, packed_rows, LANES), bf16),
            jax.ShapeDtypeStruct((rank, width), bf16),
            jax.ShapeDtypeStruct((rows, rank), bf16),
            jax.ShapeDtypeStruct((rows, rank), bf16),
        ),
        in_specs=[whole()] * 3,
        out_specs=(whole(),) * 4,
        scratch_shapes=[pltpu.VMEM((rank, width), f32)],
        compiler_params=params(),
        name="tile",
    )(arrived, tokens, cotangent)
    incoming = lax.all_to_all(terms, "seq", split_axis=0, concat_axis=0, tiled=True)
    incoming, weight = lax.optimization_barrier((incoming, weight))
    sums = pl.pallas_call(
        sum_kernel,
        out_shape=(jax.ShapeDtypeStruct((slot_count, packed_rows, LANES), f32),) * groups,
        in_specs=[smem, smem, smem, whole()],
        out_specs=(whole(),) * groups,
        compiler_params=params(),
        name="sum",
    )(group, jobs, job_slot, incoming)
    owned = (sums[0],) + tuple(shift(sums[k], k, groups) for k in range(1, groups))
    grads = pl.pallas_call(
        unpack_kernel,
        out_shape=jax.ShapeDtypeStruct((slot_count, rank, row_count), f32),
        in_specs=[whole()] * groups,
        out_specs=whole(),
        compiler_params=params(),
        name="unpack",
    )(*owned)

    block = 512
    steps = depth // block
    keys, token_gradient = pl.pallas_call(
        main_kernel,
        grid=(steps,),
        out_shape=(
            jax.ShapeDtypeStruct((rows, key_columns), bf16),
            jax.ShapeDtypeStruct((rows, depth), bf16),
        ),
        in_specs=[
            pl.BlockSpec((rows, block), lambda i: (0, i)),
            pl.BlockSpec((rows, key_columns), lambda i: (0, 0)),
            pl.BlockSpec((block, key_columns), lambda i: (i, 0)),
            pl.BlockSpec((rank, block), lambda i: (0, i)),
            pl.BlockSpec((rank, key_columns), lambda i: (0, depth // key_columns)),
            pl.BlockSpec((rows, rank), lambda i: (0, 0)),
            pl.BlockSpec((rows, rank), lambda i: (0, 0)),
        ],
        out_specs=(
            pl.BlockSpec((rows, key_columns), lambda i: (0, 0)),
            pl.BlockSpec((rows, block), lambda i: (0, i)),
        ),
        scratch_shapes=[pltpu.VMEM((rows, key_columns), f32)],
        compiler_params=params(56),
        cost_estimate=pl.CostEstimate(
            flops=4 * rows * depth * key_columns,
            bytes_accessed=2 * depth * key_columns + 4 * rows * width,
            transcendentals=0,
        ),
        name="base",
    )(tokens, cotangent, weight, adapter, adapter, hidden, back)
    return keys, token_gradient, jnp.swapaxes(grads, 1, 2)


def solution(mesh):
    placed = (
        P(("grp", "seq"), None),
        P(("grp", "seq"), None),
        P("seq", None),
        P("grp", "seq", None),
        P(),
        P(),
    )
    return jax.shard_map(
        on_device,
        mesh=mesh,
        in_specs=placed,
        out_specs=(P(("grp", "seq"), None), P(("grp", "seq"), None), P("grp", "seq", None)),
        check_vma=False,
    )
```

```python
import jax
import jax.numpy as jnp
from jax import lax
from jax.experimental import pallas as pl
from jax.experimental.pallas import tpu as pltpu
from jax.sharding import Mesh
from jax.sharding import PartitionSpec as P

SEQ = ("y", "z", "core")
TILE_ROWS = 128
LANES = 128
adapter_scale = 0.5
f32 = jnp.float32
bf16 = jnp.bfloat16
NT = (((1,), (1,)), ((), ()))
TN = (((0,), (0,)), ((), ()))


def params(vmem_mib=32):
    return pltpu.CompilerParams(vmem_limit_bytes=vmem_mib * 1024 * 1024)


def pack_kernel(a_ref, o_ref):
    slots, rank, width = a_ref.shape
    tail = width - LANES
    for s in range(slots):
        o_ref[s, :rank, :] = a_ref[s, :, :LANES]
        rest = a_ref[s, :, LANES:].astype(f32)
        pieces = [rest[8 * b : 8 * b + 8, :] for b in range(LANES // tail)]
        o_ref[s, rank:, :] = jnp.concatenate(pieces, axis=1).astype(o_ref.dtype)


def pick_kernel(group_ref, job_ref, slot_ref, a0_ref, a1_ref, a2_ref, a3_ref, o_ref):
    tiles = o_ref.shape[0]
    sources = (a0_ref, a1_ref, a2_ref, a3_ref)
    count = a0_ref.shape[0]
    me = group_ref[0]

    def step(t, carry):
        s = slot_ref[job_ref[me * tiles + t]]
        away = lax.rem(s // count - me + len(sources), len(sources))
        for k, source in enumerate(sources):

            @pl.when(away == k)
            def _():
                o_ref[t] = source[lax.rem(s, count)]

        return carry

    lax.fori_loop(0, tiles, step, 0)


def sum_kernel(group_ref, job_ref, slot_ref, x_ref, o0_ref, o1_ref, o2_ref, o3_ref):
    tiles = x_ref.shape[0]
    sinks = (o0_ref, o1_ref, o2_ref, o3_ref)
    count = o0_ref.shape[0]
    me = group_ref[0]
    for sink in sinks:
        sink[...] = jnp.zeros_like(sink)

    def step(t, carry):
        s = slot_ref[job_ref[me * tiles + t]]
        away = lax.rem(s // count - me + len(sinks), len(sinks))
        at = lax.rem(s, count)
        for k, sink in enumerate(sinks):

            @pl.when(away == k)
            def _():
                sink[at] = sink[at] + x_ref[t].astype(f32)

        return carry

    lax.fori_loop(0, tiles, step, 0)


def unpack_kernel(x0_ref, x1_ref, x2_ref, x3_ref, o_ref):
    slots, rank, width = o_ref.shape
    tail = width - LANES
    for s in range(slots):
        total = (x0_ref[s] + x1_ref[s]) + (x2_ref[s] + x3_ref[s])
        o_ref[s, :, :LANES] = total[:rank]
        rest = total[rank:]
        for b in range(LANES // tail):
            o_ref[s, 8 * b : 8 * b + 8, LANES:] = rest[:, tail * b : tail * (b + 1)]


def tile_kernel(x_ref, tok_ref, cot_ref, terms_ref, at_ref, t_ref):
    shards, _, _ = x_ref.shape
    rank = at_ref.shape[0]
    depth = tok_ref.shape[1]
    width = depth + cot_ref.shape[1]
    tail = width // shards - LANES
    per = LANES // tail
    group = per * (LANES + tail)
    lane = lax.broadcasted_iota(jnp.int32, (rank, LANES), 1)
    lane8 = lax.broadcasted_iota(jnp.int32, (8, LANES), 1)

    def unpack(a, carry):
        before = None
        for j in range(per + 1):
            if j < per:
                block = x_ref[a * per + j].astype(f32)
                main = block[:rank]
                now = main if j == 0 else pltpu.roll(main, tail * j, axis=1)
            else:
                now = None
            if before is None:
                out = now
            else:
                out = jnp.where(lane >= tail * (j - 1), rest, before)
                if now is not None:
                    out = jnp.where(lane >= tail * j, now, out)
            start = pl.multiple_of(a * group + LANES * j, LANES)
            at_ref[:, pl.ds(start, LANES)] = out.astype(at_ref.dtype)
            before = now
            if j < per:
                packed = block[rank:]
                rest = jnp.concatenate(
                    [
                        packed if b == j else pltpu.roll(packed, tail * ((j - b) % per), axis=1)
                        for b in range(per)
                    ],
                    axis=0,
                )
        return carry

    lax.fori_loop(0, shards // per, unpack, 0)

    tok = tok_ref[...]
    cot = cot_ref[...]
    hidden = lax.dot_general(
        at_ref[:, :depth], tok, NT, preferred_element_type=f32
    ).astype(bf16)
    back = lax.dot_general(
        at_ref[:, depth:width], cot, NT, preferred_element_type=f32
    ).astype(bf16)
    at_ref[:, width : width + LANES] = hidden
    at_ref[:, width + LANES :] = back
    t_ref[:, :depth] = adapter_scale * jnp.dot(back, tok, preferred_element_type=f32)
    t_ref[:, depth:] = adapter_scale * jnp.dot(hidden, cot, preferred_element_type=f32)

    def pack(a, carry):
        cols = [
            t_ref[:, pl.ds(pl.multiple_of(a * group + LANES * j, LANES), LANES)]
            for j in range(per + 1)
        ]
        for j in range(per):
            main = jnp.where(lane >= tail * j, cols[j], cols[j + 1])
            if j:
                main = pltpu.roll(main, LANES - tail * j, axis=1)
            packed = jnp.zeros((8, LANES), f32)
            for b in range(per):
                piece = cols[j + 1][8 * b : 8 * b + 8]
                if b != j:
                    piece = pltpu.roll(piece, tail * ((b - j) % per), axis=1)
                packed = jnp.where(lane8 // tail == b, piece, packed)
            terms_ref[a * per + j] = jnp.concatenate([main, packed], axis=0).astype(
                terms_ref.dtype
            )
        return carry

    lax.fori_loop(0, shards // per, pack, 0)


def base_kernel(core_ref, tok_ref, cot_ref, half_ref, other_ref, at_ref, up_ref, hid_ref, back_ref, keys_ref, grad_ref, w_ref, acc_ref, sems):
    step = pl.program_id(0)
    steps = pl.num_programs(0)
    rows = TILE_ROWS
    pairs = w_ref.shape[1] // (2 * rows)
    slot = lax.rem(step, 2)

    def copies(at, to):
        out = []
        for p in range(pairs):
            src = pl.ds(pl.multiple_of((at * pairs + p) * rows, rows), rows)
            for k, source in enumerate((half_ref, other_ref)):
                mine = core_ref[0] if k == 0 else 1 - core_ref[0]
                dst = pl.ds(pl.multiple_of(2 * p * rows + mine * rows, rows), rows)
                out.append(pltpu.make_async_copy(source.at[src], w_ref.at[to, dst], sems.at[to, 2 * p + k]))
        return out

    @pl.when(step == 0)
    def _():
        for c in copies(step, slot):
            c.start()
        acc_ref[...] = adapter_scale * lax.dot_general(
            hid_ref[...], up_ref[...], TN, preferred_element_type=f32
        )

    @pl.when(step + 1 < steps)
    def _():
        for c in copies(step + 1, 1 - slot):
            c.start()

    for c in copies(step, slot):
        c.wait()
    weight = w_ref[slot]
    acc_ref[...] += jnp.dot(tok_ref[...], weight, preferred_element_type=f32)
    grad = lax.dot_general(cot_ref[...], weight, NT, preferred_element_type=f32)
    grad += adapter_scale * lax.dot_general(
        back_ref[...], at_ref[...], TN, preferred_element_type=f32
    )
    grad_ref[...] = grad.astype(grad_ref.dtype)

    @pl.when(step == steps - 1)
    def _():
        keys_ref[...] = acc_ref[...].astype(keys_ref.dtype)


def shift(x, by, groups):
    return lax.ppermute(x, "grp", [(i, (i + by) % groups) for i in range(groups)])


def whole(memory=pltpu.VMEM):
    return pl.BlockSpec(memory_space=memory)


def on_device(tokens, cotangent, frozen_weight, adapters, tile_job, job_slot):
    rows, depth = tokens.shape
    key_columns = cotangent.shape[1]
    slot_count, row_count, rank = adapters.shape
    groups = lax.axis_size("grp")
    shards = lax.axis_size(SEQ)
    packed_rows = row_count * rank // LANES
    width = depth + key_columns
    group = lax.axis_index("grp").reshape(1).astype(jnp.int32)
    core = lax.axis_index("core").reshape(1).astype(jnp.int32)
    jobs = tile_job.reshape(-1)

    column = lax.all_gather(frozen_weight, "z", axis=0, tiled=True)

    own = pl.pallas_call(
        pack_kernel,
        out_shape=jax.ShapeDtypeStruct((slot_count, packed_rows, LANES), bf16),
        in_specs=[whole()],
        out_specs=whole(),
        compiler_params=params(),
        name="pack",
    )(jnp.swapaxes(adapters, 1, 2))
    every = (own,) + tuple(shift(own, -k, groups) for k in range(1, groups))
    smem = whole(pltpu.SMEM)
    outgoing = pl.pallas_call(
        pick_kernel,
        out_shape=jax.ShapeDtypeStruct((shards, packed_rows, LANES), bf16),
        in_specs=[smem, smem, smem] + [whole()] * groups,
        out_specs=whole(),
        compiler_params=params(),
        name="pick",
    )(group, jobs, job_slot, *every)
    outgoing, column = lax.optimization_barrier((outgoing, column))
    half = lax.all_gather(column, "y", axis=0, tiled=True)
    arrived = lax.all_to_all(outgoing, SEQ, split_axis=0, concat_axis=0, tiled=True)
    terms, adapter = pl.pallas_call(
        tile_kernel,
        out_shape=(
            jax.ShapeDtypeStruct((shards, packed_rows, LANES), bf16),
            jax.ShapeDtypeStruct((rank, width + 2 * rows), bf16),
        ),
        in_specs=[whole()] * 3,
        out_specs=(whole(),) * 2,
        scratch_shapes=[pltpu.VMEM((rank, width), f32)],
        compiler_params=params(),
        name="tile",
    )(arrived, tokens, cotangent)
    incoming = lax.all_to_all(terms, SEQ, split_axis=0, concat_axis=0, tiled=True)
    incoming, half = lax.optimization_barrier((incoming, half))
    other = lax.ppermute(half, "core", [(0, 1), (1, 0)])
    sums = pl.pallas_call(
        sum_kernel,
        out_shape=(jax.ShapeDtypeStruct((slot_count, packed_rows, LANES), f32),) * groups,
        in_specs=[smem, smem, smem, whole()],
        out_specs=(whole(),) * groups,
        compiler_params=params(56),
        name="sum",
    )(group, jobs, job_slot, incoming)
    last, other = lax.optimization_barrier((sums[-1], other))
    sums = tuple(sums[:-1]) + (last,)
    owned = (sums[0],) + tuple(shift(sums[k], k, groups) for k in range(1, groups))
    grads = pl.pallas_call(
        unpack_kernel,
        out_shape=jax.ShapeDtypeStruct((slot_count, rank, row_count), f32),
        in_specs=[whole()] * groups,
        out_specs=whole(),
        compiler_params=params(),
        name="unpack",
    )(*owned)

    block = 1024
    steps = depth // block
    keys, token_gradient = pl.pallas_call(
        base_kernel,
        grid=(steps,),
        out_shape=(
            jax.ShapeDtypeStruct((rows, key_columns), bf16),
            jax.ShapeDtypeStruct((rows, depth), bf16),
        ),
        in_specs=[
            smem,
            pl.BlockSpec((rows, block), lambda i: (0, i)),
            pl.BlockSpec((rows, key_columns), lambda i: (0, 0)),
            whole(pl.ANY),
            whole(pl.ANY),
            pl.BlockSpec((rank, block), lambda i: (0, i)),
            pl.BlockSpec((rank, key_columns), lambda i: (0, depth // key_columns)),
            pl.BlockSpec((rank, rows), lambda i: (0, width // rows)),
            pl.BlockSpec((rank, rows), lambda i: (0, width // rows + 1)),
        ],
        out_specs=(
            pl.BlockSpec((rows, key_columns), lambda i: (0, 0)),
            pl.BlockSpec((rows, block), lambda i: (0, i)),
        ),
        scratch_shapes=[
            pltpu.VMEM((2, block, key_columns), bf16),
            pltpu.VMEM((rows, key_columns), f32),
            pltpu.SemaphoreType.DMA((2, block // TILE_ROWS)),
        ],
        compiler_params=params(56),
        cost_estimate=pl.CostEstimate(
            flops=4 * rows * depth * key_columns,
            bytes_accessed=2 * depth * key_columns + 4 * rows * width,
            transcendentals=0,
        ),
        name="base",
    )(core, tokens, cotangent, half, other, adapter, adapter, adapter, adapter)
    return keys, token_gradient, jnp.swapaxes(grads, 1, 2)


def solution(mesh):
    groups, shards = mesh.devices.shape
    cores = 2
    deep = 8
    mesh = Mesh(
        mesh.devices.reshape(groups, shards // (cores * deep), deep, cores),
        ("grp", "y", "z", "core"),
    )
    every = ("grp",) + SEQ
    placed = (
        P(every, None),
        P(every, None),
        P(SEQ, None),
        P("grp", SEQ, None),
        P(),
        P(),
    )
    return jax.shard_map(
        on_device,
        mesh=mesh,
        in_specs=placed,
        out_specs=(P(every, None), P(every, None), P("grp", SEQ, None)),
        check_vma=False,
    )
```

```python
import jax
import jax.numpy as jnp
from jax import lax
from jax.experimental import pallas as pl
from jax.experimental.pallas import tpu as pltpu
from jax.sharding import Mesh
from jax.sharding import PartitionSpec as P

SEQ = ("y", "z", "core")
TILE_ROWS = 128
LANES = 128
adapter_scale = 0.5
f32 = jnp.float32
bf16 = jnp.bfloat16
NT = (((1,), (1,)), ((), ()))
TN = (((0,), (0,)), ((), ()))


def params(vmem_mib=32):
    return pltpu.CompilerParams(vmem_limit_bytes=vmem_mib * 1024 * 1024)


def pack_kernel(a_ref, o_ref):
    slots, rank, width = a_ref.shape
    tail = width - LANES
    for s in range(slots):
        o_ref[s, :rank, :] = a_ref[s, :, :LANES]
        rest = a_ref[s, :, LANES:].astype(f32)
        pieces = [rest[8 * b : 8 * b + 8, :] for b in range(LANES // tail)]
        o_ref[s, rank:, :] = jnp.concatenate(pieces, axis=1).astype(o_ref.dtype)


def pick_kernel(group_ref, job_ref, slot_ref, *refs):
    sources, (o_ref, every_ref) = refs[:-2], refs[-2:]
    tiles = o_ref.shape[0]
    count = sources[0].shape[0]
    me = group_ref[0]
    for k, source in enumerate(sources):
        every_ref[pl.ds(lax.rem(me + k, len(sources)) * count, count)] = source[...]

    def step(t, carry):
        o_ref[t] = every_ref[slot_ref[job_ref[me * tiles + t]]]
        return carry

    lax.fori_loop(0, tiles, step, 0, unroll=4)


def sum_kernel(group_ref, job_ref, slot_ref, x_ref, *refs):
    sinks, sum_ref = refs[:-1], refs[-1]
    tiles = x_ref.shape[0]
    count = sinks[0].shape[0]
    me = group_ref[0]
    sum_ref[...] = jnp.zeros_like(sum_ref)

    def step(t, carry):
        s = slot_ref[job_ref[me * tiles + t]]
        sum_ref[s] = sum_ref[s] + x_ref[t].astype(f32)
        return carry

    lax.fori_loop(0, tiles, step, 0, unroll=4)
    for k, sink in enumerate(sinks):
        sink[...] = sum_ref[pl.ds(lax.rem(me + k, len(sinks)) * count, count)].astype(sink.dtype)


def unpack_kernel(x0_ref, x1_ref, x2_ref, x3_ref, o_ref):
    slots, rank, width = o_ref.shape
    tail = width - LANES
    for s in range(slots):
        total = x0_ref[s] + (x1_ref[s].astype(f32) + x2_ref[s].astype(f32)) + x3_ref[s].astype(f32)
        o_ref[s, :, :LANES] = total[:rank]
        rest = total[rank:]
        for b in range(LANES // tail):
            o_ref[s, 8 * b : 8 * b + 8, LANES:] = rest[:, tail * b : tail * (b + 1)]


def tile_kernel(x_ref, tok_ref, cot_ref, terms_ref, at_ref, t_ref):
    shards, _, _ = x_ref.shape
    rank = at_ref.shape[0]
    depth = tok_ref.shape[1]
    width = depth + cot_ref.shape[1]
    tail = width // shards - LANES
    per = LANES // tail
    group = per * (LANES + tail)
    lane = lax.broadcasted_iota(jnp.int32, (rank, LANES), 1)
    lane8 = lax.broadcasted_iota(jnp.int32, (8, LANES), 1)

    def unpack(a, carry):
        before = None
        for j in range(per + 1):
            if j < per:
                block = x_ref[a * per + j].astype(f32)
                main = block[:rank]
                now = main if j == 0 else pltpu.roll(main, tail * j, axis=1)
            else:
                now = None
            if before is None:
                out = now
            else:
                out = jnp.where(lane >= tail * (j - 1), rest, before)
                if now is not None:
                    out = jnp.where(lane >= tail * j, now, out)
            start = pl.multiple_of(a * group + LANES * j, LANES)
            at_ref[:, pl.ds(start, LANES)] = out.astype(at_ref.dtype)
            before = now
            if j < per:
                packed = block[rank:]
                rest = jnp.concatenate(
                    [
                        packed if b == j else pltpu.roll(packed, tail * ((j - b) % per), axis=1)
                        for b in range(per)
                    ],
                    axis=0,
                )
        return carry

    lax.fori_loop(0, shards // per, unpack, 0)

    tok = tok_ref[...]
    cot = cot_ref[...]
    hidden = lax.dot_general(
        at_ref[:, :depth], tok, NT, preferred_element_type=f32
    ).astype(bf16)
    back = lax.dot_general(
        at_ref[:, depth:width], cot, NT, preferred_element_type=f32
    ).astype(bf16)
    at_ref[:, width : width + LANES] = hidden
    at_ref[:, width + LANES :] = back
    t_ref[:, :depth] = adapter_scale * jnp.dot(back, tok, preferred_element_type=f32)
    t_ref[:, depth:] = adapter_scale * jnp.dot(hidden, cot, preferred_element_type=f32)

    def pack(a, carry):
        cols = [
            t_ref[:, pl.ds(pl.multiple_of(a * group + LANES * j, LANES), LANES)]
            for j in range(per + 1)
        ]
        for j in range(per):
            main = jnp.where(lane >= tail * j, cols[j], cols[j + 1])
            if j:
                main = pltpu.roll(main, LANES - tail * j, axis=1)
            packed = jnp.zeros((8, LANES), f32)
            for b in range(per):
                piece = cols[j + 1][8 * b : 8 * b + 8]
                if b != j:
                    piece = pltpu.roll(piece, tail * ((b - j) % per), axis=1)
                packed = jnp.where(lane8 // tail == b, piece, packed)
            terms_ref[a * per + j] = jnp.concatenate([main, packed], axis=0).astype(
                terms_ref.dtype
            )
        return carry

    lax.fori_loop(0, shards // per, pack, 0)


def base_kernel(tok_ref, cot_ref, w_ref, at_ref, up_ref, hid_ref, back_ref, keys_ref, grad_ref, acc_ref):
    step = pl.program_id(0)

    @pl.when(step == 0)
    def _():
        acc_ref[...] = adapter_scale * lax.dot_general(
            hid_ref[...], up_ref[...], TN, preferred_element_type=f32
        )

    weight = w_ref[...]
    acc_ref[...] += jnp.dot(tok_ref[...], weight, preferred_element_type=f32)
    grad = lax.dot_general(cot_ref[...], weight, NT, preferred_element_type=f32)
    grad += adapter_scale * lax.dot_general(
        back_ref[...], at_ref[...], TN, preferred_element_type=f32
    )
    grad_ref[...] = grad.astype(grad_ref.dtype)

    @pl.when(step == pl.num_programs(0) - 1)
    def _():
        keys_ref[...] = acc_ref[...].astype(keys_ref.dtype)


def shift(x, by, groups):
    return lax.ppermute(x, "grp", [(i, (i + by) % groups) for i in range(groups)])


def whole(memory=pltpu.VMEM):
    return pl.BlockSpec(memory_space=memory)


def on_device(tokens, cotangent, frozen_weight, adapters, tile_job, job_slot):
    rows, depth = tokens.shape
    key_columns = cotangent.shape[1]
    slot_count, row_count, rank = adapters.shape
    groups = lax.axis_size("grp")
    shards = lax.axis_size(SEQ)
    packed_rows = row_count * rank // LANES
    width = depth + key_columns
    group = lax.axis_index("grp").reshape(1).astype(jnp.int32)
    jobs = tile_job.reshape(-1)

    weight = lax.all_gather(frozen_weight, SEQ, axis=0, tiled=True)

    own = pl.pallas_call(
        pack_kernel,
        out_shape=jax.ShapeDtypeStruct((slot_count, packed_rows, LANES), bf16),
        in_specs=[whole()],
        out_specs=whole(),
        compiler_params=params(),
        name="pack",
    )(jnp.swapaxes(adapters, 1, 2))
    every = (own,) + tuple(shift(own, -k, groups) for k in range(1, groups))
    smem = whole(pltpu.SMEM)
    outgoing = pl.pallas_call(
        pick_kernel,
        out_shape=jax.ShapeDtypeStruct((shards, packed_rows, LANES), bf16),
        in_specs=[smem, smem, smem] + [whole()] * groups,
        out_specs=whole(),
        scratch_shapes=[pltpu.VMEM((groups * slot_count, packed_rows, LANES), bf16)],
        compiler_params=params(),
        name="pick",
    )(group, jobs, job_slot, *every)
    arrived = lax.all_to_all(outgoing, SEQ, split_axis=0, concat_axis=0, tiled=True)
    terms, adapter = pl.pallas_call(
        tile_kernel,
        out_shape=(
            jax.ShapeDtypeStruct((shards, packed_rows, LANES), bf16),
            jax.ShapeDtypeStruct((rank, width + 2 * rows), bf16),
        ),
        in_specs=[whole()] * 3,
        out_specs=(whole(),) * 2,
        scratch_shapes=[pltpu.VMEM((rank, width), f32)],
        compiler_params=params(),
        name="tile",
    )(arrived, tokens, cotangent)
    incoming = lax.all_to_all(terms, SEQ, split_axis=0, concat_axis=0, tiled=True)
    sums = pl.pallas_call(
        sum_kernel,
        out_shape=(jax.ShapeDtypeStruct((slot_count, packed_rows, LANES), f32),)
        + (jax.ShapeDtypeStruct((slot_count, packed_rows, LANES), bf16),) * (groups - 1),
        in_specs=[smem, smem, smem, whole()],
        out_specs=(whole(),) * groups,
        scratch_shapes=[pltpu.VMEM((groups * slot_count, packed_rows, LANES), f32)],
        compiler_params=params(),
        name="sum",
    )(group, jobs, job_slot, incoming)
    last, weight = lax.optimization_barrier((sums[-1], weight))
    sums = tuple(sums[:-1]) + (last,)
    owned = (sums[0],) + tuple(shift(sums[k], k, groups) for k in range(1, groups))
    grads = pl.pallas_call(
        unpack_kernel,
        out_shape=jax.ShapeDtypeStruct((slot_count, rank, row_count), f32),
        in_specs=[whole()] * groups,
        out_specs=whole(),
        compiler_params=params(),
        name="unpack",
    )(*owned)

    block = 1024
    steps = depth // block
    keys, token_gradient = pl.pallas_call(
        base_kernel,
        grid=(steps,),
        out_shape=(
            jax.ShapeDtypeStruct((rows, key_columns), bf16),
            jax.ShapeDtypeStruct((rows, depth), bf16),
        ),
        in_specs=[
            pl.BlockSpec((rows, block), lambda i: (0, i)),
            pl.BlockSpec((rows, key_columns), lambda i: (0, 0)),
            pl.BlockSpec((block, key_columns), lambda i: (i, 0)),
            pl.BlockSpec((rank, block), lambda i: (0, i)),
            pl.BlockSpec((rank, key_columns), lambda i: (0, depth // key_columns)),
            pl.BlockSpec((rank, rows), lambda i: (0, width // rows)),
            pl.BlockSpec((rank, rows), lambda i: (0, width // rows + 1)),
        ],
        out_specs=(
            pl.BlockSpec((rows, key_columns), lambda i: (0, 0)),
            pl.BlockSpec((rows, block), lambda i: (0, i)),
        ),
        scratch_shapes=[pltpu.VMEM((rows, key_columns), f32)],
        compiler_params=params(56),
        cost_estimate=pl.CostEstimate(
            flops=4 * rows * depth * key_columns,
            bytes_accessed=2 * depth * key_columns + 4 * rows * width,
            transcendentals=0,
        ),
        name="base",
    )(tokens, cotangent, weight, adapter, adapter, adapter, adapter)
    return keys, token_gradient, jnp.swapaxes(grads, 1, 2)


def solution(mesh):
    groups, shards = mesh.devices.shape
    cores = 2
    deep = 8
    mesh = Mesh(
        mesh.devices.reshape(groups, shards // (cores * deep), deep, cores),
        ("grp", "y", "z", "core"),
    )
    every = ("grp",) + SEQ
    placed = (
        P(every, None),
        P(every, None),
        P(SEQ, None),
        P("grp", SEQ, None),
        P(),
        P(),
    )
    return jax.shard_map(
        on_device,
        mesh=mesh,
        in_specs=placed,
        out_specs=(P(every, None), P(every, None), P("grp", SEQ, None)),
        check_vma=False,
    )
```

```python
import jax
import jax.numpy as jnp
from jax import lax
from jax.experimental import pallas as pl
from jax.experimental.pallas import tpu as pltpu
from jax.sharding import Mesh
from jax.sharding import PartitionSpec as P

SEQ = ("y", "z", "core")
TILE_ROWS = 128
LANES = 128
adapter_scale = 0.5
f32 = jnp.float32
bf16 = jnp.bfloat16
NT = (((1,), (1,)), ((), ()))
TN = (((0,), (0,)), ((), ()))


def params(vmem_mib=32):
    return pltpu.CompilerParams(vmem_limit_bytes=vmem_mib * 1024 * 1024)


def pack_kernel(a_ref, o_ref):
    slots, rank, width = a_ref.shape
    tail = width - LANES
    for s in range(slots):
        o_ref[s, :rank, :] = a_ref[s, :, :LANES]
        rest = a_ref[s, :, LANES:].astype(f32)
        pieces = [rest[8 * b : 8 * b + 8, :] for b in range(LANES // tail)]
        o_ref[s, rank:, :] = jnp.concatenate(pieces, axis=1).astype(o_ref.dtype)


def pick_kernel(group_ref, job_ref, slot_ref, *refs):
    sources, (o_ref, every_ref) = refs[:-2], refs[-2:]
    tiles = o_ref.shape[0]
    count = sources[0].shape[0]
    me = group_ref[0]
    for k, source in enumerate(sources):
        every_ref[pl.ds(lax.rem(me + k, len(sources)) * count, count)] = source[...]

    def step(t, carry):
        o_ref[t] = every_ref[slot_ref[job_ref[me * tiles + t]]]
        return carry

    lax.fori_loop(0, tiles, step, 0, unroll=4)


def sum_kernel(group_ref, job_ref, slot_ref, x_ref, *refs):
    sinks, sum_ref = refs[:-1], refs[-1]
    tiles = x_ref.shape[0]
    count = sinks[0].shape[0]
    me = group_ref[0]
    sum_ref[...] = jnp.zeros_like(sum_ref)

    def step(t, carry):
        s = slot_ref[job_ref[me * tiles + t]]
        sum_ref[s] = sum_ref[s] + x_ref[t].astype(f32)
        return carry

    lax.fori_loop(0, tiles, step, 0, unroll=4)
    for k, sink in enumerate(sinks):
        sink[...] = sum_ref[pl.ds(lax.rem(me + k, len(sinks)) * count, count)].astype(sink.dtype)


def unpack_kernel(x0_ref, x1_ref, x2_ref, x3_ref, o_ref):
    slots, rank, width = o_ref.shape
    tail = width - LANES
    for s in range(slots):
        total = x0_ref[s] + (x1_ref[s].astype(f32) + x2_ref[s].astype(f32)) + x3_ref[s].astype(f32)
        o_ref[s, :, :LANES] = total[:rank]
        rest = total[rank:]
        for b in range(LANES // tail):
            o_ref[s, 8 * b : 8 * b + 8, LANES:] = rest[:, tail * b : tail * (b + 1)]


def tile_kernel(x_ref, tok_ref, cot_ref, terms_ref, at_ref, t_ref):
    shards, _, _ = x_ref.shape
    rank = at_ref.shape[0]
    depth = tok_ref.shape[1]
    width = depth + cot_ref.shape[1]
    tail = width // shards - LANES
    per = LANES // tail
    group = per * (LANES + tail)
    lane = lax.broadcasted_iota(jnp.int32, (rank, LANES), 1)
    lane8 = lax.broadcasted_iota(jnp.int32, (8, LANES), 1)

    def unpack(a, carry):
        before = None
        for j in range(per + 1):
            if j < per:
                block = x_ref[a * per + j].astype(f32)
                main = block[:rank]
                now = main if j == 0 else pltpu.roll(main, tail * j, axis=1)
            else:
                now = None
            if before is None:
                out = now
            else:
                out = jnp.where(lane >= tail * (j - 1), rest, before)
                if now is not None:
                    out = jnp.where(lane >= tail * j, now, out)
            start = pl.multiple_of(a * group + LANES * j, LANES)
            at_ref[:, pl.ds(start, LANES)] = out.astype(at_ref.dtype)
            before = now
            if j < per:
                packed = block[rank:]
                rest = jnp.concatenate(
                    [
                        packed if b == j else pltpu.roll(packed, tail * ((j - b) % per), axis=1)
                        for b in range(per)
                    ],
                    axis=0,
                )
        return carry

    lax.fori_loop(0, shards // per, unpack, 0)

    tok = tok_ref[...]
    cot = cot_ref[...]
    hidden = lax.dot_general(
        at_ref[:, :depth], tok, NT, preferred_element_type=f32
    ).astype(bf16)
    back = lax.dot_general(
        at_ref[:, depth:width], cot, NT, preferred_element_type=f32
    ).astype(bf16)
    at_ref[:, width : width + LANES] = hidden
    at_ref[:, width + LANES :] = back
    t_ref[:, :depth] = adapter_scale * jnp.dot(back, tok, preferred_element_type=f32)
    t_ref[:, depth:] = adapter_scale * jnp.dot(hidden, cot, preferred_element_type=f32)

    def pack(a, carry):
        cols = [
            t_ref[:, pl.ds(pl.multiple_of(a * group + LANES * j, LANES), LANES)]
            for j in range(per + 1)
        ]
        for j in range(per):
            main = jnp.where(lane >= tail * j, cols[j], cols[j + 1])
            if j:
                main = pltpu.roll(main, LANES - tail * j, axis=1)
            packed = jnp.zeros((8, LANES), f32)
            for b in range(per):
                piece = cols[j + 1][8 * b : 8 * b + 8]
                if b != j:
                    piece = pltpu.roll(piece, tail * ((b - j) % per), axis=1)
                packed = jnp.where(lane8 // tail == b, piece, packed)
            terms_ref[a * per + j] = jnp.concatenate([main, packed], axis=0).astype(
                terms_ref.dtype
            )
        return carry

    lax.fori_loop(0, shards // per, pack, 0)


def base_kernel(z_ref, tok_ref, cot_ref, w_ref, at_ref, up_ref, hid_ref, back_ref, keys_ref, grad_ref, acc_ref):
    step = pl.program_id(0) * pl.num_programs(1) + pl.program_id(1)
    _, pieces, count, quarter, _ = w_ref.shape
    span = pieces * quarter
    deep = count * pl.num_programs(1)
    order = [x * 2 + c for c in range(2) for x in range(pieces // 2)]

    @pl.when(step == 0)
    def _():
        acc_ref[...] = adapter_scale * lax.dot_general(
            hid_ref[...], up_ref[...], TN, preferred_element_type=f32
        )

    places = []
    for k in range(count):
        place = lax.rem(z_ref[0] - (pl.program_id(1) * count + k) + deep, deep)
        places.append(pl.ds(pl.multiple_of(place * span, span), span))
    weight = jnp.concatenate([w_ref[0, p, k] for k in range(count) for p in order], axis=0)
    tok = jnp.concatenate([tok_ref[:, at] for at in places], axis=1)
    down = jnp.concatenate([at_ref[:, at] for at in places], axis=1)
    acc_ref[...] += jnp.dot(tok, weight, preferred_element_type=f32)
    grad = lax.dot_general(cot_ref[...], weight, NT, preferred_element_type=f32)
    grad += adapter_scale * lax.dot_general(back_ref[...], down, TN, preferred_element_type=f32)
    grad = grad.astype(grad_ref.dtype)
    for k, at in enumerate(places):
        grad_ref[:, at] = grad[:, k * span : (k + 1) * span]

    @pl.when(step == pl.num_programs(0) * pl.num_programs(1) - 1)
    def _():
        keys_ref[...] = acc_ref[...].astype(keys_ref.dtype)


def shift(x, by, groups):
    return lax.ppermute(x, "grp", [(i, (i + by) % groups) for i in range(groups)])


def ring(x, axis, size):
    up = [x]
    down = [x]
    for _ in range(size // 2):
        up.append(lax.ppermute(up[-1], axis, [(i, (i + 1) % size) for i in range(size)]))
    for _ in range(size // 2 - 1):
        down.append(lax.ppermute(down[-1], axis, [(i, (i - 1) % size) for i in range(size)]))
    return jnp.concatenate(up + down[:0:-1], axis=0)


def whole(memory=pltpu.VMEM):
    return pl.BlockSpec(memory_space=memory)


def on_device(tokens, cotangent, frozen_weight, adapters, tile_job, job_slot):
    rows, depth = tokens.shape
    key_columns = cotangent.shape[1]
    slot_count, row_count, rank = adapters.shape
    groups = lax.axis_size("grp")
    shards = lax.axis_size(SEQ)
    packed_rows = row_count * rank // LANES
    width = depth + key_columns
    group = lax.axis_index("grp").reshape(1).astype(jnp.int32)
    z = lax.axis_index("z").reshape(1).astype(jnp.int32)
    jobs = tile_job.reshape(-1)

    quarter = TILE_ROWS // groups
    mine = lax.dynamic_slice_in_dim(frozen_weight, lax.axis_index("grp") * quarter, quarter, 0)
    column = ring(mine, "z", lax.axis_size("z"))

    own = pl.pallas_call(
        pack_kernel,
        out_shape=jax.ShapeDtypeStruct((slot_count, packed_rows, LANES), bf16),
        in_specs=[whole()],
        out_specs=whole(),
        compiler_params=params(),
        name="pack",
    )(jnp.swapaxes(adapters, 1, 2))
    every = (own,) + tuple(shift(own, -k, groups) for k in range(1, groups))
    smem = whole(pltpu.SMEM)
    outgoing = pl.pallas_call(
        pick_kernel,
        out_shape=jax.ShapeDtypeStruct((shards, packed_rows, LANES), bf16),
        in_specs=[smem, smem, smem] + [whole()] * groups,
        out_specs=whole(),
        scratch_shapes=[pltpu.VMEM((groups * slot_count, packed_rows, LANES), bf16)],
        compiler_params=params(),
        name="pick",
    )(group, jobs, job_slot, *every)
    outgoing, column = lax.optimization_barrier((outgoing, column))
    weight = lax.all_gather(column, ("y", "grp", "core"), axis=0, tiled=True)
    arrived = lax.all_to_all(outgoing, SEQ, split_axis=0, concat_axis=0, tiled=True)
    terms, adapter = pl.pallas_call(
        tile_kernel,
        out_shape=(
            jax.ShapeDtypeStruct((shards, packed_rows, LANES), bf16),
            jax.ShapeDtypeStruct((rank, width + 2 * rows), bf16),
        ),
        in_specs=[whole()] * 3,
        out_specs=(whole(),) * 2,
        scratch_shapes=[pltpu.VMEM((rank, width), f32)],
        compiler_params=params(),
        name="tile",
    )(arrived, tokens, cotangent)
    incoming = lax.all_to_all(terms, SEQ, split_axis=0, concat_axis=0, tiled=True)
    sums = pl.pallas_call(
        sum_kernel,
        out_shape=(jax.ShapeDtypeStruct((slot_count, packed_rows, LANES), f32),)
        + (jax.ShapeDtypeStruct((slot_count, packed_rows, LANES), bf16),) * (groups - 1),
        in_specs=[smem, smem, smem, whole()],
        out_specs=(whole(),) * groups,
        scratch_shapes=[pltpu.VMEM((groups * slot_count, packed_rows, LANES), f32)],
        compiler_params=params(),
        name="sum",
    )(group, jobs, job_slot, incoming)
    last, weight = lax.optimization_barrier((sums[-1], weight))
    sums = tuple(sums[:-1]) + (last,)
    owned = (sums[0],) + tuple(shift(sums[k], k, groups) for k in range(1, groups))
    grads = pl.pallas_call(
        unpack_kernel,
        out_shape=jax.ShapeDtypeStruct((slot_count, rank, row_count), f32),
        in_specs=[whole()] * groups,
        out_specs=whole(),
        compiler_params=params(),
        name="unpack",
    )(*owned)

    wide, deep, halves = lax.axis_size("y"), lax.axis_size("z"), 2
    span = depth // wide
    weight = weight.reshape(wide, shards // (wide * deep) * groups, deep, quarter, key_columns)
    keys, token_gradient = pl.pallas_call(
        base_kernel,
        grid=(wide, halves),
        out_shape=(
            jax.ShapeDtypeStruct((rows, key_columns), bf16),
            jax.ShapeDtypeStruct((rows, depth), bf16),
        ),
        in_specs=[
            smem,
            pl.BlockSpec((rows, span), lambda i, h: (0, i)),
            pl.BlockSpec((rows, key_columns), lambda i, h: (0, 0)),
            pl.BlockSpec(
                (1, weight.shape[1], deep // halves, quarter, key_columns),
                lambda i, h: (i, 0, h, 0, 0),
            ),
            pl.BlockSpec((rank, span), lambda i, h: (0, i)),
            pl.BlockSpec((rank, key_columns), lambda i, h: (0, depth // key_columns)),
            pl.BlockSpec((rank, rows), lambda i, h: (0, width // rows)),
            pl.BlockSpec((rank, rows), lambda i, h: (0, width // rows + 1)),
        ],
        out_specs=(
            pl.BlockSpec((rows, key_columns), lambda i, h: (0, 0)),
            pl.BlockSpec((rows, span), lambda i, h: (0, i)),
        ),
        scratch_shapes=[pltpu.VMEM((rows, key_columns), f32)],
        compiler_params=params(56),
        cost_estimate=pl.CostEstimate(
            flops=4 * rows * depth * key_columns,
            bytes_accessed=2 * depth * key_columns + 4 * rows * width,
            transcendentals=0,
        ),
        name="base",
    )(z, tokens, cotangent, weight, adapter, adapter, adapter, adapter)
    return keys, token_gradient, jnp.swapaxes(grads, 1, 2)


def solution(mesh):
    groups, shards = mesh.devices.shape
    cores = 2
    deep = 8
    mesh = Mesh(
        mesh.devices.reshape(groups, shards // (cores * deep), deep, cores),
        ("grp", "y", "z", "core"),
    )
    every = ("grp",) + SEQ
    placed = (
        P(every, None),
        P(every, None),
        P(SEQ, None),
        P("grp", SEQ, None),
        P(),
        P(),
    )
    return jax.shard_map(
        on_device,
        mesh=mesh,
        in_specs=placed,
        out_specs=(P(every, None), P(every, None), P("grp", SEQ, None)),
        check_vma=False,
    )
```

```python
import jax
import jax.numpy as jnp
from jax import lax
from jax.experimental import pallas as pl
from jax.experimental.pallas import tpu as pltpu
from jax.sharding import Mesh
from jax.sharding import PartitionSpec as P

SEQ = ("y", "z", "core")
TILE_ROWS = 128
LANES = 128
adapter_scale = 0.5
f32 = jnp.float32
bf16 = jnp.bfloat16
NT = (((1,), (1,)), ((), ()))
TN = (((0,), (0,)), ((), ()))


def params(vmem_mib=32):
    return pltpu.CompilerParams(vmem_limit_bytes=vmem_mib * 1024 * 1024)


def pack_kernel(a_ref, o_ref):
    slots, rank, width = a_ref.shape
    tail = width - LANES
    for s in range(slots):
        o_ref[s, :rank, :] = a_ref[s, :, :LANES]
        rest = a_ref[s, :, LANES:].astype(f32)
        pieces = [rest[8 * b : 8 * b + 8, :] for b in range(LANES // tail)]
        o_ref[s, rank:, :] = jnp.concatenate(pieces, axis=1).astype(o_ref.dtype)


def pick_kernel(group_ref, job_ref, slot_ref, *refs):
    sources, (o_ref, every_ref) = refs[:-2], refs[-2:]
    tiles = o_ref.shape[0]
    count = sources[0].shape[0]
    me = group_ref[0]
    for k, source in enumerate(sources):
        every_ref[pl.ds(lax.rem(me + k, len(sources)) * count, count)] = source[...]

    def step(t, carry):
        o_ref[t] = every_ref[slot_ref[job_ref[me * tiles + t]]]
        return carry

    lax.fori_loop(0, tiles, step, 0, unroll=4)


def sum_kernel(group_ref, job_ref, slot_ref, x_ref, *refs):
    sinks, sum_ref = refs[:-1], refs[-1]
    tiles = x_ref.shape[0]
    count = sinks[0].shape[0]
    me = group_ref[0]
    sum_ref[...] = jnp.zeros_like(sum_ref)

    def step(t, carry):
        s = slot_ref[job_ref[me * tiles + t]]
        sum_ref[s] = sum_ref[s] + x_ref[t].astype(f32)
        return carry

    lax.fori_loop(0, tiles, step, 0, unroll=4)
    for k, sink in enumerate(sinks):
        sink[...] = sum_ref[pl.ds(lax.rem(me + k, len(sinks)) * count, count)].astype(sink.dtype)


def unpack_kernel(x0_ref, x1_ref, x2_ref, x3_ref, o_ref):
    slots, rank, width = o_ref.shape
    tail = width - LANES
    for s in range(slots):
        total = x0_ref[s] + (x1_ref[s].astype(f32) + x2_ref[s].astype(f32)) + x3_ref[s].astype(f32)
        o_ref[s, :, :LANES] = total[:rank]
        rest = total[rank:]
        for b in range(LANES // tail):
            o_ref[s, 8 * b : 8 * b + 8, LANES:] = rest[:, tail * b : tail * (b + 1)]


def tile_kernel(x_ref, tok_ref, cot_ref, terms_ref, at_ref, t_ref):
    shards, _, _ = x_ref.shape
    rank = at_ref.shape[0]
    depth = tok_ref.shape[1]
    width = depth + cot_ref.shape[1]
    tail = width // shards - LANES
    per = LANES // tail
    group = per * (LANES + tail)
    lane = lax.broadcasted_iota(jnp.int32, (rank, LANES), 1)
    lane8 = lax.broadcasted_iota(jnp.int32, (8, LANES), 1)

    def unpack(a, carry):
        before = None
        for j in range(per + 1):
            if j < per:
                block = x_ref[a * per + j].astype(f32)
                main = block[:rank]
                now = main if j == 0 else pltpu.roll(main, tail * j, axis=1)
            else:
                now = None
            if before is None:
                out = now
            else:
                out = jnp.where(lane >= tail * (j - 1), rest, before)
                if now is not None:
                    out = jnp.where(lane >= tail * j, now, out)
            start = pl.multiple_of(a * group + LANES * j, LANES)
            at_ref[:, pl.ds(start, LANES)] = out.astype(at_ref.dtype)
            before = now
            if j < per:
                packed = block[rank:]
                rest = jnp.concatenate(
                    [
                        packed if b == j else pltpu.roll(packed, tail * ((j - b) % per), axis=1)
                        for b in range(per)
                    ],
                    axis=0,
                )
        return carry

    lax.fori_loop(0, shards // per, unpack, 0)

    tok = tok_ref[...]
    cot = cot_ref[...]
    hidden = lax.dot_general(
        at_ref[:, :depth], tok, NT, preferred_element_type=f32
    ).astype(bf16)
    back = lax.dot_general(
        at_ref[:, depth:width], cot, NT, preferred_element_type=f32
    ).astype(bf16)
    at_ref[:, width : width + LANES] = hidden
    at_ref[:, width + LANES :] = back
    t_ref[:, :depth] = adapter_scale * jnp.dot(back, tok, preferred_element_type=f32)
    t_ref[:, depth:] = adapter_scale * jnp.dot(hidden, cot, preferred_element_type=f32)

    def pack(a, carry):
        cols = [
            t_ref[:, pl.ds(pl.multiple_of(a * group + LANES * j, LANES), LANES)]
            for j in range(per + 1)
        ]
        for j in range(per):
            main = jnp.where(lane >= tail * j, cols[j], cols[j + 1])
            if j:
                main = pltpu.roll(main, LANES - tail * j, axis=1)
            packed = jnp.zeros((8, LANES), f32)
            for b in range(per):
                piece = cols[j + 1][8 * b : 8 * b + 8]
                if b != j:
                    piece = pltpu.roll(piece, tail * ((b - j) % per), axis=1)
                packed = jnp.where(lane8 // tail == b, piece, packed)
            terms_ref[a * per + j] = jnp.concatenate([main, packed], axis=0).astype(
                terms_ref.dtype
            )
        return carry

    lax.fori_loop(0, shards // per, pack, 0)


def columns(place_ref, y, k, parity, counts):
    deep, cores = counts
    z = lax.rem(place_ref[0] - k + deep, deep)
    start = ((y * deep + z) * cores + parity) * TILE_ROWS
    return pl.ds(pl.multiple_of(start, TILE_ROWS), TILE_ROWS)


def products(tok_ref, cot_ref, weight, adapter_ref, back, places):
    tok = jnp.concatenate([tok_ref[:, at] for at in places], axis=1)
    down = jnp.concatenate([adapter_ref[:, at] for at in places], axis=1)
    key = jnp.dot(tok, weight, preferred_element_type=f32)
    grad = lax.dot_general(cot_ref[...], weight, NT, preferred_element_type=f32)
    grad += adapter_scale * lax.dot_general(back, down, TN, preferred_element_type=f32)
    return key, grad.astype(bf16)


def fetch(source_ref, w_ref, sems):
    wide, groups = w_ref.shape[:2]
    copies = [
        [pltpu.make_async_copy(source_ref.at[y, x], w_ref.at[y, x], sems.at[y, x]) for x in range(groups)]
        for y in range(wide)
    ]
    for row in copies:
        for copy in row:
            copy.start()
    return copies


def block(copies, w_ref, y):
    groups, deep = w_ref.shape[1:3]
    for copy in copies[y]:
        copy.wait()
    return jnp.concatenate([w_ref[y, x, k] for k in range(deep) for x in range(groups)], axis=0)


def own_kernel(place_ref, tok_ref, cot_ref, half_ref, adapter_ref, key_ref, grad_ref, w_ref, sems):
    wide, _, deep, _, key_columns = half_ref.shape
    rows, depth = tok_ref.shape
    width = depth + key_columns
    span = deep * TILE_ROWS
    copies = fetch(half_ref, w_ref, sems)
    hidden = adapter_ref[:, width : width + rows]
    back = adapter_ref[:, width + rows :]
    up = adapter_ref[:, depth:width]
    key_ref[...] = adapter_scale * lax.dot_general(hidden, up, TN, preferred_element_type=f32)
    for y in range(wide):
        weight = block(copies, w_ref, y)
        places = [columns(place_ref, y, k, place_ref[1], (deep, 2)) for k in range(deep)]
        key, grad = products(tok_ref, cot_ref, weight, adapter_ref, back, places)
        key_ref[...] += key
        grad_ref[:, y * span : (y + 1) * span] = grad


def other_kernel(
    place_ref, tok_ref, cot_ref, half_ref, adapter_ref, key_ref, own_ref, keys_ref, grad_ref, acc_ref, w_ref, sems
):
    wide, _, deep, _, key_columns = half_ref.shape
    rows, depth = tok_ref.shape
    copies = fetch(half_ref, w_ref, sems)
    back = adapter_ref[:, depth + key_columns + rows :]
    acc_ref[...] = key_ref[...]
    for y in range(wide):
        weight = block(copies, w_ref, y)
        places = [columns(place_ref, y, k, 1 - place_ref[1], (deep, 2)) for k in range(deep)]
        key, grad = products(tok_ref, cot_ref, weight, adapter_ref, back, places)
        acc_ref[...] += key
        for k in range(deep):
            at = (y * deep + k) * TILE_ROWS
            grad_ref[:, columns(place_ref, y, k, place_ref[1], (deep, 2))] = own_ref[:, at : at + TILE_ROWS]
            grad_ref[:, places[k]] = grad[:, k * TILE_ROWS : (k + 1) * TILE_ROWS]
    keys_ref[...] = acc_ref[...].astype(keys_ref.dtype)


def shift(x, by, groups):
    return lax.ppermute(x, "grp", [(i, (i + by) % groups) for i in range(groups)])


def ring(x, axis, size):
    up = [x]
    down = [x]
    for _ in range(size // 2):
        up.append(lax.ppermute(up[-1], axis, [(i, (i + 1) % size) for i in range(size)]))
    for _ in range(size // 2 - 1):
        down.append(lax.ppermute(down[-1], axis, [(i, (i - 1) % size) for i in range(size)]))
    return jnp.concatenate(up + down[:0:-1], axis=0)


def whole(memory=pltpu.VMEM):
    return pl.BlockSpec(memory_space=memory)


def on_device(tokens, cotangent, frozen_weight, adapters, tile_job, job_slot):
    rows, depth = tokens.shape
    key_columns = cotangent.shape[1]
    slot_count, row_count, rank = adapters.shape
    groups = lax.axis_size("grp")
    shards = lax.axis_size(SEQ)
    packed_rows = row_count * rank // LANES
    width = depth + key_columns
    group = lax.axis_index("grp").reshape(1).astype(jnp.int32)
    place = jnp.stack([lax.axis_index("z"), lax.axis_index("core")]).astype(jnp.int32)
    jobs = tile_job.reshape(-1)

    quarter = TILE_ROWS // groups
    mine = lax.dynamic_slice_in_dim(frozen_weight, lax.axis_index("grp") * quarter, quarter, 0)
    column = ring(mine, "z", lax.axis_size("z"))

    own = pl.pallas_call(
        pack_kernel,
        out_shape=jax.ShapeDtypeStruct((slot_count, packed_rows, LANES), bf16),
        in_specs=[whole()],
        out_specs=whole(),
        compiler_params=params(),
        name="pack",
    )(jnp.swapaxes(adapters, 1, 2))
    every = (own,) + tuple(shift(own, -k, groups) for k in range(1, groups))
    smem = whole(pltpu.SMEM)
    outgoing = pl.pallas_call(
        pick_kernel,
        out_shape=jax.ShapeDtypeStruct((shards, packed_rows, LANES), bf16),
        in_specs=[smem, smem, smem] + [whole()] * groups,
        out_specs=whole(),
        scratch_shapes=[pltpu.VMEM((groups * slot_count, packed_rows, LANES), bf16)],
        compiler_params=params(),
        name="pick",
    )(group, jobs, job_slot, *every)
    outgoing, column = lax.optimization_barrier((outgoing, column))
    half = lax.all_gather(column, ("y", "grp"), axis=0, tiled=True)
    arrived = lax.all_to_all(outgoing, SEQ, split_axis=0, concat_axis=0, tiled=True)
    terms, adapter = pl.pallas_call(
        tile_kernel,
        out_shape=(
            jax.ShapeDtypeStruct((shards, packed_rows, LANES), bf16),
            jax.ShapeDtypeStruct((rank, width + 2 * rows), bf16),
        ),
        in_specs=[whole()] * 3,
        out_specs=(whole(),) * 2,
        scratch_shapes=[pltpu.VMEM((rank, width), f32)],
        compiler_params=params(),
        name="tile",
    )(arrived, tokens, cotangent)
    incoming = lax.all_to_all(terms, SEQ, split_axis=0, concat_axis=0, tiled=True)
    incoming, half = lax.optimization_barrier((incoming, half))
    other = lax.ppermute(half, "core", [(0, 1), (1, 0)])
    sums = pl.pallas_call(
        sum_kernel,
        out_shape=(jax.ShapeDtypeStruct((slot_count, packed_rows, LANES), f32),)
        + (jax.ShapeDtypeStruct((slot_count, packed_rows, LANES), bf16),) * (groups - 1),
        in_specs=[smem, smem, smem, whole()],
        out_specs=(whole(),) * groups,
        scratch_shapes=[pltpu.VMEM((groups * slot_count, packed_rows, LANES), f32)],
        compiler_params=params(),
        name="sum",
    )(group, jobs, job_slot, incoming)
    kept, half = lax.optimization_barrier((sums[0], half))
    wide, deep = lax.axis_size("y"), lax.axis_size("z")
    blocks = (wide, groups, deep, quarter, key_columns)
    cost = pl.CostEstimate(
        flops=2 * rows * depth * key_columns,
        bytes_accessed=depth * key_columns + 4 * rows * width,
        transcendentals=0,
    )
    key_part, own_part = pl.pallas_call(
        own_kernel,
        out_shape=(
            jax.ShapeDtypeStruct((rows, key_columns), f32),
            jax.ShapeDtypeStruct((rows, depth // 2), bf16),
        ),
        in_specs=[smem, whole(), whole(), whole(pltpu.HBM), whole()],
        out_specs=(whole(),) * 2,
        scratch_shapes=[pltpu.VMEM(blocks, bf16), pltpu.SemaphoreType.DMA((wide, groups))],
        compiler_params=params(50),
        cost_estimate=cost,
        name="own",
    )(place, tokens, cotangent, half.reshape(blocks), adapter)
    last, other, key_part = lax.optimization_barrier((sums[-1], other, key_part))
    sums = (kept,) + tuple(sums[1:-1]) + (last,)
    owned = (sums[0],) + tuple(shift(sums[k], k, groups) for k in range(1, groups))
    grads = pl.pallas_call(
        unpack_kernel,
        out_shape=jax.ShapeDtypeStruct((slot_count, rank, row_count), f32),
        in_specs=[whole()] * groups,
        out_specs=whole(),
        compiler_params=params(),
        name="unpack",
    )(*owned)

    keys, token_gradient = pl.pallas_call(
        other_kernel,
        out_shape=(
            jax.ShapeDtypeStruct((rows, key_columns), bf16),
            jax.ShapeDtypeStruct((rows, depth), bf16),
        ),
        in_specs=[smem, whole(), whole(), whole(pltpu.HBM), whole(), whole(), whole()],
        out_specs=(whole(),) * 2,
        scratch_shapes=[
            pltpu.VMEM((rows, key_columns), f32),
            pltpu.VMEM(blocks, bf16),
            pltpu.SemaphoreType.DMA((wide, groups)),
        ],
        compiler_params=params(50),
        cost_estimate=cost,
        name="other",
    )(place, tokens, cotangent, other.reshape(blocks), adapter, key_part, own_part)
    return keys, token_gradient, jnp.swapaxes(grads, 1, 2)


def solution(mesh):
    groups, shards = mesh.devices.shape
    cores = 2
    deep = 8
    mesh = Mesh(
        mesh.devices.reshape(groups, shards // (cores * deep), deep, cores),
        ("grp", "y", "z", "core"),
    )
    every = ("grp",) + SEQ
    placed = (
        P(every, None),
        P(every, None),
        P(SEQ, None),
        P("grp", SEQ, None),
        P(),
        P(),
    )
    return jax.shard_map(
        on_device,
        mesh=mesh,
        in_specs=placed,
        out_specs=(P(every, None), P(every, None), P("grp", SEQ, None)),
        check_vma=False,
    )
```

```python
import jax
import jax.numpy as jnp
from jax import lax
from jax.experimental import pallas as pl
from jax.experimental.pallas import tpu as pltpu
from jax.sharding import Mesh
from jax.sharding import PartitionSpec as P

SEQ = ("y", "z", "core")
TILE_ROWS = 128
LANES = 128
adapter_scale = 0.5
f32 = jnp.float32
bf16 = jnp.bfloat16
NT = (((1,), (1,)), ((), ()))
TN = (((0,), (0,)), ((), ()))


def params(vmem_mib=32):
    return pltpu.CompilerParams(vmem_limit_bytes=vmem_mib * 1024 * 1024)


def pack_kernel(a_ref, o_ref):
    slots, rank, width = a_ref.shape
    tail = width - LANES
    for s in range(slots):
        o_ref[s, :rank, :] = a_ref[s, :, :LANES]
        rest = a_ref[s, :, LANES:].astype(f32)
        pieces = [rest[8 * b : 8 * b + 8, :] for b in range(LANES // tail)]
        o_ref[s, rank:, :] = jnp.concatenate(pieces, axis=1).astype(o_ref.dtype)


def pick_kernel(group_ref, job_ref, slot_ref, *refs):
    sources, (o_ref, every_ref) = refs[:-2], refs[-2:]
    tiles = o_ref.shape[0]
    count = sources[0].shape[0]
    me = group_ref[0]
    for k, source in enumerate(sources):
        every_ref[pl.ds(lax.rem(me + k, len(sources)) * count, count)] = source[...]

    def step(t, carry):
        o_ref[t] = every_ref[slot_ref[job_ref[me * tiles + t]]]
        return carry

    lax.fori_loop(0, tiles, step, 0, unroll=4)


def sum_kernel(group_ref, job_ref, slot_ref, x_ref, *refs):
    sinks, sum_ref = refs[:-1], refs[-1]
    tiles = x_ref.shape[0]
    count = sinks[0].shape[0]
    me = group_ref[0]
    sum_ref[...] = jnp.zeros_like(sum_ref)

    def step(t, carry):
        s = slot_ref[job_ref[me * tiles + t]]
        sum_ref[s] = sum_ref[s] + x_ref[t].astype(f32)
        return carry

    lax.fori_loop(0, tiles, step, 0, unroll=4)
    for k, sink in enumerate(sinks):
        sink[...] = sum_ref[pl.ds(lax.rem(me + k, len(sinks)) * count, count)].astype(sink.dtype)


def unpack_kernel(x0_ref, x1_ref, x2_ref, x3_ref, o_ref):
    slots, rank, width = o_ref.shape
    tail = width - LANES
    for s in range(slots):
        total = x0_ref[s] + (x1_ref[s].astype(f32) + x2_ref[s].astype(f32)) + x3_ref[s].astype(f32)
        o_ref[s, :, :LANES] = total[:rank]
        rest = total[rank:]
        for b in range(LANES // tail):
            o_ref[s, 8 * b : 8 * b + 8, LANES:] = rest[:, tail * b : tail * (b + 1)]


def tile_kernel(x_ref, tok_ref, cot_ref, terms_ref, at_ref, t_ref):
    shards, _, _ = x_ref.shape
    rank = at_ref.shape[0]
    depth = tok_ref.shape[1]
    width = depth + cot_ref.shape[1]
    tail = width // shards - LANES
    per = LANES // tail
    group = per * (LANES + tail)
    lane = lax.broadcasted_iota(jnp.int32, (rank, LANES), 1)
    lane8 = lax.broadcasted_iota(jnp.int32, (8, LANES), 1)

    def unpack(a, carry):
        before = None
        for j in range(per + 1):
            if j < per:
                block = x_ref[a * per + j].astype(f32)
                main = block[:rank]
                now = main if j == 0 else pltpu.roll(main, tail * j, axis=1)
            else:
                now = None
            if before is None:
                out = now
            else:
                out = jnp.where(lane >= tail * (j - 1), rest, before)
                if now is not None:
                    out = jnp.where(lane >= tail * j, now, out)
            start = pl.multiple_of(a * group + LANES * j, LANES)
            at_ref[:, pl.ds(start, LANES)] = out.astype(at_ref.dtype)
            before = now
            if j < per:
                packed = block[rank:]
                rest = jnp.concatenate(
                    [
                        packed if b == j else pltpu.roll(packed, tail * ((j - b) % per), axis=1)
                        for b in range(per)
                    ],
                    axis=0,
                )
        return carry

    lax.fori_loop(0, shards // per, unpack, 0)

    tok = tok_ref[...]
    cot = cot_ref[...]
    hidden = lax.dot_general(
        at_ref[:, :depth], tok, NT, preferred_element_type=f32
    ).astype(bf16)
    back = lax.dot_general(
        at_ref[:, depth:width], cot, NT, preferred_element_type=f32
    ).astype(bf16)
    at_ref[:, width : width + LANES] = hidden
    at_ref[:, width + LANES :] = back
    t_ref[:, :depth] = adapter_scale * jnp.dot(back, tok, preferred_element_type=f32)
    t_ref[:, depth:] = adapter_scale * jnp.dot(hidden, cot, preferred_element_type=f32)

    def pack(a, carry):
        cols = [
            t_ref[:, pl.ds(pl.multiple_of(a * group + LANES * j, LANES), LANES)]
            for j in range(per + 1)
        ]
        for j in range(per):
            main = jnp.where(lane >= tail * j, cols[j], cols[j + 1])
            if j:
                main = pltpu.roll(main, LANES - tail * j, axis=1)
            packed = jnp.zeros((8, LANES), f32)
            for b in range(per):
                piece = cols[j + 1][8 * b : 8 * b + 8]
                if b != j:
                    piece = pltpu.roll(piece, tail * ((b - j) % per), axis=1)
                packed = jnp.where(lane8 // tail == b, piece, packed)
            terms_ref[a * per + j] = jnp.concatenate([main, packed], axis=0).astype(
                terms_ref.dtype
            )
        return carry

    lax.fori_loop(0, shards // per, pack, 0)


def base_kernel(tok_ref, cot_ref, w_ref, at_ref, up_ref, hid_ref, back_ref, keys_ref, grad_ref, acc_ref):
    step = pl.program_id(0)
    _, pieces, count, _, _ = w_ref.shape
    order = [x * 2 + c for c in range(2) for x in range(pieces // 2)]

    @pl.when(step == 0)
    def _():
        acc_ref[...] = adapter_scale * lax.dot_general(
            hid_ref[...], up_ref[...], TN, preferred_element_type=f32
        )

    weight = jnp.concatenate([w_ref[0, p, k] for k in range(count) for p in order], axis=0)
    acc_ref[...] += jnp.dot(tok_ref[...], weight, preferred_element_type=f32)
    grad = lax.dot_general(cot_ref[...], weight, NT, preferred_element_type=f32)
    grad += adapter_scale * lax.dot_general(
        back_ref[...], at_ref[...], TN, preferred_element_type=f32
    )
    grad_ref[...] = grad.astype(grad_ref.dtype)

    @pl.when(step == pl.num_programs(0) - 1)
    def _():
        keys_ref[...] = acc_ref[...].astype(keys_ref.dtype)


def shift(x, by, groups):
    return lax.ppermute(x, "grp", [(i, (i + by) % groups) for i in range(groups)])


def whole(memory=pltpu.VMEM):
    return pl.BlockSpec(memory_space=memory)


def on_device(tokens, cotangent, frozen_weight, adapters, tile_job, job_slot):
    rows, depth = tokens.shape
    key_columns = cotangent.shape[1]
    slot_count, row_count, rank = adapters.shape
    groups = lax.axis_size("grp")
    shards = lax.axis_size(SEQ)
    packed_rows = row_count * rank // LANES
    width = depth + key_columns
    group = lax.axis_index("grp").reshape(1).astype(jnp.int32)
    jobs = tile_job.reshape(-1)

    quarter = TILE_ROWS // groups
    mine = lax.dynamic_slice_in_dim(frozen_weight, lax.axis_index("grp") * quarter, quarter, 0)
    deep = lax.axis_size("z")
    column = lax.all_to_all(
        jnp.broadcast_to(mine, (deep,) + mine.shape), "z", split_axis=0, concat_axis=0, tiled=True
    ).reshape(deep * quarter, -1)

    own = pl.pallas_call(
        pack_kernel,
        out_shape=jax.ShapeDtypeStruct((slot_count, packed_rows, LANES), bf16),
        in_specs=[whole()],
        out_specs=whole(),
        compiler_params=params(),
        name="pack",
    )(jnp.swapaxes(adapters, 1, 2))
    every = (own,) + tuple(shift(own, -k, groups) for k in range(1, groups))
    smem = whole(pltpu.SMEM)
    outgoing = pl.pallas_call(
        pick_kernel,
        out_shape=jax.ShapeDtypeStruct((shards, packed_rows, LANES), bf16),
        in_specs=[smem, smem, smem] + [whole()] * groups,
        out_specs=whole(),
        scratch_shapes=[pltpu.VMEM((groups * slot_count, packed_rows, LANES), bf16)],
        compiler_params=params(),
        name="pick",
    )(group, jobs, job_slot, *every)
    outgoing, column = lax.optimization_barrier((outgoing, column))
    weight = lax.all_gather(column, ("y", "grp", "core"), axis=0, tiled=True)
    arrived = lax.all_to_all(outgoing, SEQ, split_axis=0, concat_axis=0, tiled=True)
    terms, adapter = pl.pallas_call(
        tile_kernel,
        out_shape=(
            jax.ShapeDtypeStruct((shards, packed_rows, LANES), bf16),
            jax.ShapeDtypeStruct((rank, width + 2 * rows), bf16),
        ),
        in_specs=[whole()] * 3,
        out_specs=(whole(),) * 2,
        scratch_shapes=[pltpu.VMEM((rank, width), f32)],
        compiler_params=params(),
        name="tile",
    )(arrived, tokens, cotangent)
    incoming = lax.all_to_all(terms, SEQ, split_axis=0, concat_axis=0, tiled=True)
    sums = pl.pallas_call(
        sum_kernel,
        out_shape=(jax.ShapeDtypeStruct((slot_count, packed_rows, LANES), f32),)
        + (jax.ShapeDtypeStruct((slot_count, packed_rows, LANES), bf16),) * (groups - 1),
        in_specs=[smem, smem, smem, whole()],
        out_specs=(whole(),) * groups,
        scratch_shapes=[pltpu.VMEM((groups * slot_count, packed_rows, LANES), f32)],
        compiler_params=params(),
        name="sum",
    )(group, jobs, job_slot, incoming)
    last, weight = lax.optimization_barrier((sums[-1], weight))
    sums = tuple(sums[:-1]) + (last,)
    owned = (sums[0],) + tuple(shift(sums[k], k, groups) for k in range(1, groups))
    grads = pl.pallas_call(
        unpack_kernel,
        out_shape=jax.ShapeDtypeStruct((slot_count, rank, row_count), f32),
        in_specs=[whole()] * groups,
        out_specs=whole(),
        compiler_params=params(),
        name="unpack",
    )(*owned)

    wide, halves = lax.axis_size("y"), 2
    block = depth // (wide * halves)
    weight = weight.reshape(wide, shards // (wide * deep) * groups, deep, quarter, key_columns)
    keys, token_gradient = pl.pallas_call(
        base_kernel,
        grid=(wide * halves,),
        out_shape=(
            jax.ShapeDtypeStruct((rows, key_columns), bf16),
            jax.ShapeDtypeStruct((rows, depth), bf16),
        ),
        in_specs=[
            pl.BlockSpec((rows, block), lambda i: (0, i)),
            pl.BlockSpec((rows, key_columns), lambda i: (0, 0)),
            pl.BlockSpec(
                (1, weight.shape[1], deep // halves, quarter, key_columns),
                lambda i: (i // halves, 0, i % halves, 0, 0),
            ),
            pl.BlockSpec((rank, block), lambda i: (0, i)),
            pl.BlockSpec((rank, key_columns), lambda i: (0, depth // key_columns)),
            pl.BlockSpec((rank, rows), lambda i: (0, width // rows)),
            pl.BlockSpec((rank, rows), lambda i: (0, width // rows + 1)),
        ],
        out_specs=(
            pl.BlockSpec((rows, key_columns), lambda i: (0, 0)),
            pl.BlockSpec((rows, block), lambda i: (0, i)),
        ),
        scratch_shapes=[pltpu.VMEM((rows, key_columns), f32)],
        compiler_params=params(56),
        cost_estimate=pl.CostEstimate(
            flops=4 * rows * depth * key_columns,
            bytes_accessed=2 * depth * key_columns + 4 * rows * width,
            transcendentals=0,
        ),
        name="base",
    )(tokens, cotangent, weight, adapter, adapter, adapter, adapter)
    return keys, token_gradient, jnp.swapaxes(grads, 1, 2)


def solution(mesh):
    groups, shards = mesh.devices.shape
    cores = 2
    deep = 8
    mesh = Mesh(
        mesh.devices.reshape(groups, shards // (cores * deep), deep, cores),
        ("grp", "y", "z", "core"),
    )
    every = ("grp",) + SEQ
    placed = (
        P(every, None),
        P(every, None),
        P(SEQ, None),
        P("grp", SEQ, None),
        P(),
        P(),
    )
    return jax.shard_map(
        on_device,
        mesh=mesh,
        in_specs=placed,
        out_specs=(P(every, None), P(every, None), P("grp", SEQ, None)),
        check_vma=False,
    )
```

```python
import jax
import jax.numpy as jnp
from jax import lax
from jax.experimental import pallas as pl
from jax.experimental.pallas import tpu as pltpu
from jax.sharding import Mesh
from jax.sharding import PartitionSpec as P

SEQ = ("y", "z", "core")
TILE_ROWS = 128
LANES = 128
adapter_scale = 0.5
f32 = jnp.float32
bf16 = jnp.bfloat16
NT = (((1,), (1,)), ((), ()))
TN = (((0,), (0,)), ((), ()))


def params(vmem_mib=32):
    return pltpu.CompilerParams(vmem_limit_bytes=vmem_mib * 1024 * 1024)


def pack_kernel(a_ref, o_ref):
    slots, rank, width = a_ref.shape
    tail = width - LANES
    for s in range(slots):
        o_ref[s, :rank, :] = a_ref[s, :, :LANES]
        rest = a_ref[s, :, LANES:].astype(f32)
        pieces = [rest[8 * b : 8 * b + 8, :] for b in range(LANES // tail)]
        o_ref[s, rank:, :] = jnp.concatenate(pieces, axis=1).astype(o_ref.dtype)


def pick_kernel(group_ref, job_ref, slot_ref, *refs):
    sources, (o_ref, every_ref) = refs[:-2], refs[-2:]
    tiles = o_ref.shape[0]
    count = sources[0].shape[0]
    me = group_ref[0]
    for k, source in enumerate(sources):
        every_ref[pl.ds(lax.rem(me + k, len(sources)) * count, count)] = source[...]

    def step(t, carry):
        o_ref[t] = every_ref[slot_ref[job_ref[me * tiles + t]]]
        return carry

    lax.fori_loop(0, tiles, step, 0, unroll=4)


def sum_kernel(group_ref, job_ref, slot_ref, x_ref, *refs):
    sinks, sum_ref = refs[:-1], refs[-1]
    tiles = x_ref.shape[0]
    count = sinks[0].shape[0]
    me = group_ref[0]
    sum_ref[...] = jnp.zeros_like(sum_ref)

    def step(t, carry):
        s = slot_ref[job_ref[me * tiles + t]]
        sum_ref[s] = sum_ref[s] + x_ref[t].astype(f32)
        return carry

    lax.fori_loop(0, tiles, step, 0, unroll=4)
    for k, sink in enumerate(sinks):
        sink[...] = sum_ref[pl.ds(lax.rem(me + k, len(sinks)) * count, count)].astype(sink.dtype)


def unpack_kernel(x0_ref, x1_ref, x2_ref, x3_ref, o_ref):
    slots, rank, width = o_ref.shape
    tail = width - LANES
    for s in range(slots):
        total = x0_ref[s] + (x1_ref[s].astype(f32) + x2_ref[s].astype(f32)) + x3_ref[s].astype(f32)
        o_ref[s, :, :LANES] = total[:rank]
        rest = total[rank:]
        for b in range(LANES // tail):
            o_ref[s, 8 * b : 8 * b + 8, LANES:] = rest[:, tail * b : tail * (b + 1)]


def tile_kernel(x_ref, tok_ref, cot_ref, terms_ref, at_ref, t_ref):
    shards, _, _ = x_ref.shape
    rank = at_ref.shape[0]
    depth = tok_ref.shape[1]
    width = depth + cot_ref.shape[1]
    tail = width // shards - LANES
    per = LANES // tail
    group = per * (LANES + tail)
    lane = lax.broadcasted_iota(jnp.int32, (rank, LANES), 1)
    lane8 = lax.broadcasted_iota(jnp.int32, (8, LANES), 1)

    def unpack(a, carry):
        before = None
        for j in range(per + 1):
            if j < per:
                block = x_ref[a * per + j].astype(f32)
                main = block[:rank]
                now = main if j == 0 else pltpu.roll(main, tail * j, axis=1)
            else:
                now = None
            if before is None:
                out = now
            else:
                out = jnp.where(lane >= tail * (j - 1), rest, before)
                if now is not None:
                    out = jnp.where(lane >= tail * j, now, out)
            start = pl.multiple_of(a * group + LANES * j, LANES)
            at_ref[:, pl.ds(start, LANES)] = out.astype(at_ref.dtype)
            before = now
            if j < per:
                packed = block[rank:]
                rest = jnp.concatenate(
                    [
                        packed if b == j else pltpu.roll(packed, tail * ((j - b) % per), axis=1)
                        for b in range(per)
                    ],
                    axis=0,
                )
        return carry

    lax.fori_loop(0, shards // per, unpack, 0)

    tok = tok_ref[...]
    cot = cot_ref[...]
    hidden = lax.dot_general(
        at_ref[:, :depth], tok, NT, preferred_element_type=f32
    ).astype(bf16)
    back = lax.dot_general(
        at_ref[:, depth:width], cot, NT, preferred_element_type=f32
    ).astype(bf16)
    at_ref[:, width : width + LANES] = hidden
    at_ref[:, width + LANES :] = back
    t_ref[:, :depth] = adapter_scale * jnp.dot(back, tok, preferred_element_type=f32)
    t_ref[:, depth:] = adapter_scale * jnp.dot(hidden, cot, preferred_element_type=f32)

    def pack(a, carry):
        cols = [
            t_ref[:, pl.ds(pl.multiple_of(a * group + LANES * j, LANES), LANES)]
            for j in range(per + 1)
        ]
        for j in range(per):
            main = jnp.where(lane >= tail * j, cols[j], cols[j + 1])
            if j:
                main = pltpu.roll(main, LANES - tail * j, axis=1)
            packed = jnp.zeros((8, LANES), f32)
            for b in range(per):
                piece = cols[j + 1][8 * b : 8 * b + 8]
                if b != j:
                    piece = pltpu.roll(piece, tail * ((b - j) % per), axis=1)
                packed = jnp.where(lane8 // tail == b, piece, packed)
            terms_ref[a * per + j] = jnp.concatenate([main, packed], axis=0).astype(
                terms_ref.dtype
            )
        return carry

    lax.fori_loop(0, shards // per, pack, 0)


def columns(y, z, parity, deep):
    start = ((y * deep + z) * 2 + parity) * TILE_ROWS
    return pl.ds(pl.multiple_of(start, TILE_ROWS), TILE_ROWS)


def products(tok_ref, cot_ref, weight, adapter_ref, back, places):
    tok = jnp.concatenate([tok_ref[:, at] for at in places], axis=1)
    down = jnp.concatenate([adapter_ref[:, at] for at in places], axis=1)
    key = jnp.dot(tok, weight, preferred_element_type=f32)
    grad = lax.dot_general(cot_ref[...], weight, NT, preferred_element_type=f32)
    grad += adapter_scale * lax.dot_general(back, down, TN, preferred_element_type=f32)
    return key, grad.astype(bf16)


def fetch(place_ref, core, sources, w_ref, sems):
    wide, groups = w_ref.shape[:2]
    for a, source in enumerate(sources):
        for b in range(source.shape[0]):
            back_y = jnp.where(core == 0, b, a)
            back_g = jnp.where(core == 0, a, b)
            y = lax.rem(place_ref[1] - back_y + wide, wide)
            g = lax.rem(place_ref[0] - back_g + groups, groups)
            pltpu.make_async_copy(source.at[b], w_ref.at[y, g], sems.at[y, g]).start()


def block(source, w_ref, sems, y):
    groups, deep = w_ref.shape[1:3]
    for g in range(groups):
        pltpu.make_async_copy(source.at[0], w_ref.at[y, g], sems.at[y, g]).wait()
    return jnp.concatenate([w_ref[y, g, z] for z in range(deep) for g in range(groups)], axis=0)


def own_kernel(place_ref, tok_ref, cot_ref, s0, s1, s2, s3, adapter_ref, key_ref, grad_ref, w_ref, sems):
    wide, _, deep, _, key_columns = w_ref.shape
    rows, depth = tok_ref.shape
    width = depth + key_columns
    span = deep * TILE_ROWS
    core = place_ref[2]
    fetch(place_ref, core, (s0, s1, s2, s3), w_ref, sems)
    hidden = adapter_ref[:, width : width + rows]
    back = adapter_ref[:, width + rows :]
    up = adapter_ref[:, depth:width]
    key_ref[...] = adapter_scale * lax.dot_general(hidden, up, TN, preferred_element_type=f32)
    for y in range(wide):
        weight = block(s0, w_ref, sems, y)
        places = [columns(y, z, core, deep) for z in range(deep)]
        key, grad = products(tok_ref, cot_ref, weight, adapter_ref, back, places)
        key_ref[...] += key
        grad_ref[:, y * span : (y + 1) * span] = grad


def other_kernel(
    place_ref, tok_ref, cot_ref, s0, s1, s2, s3, adapter_ref, key_ref, own_ref, keys_ref, grad_ref, acc_ref, w_ref, sems
):
    wide, _, deep, _, key_columns = w_ref.shape
    rows, depth = tok_ref.shape
    core = place_ref[2]
    fetch(place_ref, 1 - core, (s0, s1, s2, s3), w_ref, sems)
    back = adapter_ref[:, depth + key_columns + rows :]
    acc_ref[...] = key_ref[...]
    for y in range(wide):
        weight = block(s0, w_ref, sems, y)
        places = [columns(y, z, 1 - core, deep) for z in range(deep)]
        key, grad = products(tok_ref, cot_ref, weight, adapter_ref, back, places)
        acc_ref[...] += key
        for z in range(deep):
            at = (y * deep + z) * TILE_ROWS
            grad_ref[:, columns(y, z, core, deep)] = own_ref[:, at : at + TILE_ROWS]
            grad_ref[:, places[z]] = grad[:, z * TILE_ROWS : (z + 1) * TILE_ROWS]
    keys_ref[...] = acc_ref[...].astype(keys_ref.dtype)


def shift(x, by, groups):
    return lax.ppermute(x, "grp", [(i, (i + by) % groups) for i in range(groups)])


def route(x, by, groups, wide, first):
    pairs = []
    for g in range(groups):
        for y in range(wide):
            for c in range(2):
                along_y = (c == 0) == first
                to = (g, (y + by) % wide) if along_y else ((g + by) % groups, y)
                pairs.append(((g * wide + y) * 2 + c, (to[0] * wide + to[1]) * 2 + c))
    return lax.ppermute(x, ("grp", "y", "core"), pairs)


def whole(memory=pltpu.VMEM):
    return pl.BlockSpec(memory_space=memory)


def on_device(tokens, cotangent, frozen_weight, adapters, tile_job, job_slot):
    rows, depth = tokens.shape
    key_columns = cotangent.shape[1]
    slot_count, row_count, rank = adapters.shape
    groups = lax.axis_size("grp")
    shards = lax.axis_size(SEQ)
    packed_rows = row_count * rank // LANES
    width = depth + key_columns
    group = lax.axis_index("grp").reshape(1).astype(jnp.int32)
    place = jnp.stack([lax.axis_index("grp"), lax.axis_index("y"), lax.axis_index("core")])
    place = place.astype(jnp.int32)
    jobs = tile_job.reshape(-1)

    quarter = TILE_ROWS // groups
    wide, deep = lax.axis_size("y"), lax.axis_size("z")
    mine = lax.dynamic_slice_in_dim(frozen_weight, lax.axis_index("grp") * quarter, quarter, 0)
    column = lax.all_to_all(
        jnp.broadcast_to(mine, (deep,) + mine.shape), "z", split_axis=0, concat_axis=0, tiled=True
    )
    line = jnp.stack([column] + [route(column, k, groups, wide, True) for k in range(1, wide)])
    halves = [line] + [route(line, k, groups, wide, False) for k in range(1, groups)]
    others = [lax.ppermute(x, "core", [(0, 1), (1, 0)]) for x in halves]

    own = pl.pallas_call(
        pack_kernel,
        out_shape=jax.ShapeDtypeStruct((slot_count, packed_rows, LANES), bf16),
        in_specs=[whole()],
        out_specs=whole(),
        compiler_params=params(),
        name="pack",
    )(jnp.swapaxes(adapters, 1, 2))
    every = (own,) + tuple(shift(own, -k, groups) for k in range(1, groups))
    smem = whole(pltpu.SMEM)
    outgoing = pl.pallas_call(
        pick_kernel,
        out_shape=jax.ShapeDtypeStruct((shards, packed_rows, LANES), bf16),
        in_specs=[smem, smem, smem] + [whole()] * groups,
        out_specs=whole(),
        scratch_shapes=[pltpu.VMEM((groups * slot_count, packed_rows, LANES), bf16)],
        compiler_params=params(),
        name="pick",
    )(group, jobs, job_slot, *every)
    arrived = lax.all_to_all(outgoing, SEQ, split_axis=0, concat_axis=0, tiled=True)
    terms, adapter = pl.pallas_call(
        tile_kernel,
        out_shape=(
            jax.ShapeDtypeStruct((shards, packed_rows, LANES), bf16),
            jax.ShapeDtypeStruct((rank, width + 2 * rows), bf16),
        ),
        in_specs=[whole()] * 3,
        out_specs=(whole(),) * 2,
        scratch_shapes=[pltpu.VMEM((rank, width), f32)],
        compiler_params=params(),
        name="tile",
    )(arrived, tokens, cotangent)
    incoming = lax.all_to_all(terms, SEQ, split_axis=0, concat_axis=0, tiled=True)
    incoming, others = lax.optimization_barrier((incoming, others))
    sums = pl.pallas_call(
        sum_kernel,
        out_shape=(jax.ShapeDtypeStruct((slot_count, packed_rows, LANES), f32),)
        + (jax.ShapeDtypeStruct((slot_count, packed_rows, LANES), bf16),) * (groups - 1),
        in_specs=[smem, smem, smem, whole()],
        out_specs=(whole(),) * groups,
        scratch_shapes=[pltpu.VMEM((groups * slot_count, packed_rows, LANES), f32)],
        compiler_params=params(),
        name="sum",
    )(group, jobs, job_slot, incoming)
    kept, line = lax.optimization_barrier((sums[0], line))
    sums = (kept,) + tuple(sums[1:])
    blocks = (wide, groups, deep, quarter, key_columns)
    cost = pl.CostEstimate(
        flops=2 * rows * depth * key_columns,
        bytes_accessed=depth * key_columns + 4 * rows * width,
        transcendentals=0,
    )
    key_part, own_part = pl.pallas_call(
        own_kernel,
        out_shape=(
            jax.ShapeDtypeStruct((rows, key_columns), f32),
            jax.ShapeDtypeStruct((rows, depth // 2), bf16),
        ),
        in_specs=[smem, whole(), whole()] + [whole(pltpu.HBM)] * groups + [whole()],
        out_specs=(whole(),) * 2,
        scratch_shapes=[pltpu.VMEM(blocks, bf16), pltpu.SemaphoreType.DMA((wide, groups))],
        compiler_params=params(50),
        cost_estimate=cost,
        name="own",
    )(place, tokens, cotangent, line, *halves[1:], adapter)
    owned = (sums[0],) + tuple(shift(sums[k], k, groups) for k in range(1, groups))
    grads = pl.pallas_call(
        unpack_kernel,
        out_shape=jax.ShapeDtypeStruct((slot_count, rank, row_count), f32),
        in_specs=[whole()] * groups,
        out_specs=whole(),
        compiler_params=params(),
        name="unpack",
    )(*owned)

    keys, token_gradient = pl.pallas_call(
        other_kernel,
        out_shape=(
            jax.ShapeDtypeStruct((rows, key_columns), bf16),
            jax.ShapeDtypeStruct((rows, depth), bf16),
        ),
        in_specs=[smem, whole(), whole()] + [whole(pltpu.HBM)] * groups + [whole()] * 3,
        out_specs=(whole(),) * 2,
        scratch_shapes=[
            pltpu.VMEM((rows, key_columns), f32),
            pltpu.VMEM(blocks, bf16),
            pltpu.SemaphoreType.DMA((wide, groups)),
        ],
        compiler_params=params(50),
        cost_estimate=cost,
        name="other",
    )(place, tokens, cotangent, *others, adapter, key_part, own_part)
    return keys, token_gradient, jnp.swapaxes(grads, 1, 2)


def solution(mesh):
    groups, shards = mesh.devices.shape
    cores = 2
    deep = 8
    mesh = Mesh(
        mesh.devices.reshape(groups, shards // (cores * deep), deep, cores),
        ("grp", "y", "z", "core"),
    )
    every = ("grp",) + SEQ
    placed = (
        P(every, None),
        P(every, None),
        P(SEQ, None),
        P("grp", SEQ, None),
        P(),
        P(),
    )
    return jax.shard_map(
        on_device,
        mesh=mesh,
        in_specs=placed,
        out_specs=(P(every, None), P(every, None), P("grp", SEQ, None)),
        check_vma=False,
    )
```

```python
import jax
import jax.numpy as jnp
from jax import lax
from jax.experimental import pallas as pl
from jax.experimental.pallas import tpu as pltpu
from jax.sharding import Mesh
from jax.sharding import PartitionSpec as P

SEQ = ("y", "z", "core")
TILE_ROWS = 128
LANES = 128
adapter_scale = 0.5
f32 = jnp.float32
bf16 = jnp.bfloat16
NT = (((1,), (1,)), ((), ()))
TN = (((0,), (0,)), ((), ()))


def params(vmem_mib=32):
    return pltpu.CompilerParams(vmem_limit_bytes=vmem_mib * 1024 * 1024)


def pack_kernel(a_ref, o_ref):
    slots, rank, width = a_ref.shape
    tail = width - LANES
    for s in range(slots):
        o_ref[s, :rank, :] = a_ref[s, :, :LANES]
        rest = a_ref[s, :, LANES:].astype(f32)
        pieces = [rest[8 * b : 8 * b + 8, :] for b in range(LANES // tail)]
        o_ref[s, rank:, :] = jnp.concatenate(pieces, axis=1).astype(o_ref.dtype)


def pick_kernel(group_ref, job_ref, slot_ref, *refs):
    sources, (o_ref, every_ref) = refs[:-2], refs[-2:]
    tiles = o_ref.shape[0]
    count = sources[0].shape[0]
    me = group_ref[0]
    for k, source in enumerate(sources):
        every_ref[pl.ds(lax.rem(me + k, len(sources)) * count, count)] = source[...]

    def step(t, carry):
        o_ref[t] = every_ref[slot_ref[job_ref[me * tiles + t]]]
        return carry

    lax.fori_loop(0, tiles, step, 0, unroll=4)


def sum_kernel(group_ref, job_ref, slot_ref, x_ref, *refs):
    sinks, sum_ref = refs[:-1], refs[-1]
    tiles = x_ref.shape[0]
    count = sinks[0].shape[0]
    me = group_ref[0]
    sum_ref[...] = jnp.zeros_like(sum_ref)

    def step(t, carry):
        s = slot_ref[job_ref[me * tiles + t]]
        sum_ref[s] = sum_ref[s] + x_ref[t].astype(f32)
        return carry

    lax.fori_loop(0, tiles, step, 0, unroll=4)
    for k, sink in enumerate(sinks):
        sink[...] = sum_ref[pl.ds(lax.rem(me + k, len(sinks)) * count, count)].astype(sink.dtype)


def unpack_kernel(x0_ref, x1_ref, x2_ref, x3_ref, o_ref):
    slots, rank, width = o_ref.shape
    tail = width - LANES
    for s in range(slots):
        total = x0_ref[s] + (x1_ref[s].astype(f32) + x2_ref[s].astype(f32)) + x3_ref[s].astype(f32)
        o_ref[s, :, :LANES] = total[:rank]
        rest = total[rank:]
        for b in range(LANES // tail):
            o_ref[s, 8 * b : 8 * b + 8, LANES:] = rest[:, tail * b : tail * (b + 1)]


def tile_kernel(x_ref, tok_ref, cot_ref, terms_ref, at_ref, t_ref):
    shards, _, _ = x_ref.shape
    rank = at_ref.shape[0]
    depth = tok_ref.shape[1]
    width = depth + cot_ref.shape[1]
    tail = width // shards - LANES
    per = LANES // tail
    group = per * (LANES + tail)
    lane = lax.broadcasted_iota(jnp.int32, (rank, LANES), 1)
    lane8 = lax.broadcasted_iota(jnp.int32, (8, LANES), 1)

    def unpack(a, carry):
        before = None
        for j in range(per + 1):
            if j < per:
                block = x_ref[a * per + j].astype(f32)
                main = block[:rank]
                now = main if j == 0 else pltpu.roll(main, tail * j, axis=1)
            else:
                now = None
            if before is None:
                out = now
            else:
                out = jnp.where(lane >= tail * (j - 1), rest, before)
                if now is not None:
                    out = jnp.where(lane >= tail * j, now, out)
            start = pl.multiple_of(a * group + LANES * j, LANES)
            at_ref[:, pl.ds(start, LANES)] = out.astype(at_ref.dtype)
            before = now
            if j < per:
                packed = block[rank:]
                rest = jnp.concatenate(
                    [
                        packed if b == j else pltpu.roll(packed, tail * ((j - b) % per), axis=1)
                        for b in range(per)
                    ],
                    axis=0,
                )
        return carry

    lax.fori_loop(0, shards // per, unpack, 0)

    tok = tok_ref[...]
    cot = cot_ref[...]
    hidden = lax.dot_general(
        at_ref[:, :depth], tok, NT, preferred_element_type=f32
    ).astype(bf16)
    back = lax.dot_general(
        at_ref[:, depth:width], cot, NT, preferred_element_type=f32
    ).astype(bf16)
    at_ref[:, width : width + LANES] = hidden
    at_ref[:, width + LANES :] = back
    t_ref[:, :depth] = adapter_scale * jnp.dot(back, tok, preferred_element_type=f32)
    t_ref[:, depth:] = adapter_scale * jnp.dot(hidden, cot, preferred_element_type=f32)

    def pack(a, carry):
        cols = [
            t_ref[:, pl.ds(pl.multiple_of(a * group + LANES * j, LANES), LANES)]
            for j in range(per + 1)
        ]
        for j in range(per):
            main = jnp.where(lane >= tail * j, cols[j], cols[j + 1])
            if j:
                main = pltpu.roll(main, LANES - tail * j, axis=1)
            packed = jnp.zeros((8, LANES), f32)
            for b in range(per):
                piece = cols[j + 1][8 * b : 8 * b + 8]
                if b != j:
                    piece = pltpu.roll(piece, tail * ((b - j) % per), axis=1)
                packed = jnp.where(lane8 // tail == b, piece, packed)
            terms_ref[a * per + j] = jnp.concatenate([main, packed], axis=0).astype(
                terms_ref.dtype
            )
        return carry

    lax.fori_loop(0, shards // per, pack, 0)


def join_kernel(x0, x1, x2, x3, o_ref, sems):
    copies = [
        pltpu.make_async_copy(x, o_ref.at[k], sems.at[k]) for k, x in enumerate((x0, x1, x2, x3))
    ]
    for copy in copies:
        copy.start()
    for copy in copies:
        copy.wait()


def fetch(place_ref, core, sources, w_ref, sems):
    wide, _, groups = w_ref.shape[:3]
    for a, source in enumerate(sources):
        for b in range(source.shape[0]):
            back_y = jnp.where(core == 0, b, a)
            back_g = jnp.where(core == 0, a, b)
            y = lax.rem(place_ref[1] - back_y + wide, wide)
            g = lax.rem(place_ref[0] - back_g + groups, groups)
            pltpu.make_async_copy(source.at[b], w_ref.at[y, core, g], sems.at[y, core, g]).start()


def base_kernel(
    place_ref, tok_ref, cot_ref, s0, s1, s2, s3, t0, t1, t2, t3, adapter_ref, keys_ref, out_ref,
    w_ref, grad_ref, acc_ref, sems, out_sems,
):
    wide, cores, groups, deep, _, key_columns = w_ref.shape
    rows, depth = tok_ref.shape
    width = depth + key_columns
    core = place_ref[2]
    fetch(place_ref, core, (s0, s1, s2, s3), w_ref, sems)
    fetch(place_ref, 1 - core, (t0, t1, t2, t3), w_ref, sems)
    hidden = adapter_ref[:, width : width + rows]
    back = adapter_ref[:, width + rows :]
    up = adapter_ref[:, depth:width]
    acc_ref[...] = adapter_scale * lax.dot_general(hidden, up, TN, preferred_element_type=f32)
    halves = 2
    span = depth // (wide * halves)
    stores = []
    for y in range(wide):
        for c in range(cores):
            for g in range(groups):
                pltpu.make_async_copy(s0.at[0], w_ref.at[y, c, g], sems.at[y, c, g]).wait()
        for h in range(halves):
            at = slice((y * halves + h) * span, (y * halves + h + 1) * span)
            weight = jnp.concatenate(
                [
                    w_ref[y, c, g, z]
                    for z in range(h * deep // halves, (h + 1) * deep // halves)
                    for c in range(cores)
                    for g in range(groups)
                ],
                axis=0,
            )
            acc_ref[...] += jnp.dot(tok_ref[:, at], weight, preferred_element_type=f32)
            grad = lax.dot_general(cot_ref[...], weight, NT, preferred_element_type=f32)
            grad += adapter_scale * lax.dot_general(
                back, adapter_ref[:, at], TN, preferred_element_type=f32
            )
            grad_ref[:, at] = grad.astype(grad_ref.dtype)
            stores.append(
                pltpu.make_async_copy(
                    grad_ref.at[:, at], out_ref.at[:, at], out_sems.at[y * halves + h]
                )
            )
            stores[-1].start()
    keys_ref[...] = acc_ref[...].astype(keys_ref.dtype)
    for store in stores:
        store.wait()


def shift(x, by, groups):
    return lax.ppermute(x, "grp", [(i, (i + by) % groups) for i in range(groups)])


def route(x, by, groups, wide, first):
    pairs = []
    for g in range(groups):
        for y in range(wide):
            for c in range(2):
                along_y = (c == 0) == first
                to = (g, (y + by) % wide) if along_y else ((g + by) % groups, y)
                pairs.append(((g * wide + y) * 2 + c, (to[0] * wide + to[1]) * 2 + c))
    return lax.ppermute(x, ("grp", "y", "core"), pairs)


def whole(memory=pltpu.VMEM):
    return pl.BlockSpec(memory_space=memory)


def on_device(tokens, cotangent, frozen_weight, adapters, tile_job, job_slot):
    rows, depth = tokens.shape
    key_columns = cotangent.shape[1]
    slot_count, row_count, rank = adapters.shape
    groups = lax.axis_size("grp")
    shards = lax.axis_size(SEQ)
    packed_rows = row_count * rank // LANES
    width = depth + key_columns
    group = lax.axis_index("grp").reshape(1).astype(jnp.int32)
    place = jnp.stack([lax.axis_index("grp"), lax.axis_index("y"), lax.axis_index("core")])
    place = place.astype(jnp.int32)
    jobs = tile_job.reshape(-1)

    quarter = TILE_ROWS // groups
    wide, deep = lax.axis_size("y"), lax.axis_size("z")
    mine = lax.dynamic_slice_in_dim(frozen_weight, lax.axis_index("grp") * quarter, quarter, 0)
    column = lax.all_to_all(
        jnp.broadcast_to(mine, (deep,) + mine.shape), "z", split_axis=0, concat_axis=0, tiled=True
    )
    line = pl.pallas_call(
        join_kernel,
        out_shape=jax.ShapeDtypeStruct((wide,) + column.shape, bf16),
        in_specs=[whole(pl.ANY)] * wide,
        out_specs=whole(pl.ANY),
        scratch_shapes=[pltpu.SemaphoreType.DMA((wide,))],
        compiler_params=params(),
        name="join",
    )(column, *[route(column, k, groups, wide, True) for k in range(1, wide)])
    halves = [line] + [route(line, k, groups, wide, False) for k in range(1, groups)]
    others = [lax.ppermute(x, "core", [(0, 1), (1, 0)]) for x in halves]

    own = pl.pallas_call(
        pack_kernel,
        out_shape=jax.ShapeDtypeStruct((slot_count, packed_rows, LANES), bf16),
        in_specs=[whole()],
        out_specs=whole(),
        compiler_params=params(),
        name="pack",
    )(jnp.swapaxes(adapters, 1, 2))
    every = (own,) + tuple(shift(own, -k, groups) for k in range(1, groups))
    smem = whole(pltpu.SMEM)
    outgoing = pl.pallas_call(
        pick_kernel,
        out_shape=jax.ShapeDtypeStruct((shards, packed_rows, LANES), bf16),
        in_specs=[smem, smem, smem] + [whole()] * groups,
        out_specs=whole(),
        scratch_shapes=[pltpu.VMEM((groups * slot_count, packed_rows, LANES), bf16)],
        compiler_params=params(),
        name="pick",
    )(group, jobs, job_slot, *every)
    arrived = lax.all_to_all(outgoing, SEQ, split_axis=0, concat_axis=0, tiled=True)
    terms, adapter = pl.pallas_call(
        tile_kernel,
        out_shape=(
            jax.ShapeDtypeStruct((shards, packed_rows, LANES), bf16),
            jax.ShapeDtypeStruct((rank, width + 2 * rows), bf16),
        ),
        in_specs=[whole()] * 3,
        out_specs=(whole(),) * 2,
        scratch_shapes=[pltpu.VMEM((rank, width), f32)],
        compiler_params=params(),
        name="tile",
    )(arrived, tokens, cotangent)
    incoming = lax.all_to_all(terms, SEQ, split_axis=0, concat_axis=0, tiled=True)
    incoming, others[0] = lax.optimization_barrier((incoming, others[0]))
    sums = pl.pallas_call(
        sum_kernel,
        out_shape=(jax.ShapeDtypeStruct((slot_count, packed_rows, LANES), f32),)
        + (jax.ShapeDtypeStruct((slot_count, packed_rows, LANES), bf16),) * (groups - 1),
        in_specs=[smem, smem, smem, whole()],
        out_specs=(whole(),) * groups,
        scratch_shapes=[pltpu.VMEM((groups * slot_count, packed_rows, LANES), f32)],
        compiler_params=params(),
        name="sum",
    )(group, jobs, job_slot, incoming)
    kept, halves[0] = lax.optimization_barrier((sums[0], halves[0]))
    last, others = lax.optimization_barrier((sums[-1], others))
    sums = (kept,) + tuple(sums[1:-1]) + (last,)
    owned = (sums[0],) + tuple(shift(sums[k], k, groups) for k in range(1, groups))
    grads = pl.pallas_call(
        unpack_kernel,
        out_shape=jax.ShapeDtypeStruct((slot_count, rank, row_count), f32),
        in_specs=[whole()] * groups,
        out_specs=whole(),
        compiler_params=params(),
        name="unpack",
    )(*owned)

    blocks = (wide, 2, groups, deep, quarter, key_columns)
    keys, token_gradient = pl.pallas_call(
        base_kernel,
        out_shape=(
            jax.ShapeDtypeStruct((rows, key_columns), bf16),
            jax.ShapeDtypeStruct((rows, depth), bf16),
        ),
        in_specs=[smem, whole(), whole()] + [whole(pltpu.HBM)] * (2 * groups) + [whole()],
        out_specs=(whole(), whole(pltpu.HBM)),
        scratch_shapes=[
            pltpu.VMEM(blocks, bf16),
            pltpu.VMEM((rows, depth), bf16),
            pltpu.VMEM((rows, key_columns), f32),
            pltpu.SemaphoreType.DMA(blocks[:3]),
            pltpu.SemaphoreType.DMA((2 * wide,)),
        ],
        compiler_params=params(50),
        cost_estimate=pl.CostEstimate(
            flops=4 * rows * depth * key_columns,
            bytes_accessed=2 * depth * key_columns + 4 * rows * width,
            transcendentals=0,
        ),
        name="base",
    )(place, tokens, cotangent, *halves, *others, adapter)
    return keys, token_gradient, jnp.swapaxes(grads, 1, 2)


def solution(mesh):
    groups, shards = mesh.devices.shape
    cores = 2
    deep = 8
    mesh = Mesh(
        mesh.devices.reshape(groups, shards // (cores * deep), deep, cores),
        ("grp", "y", "z", "core"),
    )
    every = ("grp",) + SEQ
    placed = (
        P(every, None),
        P(every, None),
        P(SEQ, None),
        P("grp", SEQ, None),
        P(),
        P(),
    )
    return jax.shard_map(
        on_device,
        mesh=mesh,
        in_specs=placed,
        out_specs=(P(every, None), P(every, None), P("grp", SEQ, None)),
        check_vma=False,
    )
```

```python
import jax
import jax.numpy as jnp
from jax import lax
from jax.experimental import pallas as pl
from jax.experimental.pallas import tpu as pltpu
from jax.sharding import Mesh
from jax.sharding import PartitionSpec as P

SEQ = ("y", "z", "core")
TILE_ROWS = 128
LANES = 128
adapter_scale = 0.5
f32 = jnp.float32
bf16 = jnp.bfloat16
NT = (((1,), (1,)), ((), ()))
TN = (((0,), (0,)), ((), ()))


def params(vmem_mib=32):
    return pltpu.CompilerParams(vmem_limit_bytes=vmem_mib * 1024 * 1024)


def pack_kernel(a_ref, o_ref):
    slots, rank, width = a_ref.shape
    tail = width - LANES
    for s in range(slots):
        o_ref[s, :rank, :] = a_ref[s, :, :LANES]
        rest = a_ref[s, :, LANES:].astype(f32)
        pieces = [rest[8 * b : 8 * b + 8, :] for b in range(LANES // tail)]
        o_ref[s, rank:, :] = jnp.concatenate(pieces, axis=1).astype(o_ref.dtype)


def pick_kernel(group_ref, job_ref, slot_ref, *refs):
    sources, (o_ref, every_ref) = refs[:-2], refs[-2:]
    tiles = o_ref.shape[0]
    count = sources[0].shape[0]
    me = group_ref[0]
    for k, source in enumerate(sources):
        every_ref[pl.ds(lax.rem(me + k, len(sources)) * count, count)] = source[...]

    def step(t, carry):
        o_ref[t] = every_ref[slot_ref[job_ref[me * tiles + t]]]
        return carry

    lax.fori_loop(0, tiles, step, 0, unroll=4)


def sum_kernel(group_ref, job_ref, slot_ref, x_ref, *refs):
    sinks, sum_ref = refs[:-1], refs[-1]
    tiles = x_ref.shape[0]
    count = sinks[0].shape[0]
    me = group_ref[0]
    sum_ref[...] = jnp.zeros_like(sum_ref)

    def step(t, carry):
        s = slot_ref[job_ref[me * tiles + t]]
        sum_ref[s] = sum_ref[s] + x_ref[t].astype(f32)
        return carry

    lax.fori_loop(0, tiles, step, 0, unroll=4)
    for k, sink in enumerate(sinks):
        sink[...] = sum_ref[pl.ds(lax.rem(me + k, len(sinks)) * count, count)].astype(sink.dtype)


def unpack_kernel(x0_ref, x1_ref, x2_ref, x3_ref, o_ref):
    slots, rank, width = o_ref.shape
    tail = width - LANES
    for s in range(slots):
        total = x0_ref[s] + (x1_ref[s].astype(f32) + x2_ref[s].astype(f32)) + x3_ref[s].astype(f32)
        o_ref[s, :, :LANES] = total[:rank]
        rest = total[rank:]
        for b in range(LANES // tail):
            o_ref[s, 8 * b : 8 * b + 8, LANES:] = rest[:, tail * b : tail * (b + 1)]


def tile_kernel(x_ref, tok_ref, cot_ref, terms_out, at_out, t_ref, terms_ref, at_ref, sems):
    shards, _, _ = x_ref.shape
    rank = at_ref.shape[0]
    depth = tok_ref.shape[1]
    width = depth + cot_ref.shape[1]
    tail = width // shards - LANES
    per = LANES // tail
    group = per * (LANES + tail)
    lane = lax.broadcasted_iota(jnp.int32, (rank, LANES), 1)
    lane8 = lax.broadcasted_iota(jnp.int32, (8, LANES), 1)

    def unpack(a, carry):
        before = None
        for j in range(per + 1):
            if j < per:
                block = x_ref[a * per + j].astype(f32)
                main = block[:rank]
                now = main if j == 0 else pltpu.roll(main, tail * j, axis=1)
            else:
                now = None
            if before is None:
                out = now
            else:
                out = jnp.where(lane >= tail * (j - 1), rest, before)
                if now is not None:
                    out = jnp.where(lane >= tail * j, now, out)
            start = pl.multiple_of(a * group + LANES * j, LANES)
            at_ref[:, pl.ds(start, LANES)] = out.astype(at_ref.dtype)
            before = now
            if j < per:
                packed = block[rank:]
                rest = jnp.concatenate(
                    [
                        packed if b == j else pltpu.roll(packed, tail * ((j - b) % per), axis=1)
                        for b in range(per)
                    ],
                    axis=0,
                )
        return carry

    lax.fori_loop(0, shards // per, unpack, 0)

    tok = tok_ref[...]
    cot = cot_ref[...]
    hidden = lax.dot_general(
        at_ref[:, :depth], tok, NT, preferred_element_type=f32
    ).astype(bf16)
    back = lax.dot_general(
        at_ref[:, depth:width], cot, NT, preferred_element_type=f32
    ).astype(bf16)
    at_ref[:, width : width + LANES] = hidden
    at_ref[:, width + LANES :] = back
    at_copy = pltpu.make_async_copy(at_ref, at_out, sems.at[0])
    at_copy.start()
    t_ref[:, :depth] = adapter_scale * jnp.dot(back, tok, preferred_element_type=f32)
    t_ref[:, depth:] = adapter_scale * jnp.dot(hidden, cot, preferred_element_type=f32)

    def pack(a, carry):
        cols = [
            t_ref[:, pl.ds(pl.multiple_of(a * group + LANES * j, LANES), LANES)]
            for j in range(per + 1)
        ]
        for j in range(per):
            main = jnp.where(lane >= tail * j, cols[j], cols[j + 1])
            if j:
                main = pltpu.roll(main, LANES - tail * j, axis=1)
            packed = jnp.zeros((8, LANES), f32)
            for b in range(per):
                piece = cols[j + 1][8 * b : 8 * b + 8]
                if b != j:
                    piece = pltpu.roll(piece, tail * ((b - j) % per), axis=1)
                packed = jnp.where(lane8 // tail == b, piece, packed)
            terms_ref[a * per + j] = jnp.concatenate([main, packed], axis=0).astype(
                terms_ref.dtype
            )
        return carry

    for a in range(shards // per):
        pack(a, 0)
        piece = slice(a * per, (a + 1) * per)
        pltpu.make_async_copy(terms_ref.at[piece], terms_out.at[piece], sems.at[a + 1]).start()
    for a in range(shards // per):
        piece = slice(a * per, (a + 1) * per)
        pltpu.make_async_copy(terms_ref.at[piece], terms_out.at[piece], sems.at[a + 1]).wait()
    at_copy.wait()


def join_kernel(x0, x1, x2, x3, o_ref, sems):
    copies = [
        pltpu.make_async_copy(x, o_ref.at[k], sems.at[k]) for k, x in enumerate((x0, x1, x2, x3))
    ]
    for copy in copies:
        copy.start()
    for copy in copies:
        copy.wait()


def base_kernel(
    place_ref, tok_ref, cot_in, s0, s1, s2, s3, t0, t1, t2, t3, adapter_in, keys_ref, out_ref,
    w_ref, grad_ref, acc_ref, cot_ref, adapter_ref, sems, out_sems, in_sems,
):
    wide, cores, groups, deep, _, key_columns = w_ref.shape
    rows, depth = tok_ref.shape
    width = depth + key_columns
    core = place_ref[2]
    inputs = [
        pltpu.make_async_copy(cot_in, cot_ref, in_sems.at[0]),
        pltpu.make_async_copy(adapter_in, adapter_ref, in_sems.at[1]),
    ]
    for copy in inputs:
        copy.start()

    def fetch(source, back, c, k):
        g = lax.rem(place_ref[0] - k + groups, groups)
        pltpu.make_async_copy(source, w_ref.at[back, c, g], sems.at[back, c, g]).start()

    def fetch_all(along_y_first, along_y_second):
        for back in range(wide):
            for k in range(groups):
                fetch(along_y_first[k].at[back], back, 0, k)
                fetch(along_y_second[back].at[k], back, 1, k)

    @pl.when(core == 0)
    def _():
        fetch_all((s0, s1, s2, s3), (t0, t1, t2, t3))

    @pl.when(core == 1)
    def _():
        fetch_all((t0, t1, t2, t3), (s0, s1, s2, s3))

    for copy in inputs:
        copy.wait()
    hidden = adapter_ref[:, width : width + rows]
    back = adapter_ref[:, width + rows :]
    up = adapter_ref[:, depth:width]
    acc_ref[...] = adapter_scale * lax.dot_general(hidden, up, TN, preferred_element_type=f32)
    halves = 2
    span = depth // (wide * halves)
    stores = []
    for step in range(wide):
        y = lax.rem(place_ref[1] - step + wide, wide)
        for c in range(cores):
            for g in range(groups):
                pltpu.make_async_copy(s0.at[0], w_ref.at[step, c, g], sems.at[step, c, g]).wait()
        for h in range(halves):
            at = pl.ds(pl.multiple_of((y * halves + h) * span, span), span)
            weight = jnp.concatenate(
                [
                    w_ref[step, c, g, z]
                    for z in range(h * deep // halves, (h + 1) * deep // halves)
                    for c in range(cores)
                    for g in range(groups)
                ],
                axis=0,
            )
            acc_ref[...] += jnp.dot(tok_ref[:, at], weight, preferred_element_type=f32)
            grad = lax.dot_general(cot_ref[...], weight, NT, preferred_element_type=f32)
            grad += adapter_scale * lax.dot_general(
                back, adapter_ref[:, at], TN, preferred_element_type=f32
            )
            grad_ref[:, at] = grad.astype(grad_ref.dtype)
            store = pltpu.make_async_copy(
                grad_ref.at[:, at], out_ref.at[:, at], out_sems.at[step * halves + h]
            )
            store.start()
            stores.append(store)
    keys_ref[...] = acc_ref[...].astype(keys_ref.dtype)
    for store in stores:
        store.wait()


def shift(x, by, groups):
    return lax.ppermute(x, "grp", [(i, (i + by) % groups) for i in range(groups)])


def route(x, by, groups, wide, first):
    pairs = []
    for g in range(groups):
        for y in range(wide):
            for c in range(2):
                along_y = (c == 0) == first
                to = (g, (y + by) % wide) if along_y else ((g + by) % groups, y)
                pairs.append(((g * wide + y) * 2 + c, (to[0] * wide + to[1]) * 2 + c))
    return lax.ppermute(x, ("grp", "y", "core"), pairs)


def whole(memory=pltpu.VMEM):
    return pl.BlockSpec(memory_space=memory)


def on_device(tokens, cotangent, frozen_weight, adapters, tile_job, job_slot):
    rows, depth = tokens.shape
    key_columns = cotangent.shape[1]
    slot_count, row_count, rank = adapters.shape
    groups = lax.axis_size("grp")
    shards = lax.axis_size(SEQ)
    packed_rows = row_count * rank // LANES
    width = depth + key_columns
    group = lax.axis_index("grp").reshape(1).astype(jnp.int32)
    place = jnp.stack([lax.axis_index("grp"), lax.axis_index("y"), lax.axis_index("core")])
    place = place.astype(jnp.int32)
    jobs = tile_job.reshape(-1)

    quarter = TILE_ROWS // groups
    wide, deep = lax.axis_size("y"), lax.axis_size("z")
    mine = lax.dynamic_slice_in_dim(frozen_weight, lax.axis_index("grp") * quarter, quarter, 0)
    column = lax.all_to_all(
        jnp.broadcast_to(mine, (deep,) + mine.shape), "z", split_axis=0, concat_axis=0, tiled=True
    )
    line = pl.pallas_call(
        join_kernel,
        out_shape=jax.ShapeDtypeStruct((wide,) + column.shape, bf16),
        in_specs=[whole()] * wide,
        out_specs=whole(pltpu.HBM),
        scratch_shapes=[pltpu.SemaphoreType.DMA((wide,))],
        compiler_params=params(),
        name="join",
    )(column, *[route(column, k, groups, wide, True) for k in range(1, wide)])
    halves = [line] + [route(line, k, groups, wide, False) for k in range(1, groups)]
    others = [lax.ppermute(x, "core", [(0, 1), (1, 0)]) for x in halves]

    own = pl.pallas_call(
        pack_kernel,
        out_shape=jax.ShapeDtypeStruct((slot_count, packed_rows, LANES), bf16),
        in_specs=[whole()],
        out_specs=whole(),
        compiler_params=params(),
        name="pack",
    )(jnp.swapaxes(adapters, 1, 2))
    every = (own,) + tuple(shift(own, -k, groups) for k in range(1, groups))
    smem = whole(pltpu.SMEM)
    outgoing = pl.pallas_call(
        pick_kernel,
        out_shape=jax.ShapeDtypeStruct((shards, packed_rows, LANES), bf16),
        in_specs=[smem, smem, smem] + [whole()] * groups,
        out_specs=whole(),
        scratch_shapes=[pltpu.VMEM((groups * slot_count, packed_rows, LANES), bf16)],
        compiler_params=params(),
        name="pick",
    )(group, jobs, job_slot, *every)
    arrived = lax.all_to_all(outgoing, SEQ, split_axis=0, concat_axis=0, tiled=True)
    terms, adapter = pl.pallas_call(
        tile_kernel,
        out_shape=(
            jax.ShapeDtypeStruct((shards, packed_rows, LANES), bf16),
            jax.ShapeDtypeStruct((rank, width + 2 * rows), bf16),
        ),
        in_specs=[whole()] * 3,
        out_specs=(whole(pltpu.HBM),) * 2,
        scratch_shapes=[
            pltpu.VMEM((rank, width), f32),
            pltpu.VMEM((shards, packed_rows, LANES), bf16),
            pltpu.VMEM((rank, width + 2 * rows), bf16),
            pltpu.SemaphoreType.DMA((shards + 1,)),
        ],
        compiler_params=params(32),
        name="tile",
    )(arrived, tokens, cotangent)
    incoming = lax.all_to_all(terms, SEQ, split_axis=0, concat_axis=0, tiled=True)
    incoming, others[0] = lax.optimization_barrier((incoming, others[0]))
    sums = pl.pallas_call(
        sum_kernel,
        out_shape=(jax.ShapeDtypeStruct((slot_count, packed_rows, LANES), f32),)
        + (jax.ShapeDtypeStruct((slot_count, packed_rows, LANES), bf16),) * (groups - 1),
        in_specs=[smem, smem, smem, whole()],
        out_specs=(whole(),) * groups,
        scratch_shapes=[pltpu.VMEM((groups * slot_count, packed_rows, LANES), f32)],
        compiler_params=params(),
        name="sum",
    )(group, jobs, job_slot, incoming)
    kept, halves[0] = lax.optimization_barrier((sums[0], halves[0]))
    last, others = lax.optimization_barrier((sums[-1], others))
    sums = (kept,) + tuple(sums[1:-1]) + (last,)
    owned = (sums[0],) + tuple(shift(sums[k], k, groups) for k in range(1, groups))
    grads = pl.pallas_call(
        unpack_kernel,
        out_shape=jax.ShapeDtypeStruct((slot_count, rank, row_count), f32),
        in_specs=[whole()] * groups,
        out_specs=whole(),
        compiler_params=params(),
        name="unpack",
    )(*owned)

    blocks = (wide, 2, groups, deep, quarter, key_columns)
    keys, token_gradient = pl.pallas_call(
        base_kernel,
        out_shape=(
            jax.ShapeDtypeStruct((rows, key_columns), bf16),
            jax.ShapeDtypeStruct((rows, depth), bf16),
        ),
        in_specs=[smem, whole()] + [whole(pltpu.HBM)] * (2 * groups + 2),
        out_specs=(whole(), whole(pltpu.HBM)),
        scratch_shapes=[
            pltpu.VMEM(blocks, bf16),
            pltpu.VMEM((rows, depth), bf16),
            pltpu.VMEM((rows, key_columns), f32),
            pltpu.VMEM((rows, key_columns), bf16),
            pltpu.VMEM((rank, width + 2 * rows), bf16),
            pltpu.SemaphoreType.DMA(blocks[:3]),
            pltpu.SemaphoreType.DMA((2 * wide,)),
            pltpu.SemaphoreType.DMA((2,)),
        ],
        compiler_params=params(58),
        cost_estimate=pl.CostEstimate(
            flops=4 * rows * depth * key_columns,
            bytes_accessed=2 * depth * key_columns + 4 * rows * width,
            transcendentals=0,
        ),
        name="base",
    )(place, tokens, cotangent, *halves, *others, adapter)
    return keys, token_gradient, jnp.swapaxes(grads, 1, 2)


def solution(mesh):
    groups, shards = mesh.devices.shape
    cores = 2
    deep = 8
    mesh = Mesh(
        mesh.devices.reshape(groups, shards // (cores * deep), deep, cores),
        ("grp", "y", "z", "core"),
    )
    every = ("grp",) + SEQ
    placed = (
        P(every, None),
        P(every, None),
        P(SEQ, None),
        P("grp", SEQ, None),
        P(),
        P(),
    )
    return jax.shard_map(
        on_device,
        mesh=mesh,
        in_specs=placed,
        out_specs=(P(every, None), P(every, None), P("grp", SEQ, None)),
        check_vma=False,
    )
```

```python
import jax
import jax.numpy as jnp
from jax import lax
from jax.experimental import pallas as pl
from jax.experimental.pallas import tpu as pltpu
from jax.sharding import Mesh
from jax.sharding import PartitionSpec as P

SEQ = ("y", "z", "core")
TILE_ROWS = 128
LANES = 128
adapter_scale = 0.5
f32 = jnp.float32
bf16 = jnp.bfloat16
NT = (((1,), (1,)), ((), ()))
TN = (((0,), (0,)), ((), ()))


def params(vmem_mib=32):
    return pltpu.CompilerParams(vmem_limit_bytes=vmem_mib * 1024 * 1024)


def pack_kernel(a_ref, o_ref):
    slots, rank, width = a_ref.shape
    tail = width - LANES
    for s in range(slots):
        o_ref[s, :rank, :] = a_ref[s, :, :LANES]
        rest = a_ref[s, :, LANES:].astype(f32)
        pieces = [rest[8 * b : 8 * b + 8, :] for b in range(LANES // tail)]
        o_ref[s, rank:, :] = jnp.concatenate(pieces, axis=1).astype(o_ref.dtype)


def pick_kernel(group_ref, job_ref, slot_ref, *refs):
    sources, (o_ref, every_ref) = refs[:-2], refs[-2:]
    tiles = o_ref.shape[0]
    count = sources[0].shape[0]
    me = group_ref[0]
    for k, source in enumerate(sources):
        every_ref[pl.ds(lax.rem(me + k, len(sources)) * count, count)] = source[...]

    def step(t, carry):
        o_ref[t] = every_ref[slot_ref[job_ref[me * tiles + t]]]
        return carry

    lax.fori_loop(0, tiles, step, 0, unroll=4)


def sum_kernel(group_ref, job_ref, slot_ref, x_ref, *refs):
    sinks, sum_ref = refs[:-1], refs[-1]
    tiles = x_ref.shape[0]
    count = sinks[0].shape[0]
    me = group_ref[0]
    sum_ref[...] = jnp.zeros_like(sum_ref)

    def step(t, carry):
        s = slot_ref[job_ref[me * tiles + t]]
        sum_ref[s] = sum_ref[s] + x_ref[t].astype(f32)
        return carry

    lax.fori_loop(0, tiles, step, 0, unroll=4)
    for k, sink in enumerate(sinks):
        sink[...] = sum_ref[pl.ds(lax.rem(me + k, len(sinks)) * count, count)].astype(sink.dtype)


def unpack_kernel(x0_ref, x1_ref, x2_ref, x3_ref, o_ref):
    slots, rank, width = o_ref.shape
    tail = width - LANES
    for s in range(slots):
        total = x0_ref[s] + (x1_ref[s].astype(f32) + x2_ref[s].astype(f32)) + x3_ref[s].astype(f32)
        o_ref[s, :, :LANES] = total[:rank]
        rest = total[rank:]
        for b in range(LANES // tail):
            o_ref[s, 8 * b : 8 * b + 8, LANES:] = rest[:, tail * b : tail * (b + 1)]


def tile_kernel(x_ref, tok_ref, cot_ref, terms_ref, at_ref, t_ref):
    shards, _, _ = x_ref.shape
    rank = at_ref.shape[0]
    depth = tok_ref.shape[1]
    width = depth + cot_ref.shape[1]
    tail = width // shards - LANES
    per = LANES // tail
    group = per * (LANES + tail)
    lane = lax.broadcasted_iota(jnp.int32, (rank, LANES), 1)
    lane8 = lax.broadcasted_iota(jnp.int32, (8, LANES), 1)

    def unpack(a, carry):
        before = None
        for j in range(per + 1):
            if j < per:
                block = x_ref[a * per + j].astype(f32)
                main = block[:rank]
                now = main if j == 0 else pltpu.roll(main, tail * j, axis=1)
            else:
                now = None
            if before is None:
                out = now
            else:
                out = jnp.where(lane >= tail * (j - 1), rest, before)
                if now is not None:
                    out = jnp.where(lane >= tail * j, now, out)
            start = pl.multiple_of(a * group + LANES * j, LANES)
            at_ref[:, pl.ds(start, LANES)] = out.astype(at_ref.dtype)
            before = now
            if j < per:
                packed = block[rank:]
                rest = jnp.concatenate(
                    [
                        packed if b == j else pltpu.roll(packed, tail * ((j - b) % per), axis=1)
                        for b in range(per)
                    ],
                    axis=0,
                )
        return carry

    lax.fori_loop(0, shards // per, unpack, 0)

    tok = tok_ref[...]
    cot = cot_ref[...]
    hidden = lax.dot_general(
        at_ref[:, :depth], tok, NT, preferred_element_type=f32
    ).astype(bf16)
    back = lax.dot_general(
        at_ref[:, depth:width], cot, NT, preferred_element_type=f32
    ).astype(bf16)
    at_ref[:, width : width + LANES] = hidden
    at_ref[:, width + LANES :] = back
    t_ref[:, :depth] = adapter_scale * jnp.dot(back, tok, preferred_element_type=f32)
    t_ref[:, depth:] = adapter_scale * jnp.dot(hidden, cot, preferred_element_type=f32)

    def pack(a, carry):
        cols = [
            t_ref[:, pl.ds(pl.multiple_of(a * group + LANES * j, LANES), LANES)]
            for j in range(per + 1)
        ]
        for j in range(per):
            main = jnp.where(lane >= tail * j, cols[j], cols[j + 1])
            if j:
                main = pltpu.roll(main, LANES - tail * j, axis=1)
            packed = jnp.zeros((8, LANES), f32)
            for b in range(per):
                piece = cols[j + 1][8 * b : 8 * b + 8]
                if b != j:
                    piece = pltpu.roll(piece, tail * ((b - j) % per), axis=1)
                packed = jnp.where(lane8 // tail == b, piece, packed)
            terms_ref[a * per + j] = jnp.concatenate([main, packed], axis=0).astype(
                terms_ref.dtype
            )
        return carry

    lax.fori_loop(0, shards // per, pack, 0)


def join_kernel(x0, x1, x2, x3, o_ref, sems):
    copies = [
        pltpu.make_async_copy(x, o_ref.at[k], sems.at[k]) for k, x in enumerate((x0, x1, x2, x3))
    ]
    for copy in copies:
        copy.start()
    for copy in copies:
        copy.wait()


def base_kernel(
    place_ref, tok_ref, cot_in, s0, s1, s2, s3, t0, t1, t2, t3, adapter_in, keys_ref, out_ref,
    w_ref, grad_ref, acc_ref, cot_ref, adapter_ref, sems, out_sems, in_sems,
):
    wide, cores, groups, deep, _, key_columns = w_ref.shape
    rows, depth = tok_ref.shape
    width = depth + key_columns
    core = place_ref[2]
    inputs = [
        pltpu.make_async_copy(cot_in, cot_ref, in_sems.at[0]),
        pltpu.make_async_copy(adapter_in, adapter_ref, in_sems.at[1]),
    ]
    for copy in inputs:
        copy.start()

    def fetch(source, back, c, k):
        g = lax.rem(place_ref[0] - k + groups, groups)
        pltpu.make_async_copy(source, w_ref.at[back, c, g], sems.at[back, c, g]).start()

    def fetch_all(along_y_first, along_y_second):
        for back in range(wide):
            for k in range(groups):
                fetch(along_y_first[k].at[back], back, 0, k)
                fetch(along_y_second[back].at[k], back, 1, k)

    @pl.when(core == 0)
    def _():
        fetch_all((s0, s1, s2, s3), (t0, t1, t2, t3))

    @pl.when(core == 1)
    def _():
        fetch_all((t0, t1, t2, t3), (s0, s1, s2, s3))

    for copy in inputs:
        copy.wait()
    hidden = adapter_ref[:, width : width + rows]
    back = adapter_ref[:, width + rows :]
    up = adapter_ref[:, depth:width]
    acc_ref[...] = adapter_scale * lax.dot_general(hidden, up, TN, preferred_element_type=f32)
    halves = 1
    span = depth // (wide * halves)
    stores = []
    for step in range(wide):
        y = lax.rem(place_ref[1] - step + wide, wide)
        for c in range(cores):
            for g in range(groups):
                pltpu.make_async_copy(s0.at[0], w_ref.at[step, c, g], sems.at[step, c, g]).wait()
        for h in range(halves):
            at = pl.ds(pl.multiple_of((y * halves + h) * span, span), span)
            weight = jnp.concatenate(
                [
                    w_ref[step, c, g, z]
                    for z in range(h * deep // halves, (h + 1) * deep // halves)
                    for c in range(cores)
                    for g in range(groups)
                ],
                axis=0,
            )
            acc_ref[...] += jnp.dot(tok_ref[:, at], weight, preferred_element_type=f32)
            grad = lax.dot_general(weight, cot_ref[...], NT, preferred_element_type=f32)
            grad += adapter_scale * lax.dot_general(
                adapter_ref[:, at], back, TN, preferred_element_type=f32
            )
            grad_ref[:, at] = grad.T.astype(grad_ref.dtype)
            store = pltpu.make_async_copy(
                grad_ref.at[:, at], out_ref.at[:, at], out_sems.at[step * halves + h]
            )
            store.start()
            stores.append(store)
    keys_ref[...] = acc_ref[...].astype(keys_ref.dtype)
    for store in stores:
        store.wait()


def shift(x, by, groups):
    return lax.ppermute(x, "grp", [(i, (i + by) % groups) for i in range(groups)])


def route(x, by, groups, wide, first):
    pairs = []
    for g in range(groups):
        for y in range(wide):
            for c in range(2):
                along_y = (c == 0) == first
                to = (g, (y + by) % wide) if along_y else ((g + by) % groups, y)
                pairs.append(((g * wide + y) * 2 + c, (to[0] * wide + to[1]) * 2 + c))
    return lax.ppermute(x, ("grp", "y", "core"), pairs)


def whole(memory=pltpu.VMEM):
    return pl.BlockSpec(memory_space=memory)


def on_device(tokens, cotangent, frozen_weight, adapters, tile_job, job_slot):
    rows, depth = tokens.shape
    key_columns = cotangent.shape[1]
    slot_count, row_count, rank = adapters.shape
    groups = lax.axis_size("grp")
    shards = lax.axis_size(SEQ)
    packed_rows = row_count * rank // LANES
    width = depth + key_columns
    group = lax.axis_index("grp").reshape(1).astype(jnp.int32)
    place = jnp.stack([lax.axis_index("grp"), lax.axis_index("y"), lax.axis_index("core")])
    place = place.astype(jnp.int32)
    jobs = tile_job.reshape(-1)

    quarter = TILE_ROWS // groups
    wide, deep = lax.axis_size("y"), lax.axis_size("z")
    mine = lax.dynamic_slice_in_dim(frozen_weight, lax.axis_index("grp") * quarter, quarter, 0)
    column = lax.all_to_all(
        jnp.broadcast_to(mine, (deep,) + mine.shape), "z", split_axis=0, concat_axis=0, tiled=True
    )
    line = pl.pallas_call(
        join_kernel,
        out_shape=jax.ShapeDtypeStruct((wide,) + column.shape, bf16),
        in_specs=[whole()] * wide,
        out_specs=whole(pltpu.HBM),
        scratch_shapes=[pltpu.SemaphoreType.DMA((wide,))],
        compiler_params=params(),
        name="join",
    )(column, *[route(column, k, groups, wide, True) for k in range(1, wide)])
    halves = [line] + [route(line, k, groups, wide, False) for k in range(1, groups)]
    others = [lax.ppermute(x, "core", [(0, 1), (1, 0)]) for x in halves]

    own = pl.pallas_call(
        pack_kernel,
        out_shape=jax.ShapeDtypeStruct((slot_count, packed_rows, LANES), bf16),
        in_specs=[whole()],
        out_specs=whole(),
        compiler_params=params(),
        name="pack",
    )(jnp.swapaxes(adapters, 1, 2))
    every = (own,) + tuple(shift(own, -k, groups) for k in range(1, groups))
    smem = whole(pltpu.SMEM)
    outgoing = pl.pallas_call(
        pick_kernel,
        out_shape=jax.ShapeDtypeStruct((shards, packed_rows, LANES), bf16),
        in_specs=[smem, smem, smem] + [whole()] * groups,
        out_specs=whole(),
        scratch_shapes=[pltpu.VMEM((groups * slot_count, packed_rows, LANES), bf16)],
        compiler_params=params(),
        name="pick",
    )(group, jobs, job_slot, *every)
    arrived = lax.all_to_all(outgoing, SEQ, split_axis=0, concat_axis=0, tiled=True)
    terms, adapter = pl.pallas_call(
        tile_kernel,
        out_shape=(
            jax.ShapeDtypeStruct((shards, packed_rows, LANES), bf16),
            jax.ShapeDtypeStruct((rank, width + 2 * rows), bf16),
        ),
        in_specs=[whole()] * 3,
        out_specs=(whole(),) * 2,
        scratch_shapes=[pltpu.VMEM((rank, width), f32)],
        compiler_params=params(32),
        name="tile",
    )(arrived, tokens, cotangent)
    incoming = lax.all_to_all(terms, SEQ, split_axis=0, concat_axis=0, tiled=True)
    incoming, others[0] = lax.optimization_barrier((incoming, others[0]))
    sums = pl.pallas_call(
        sum_kernel,
        out_shape=(jax.ShapeDtypeStruct((slot_count, packed_rows, LANES), f32),)
        + (jax.ShapeDtypeStruct((slot_count, packed_rows, LANES), bf16),) * (groups - 1),
        in_specs=[smem, smem, smem, whole()],
        out_specs=(whole(),) * groups,
        scratch_shapes=[pltpu.VMEM((groups * slot_count, packed_rows, LANES), f32)],
        compiler_params=params(),
        name="sum",
    )(group, jobs, job_slot, incoming)
    kept, halves[0] = lax.optimization_barrier((sums[0], halves[0]))
    last, others = lax.optimization_barrier((sums[-1], others))
    sums = (kept,) + tuple(sums[1:-1]) + (last,)
    owned = (sums[0],) + tuple(shift(sums[k], k, groups) for k in range(1, groups))
    grads = pl.pallas_call(
        unpack_kernel,
        out_shape=jax.ShapeDtypeStruct((slot_count, rank, row_count), f32),
        in_specs=[whole()] * groups,
        out_specs=whole(),
        compiler_params=params(),
        name="unpack",
    )(*owned)

    blocks = (wide, 2, groups, deep, quarter, key_columns)
    keys, token_gradient = pl.pallas_call(
        base_kernel,
        out_shape=(
            jax.ShapeDtypeStruct((rows, key_columns), bf16),
            jax.ShapeDtypeStruct((rows, depth), bf16),
        ),
        in_specs=[smem, whole()] + [whole(pltpu.HBM)] * (2 * groups + 2),
        out_specs=(whole(), whole(pltpu.HBM)),
        scratch_shapes=[
            pltpu.VMEM(blocks, bf16),
            pltpu.VMEM((rows, depth), bf16),
            pltpu.VMEM((rows, key_columns), f32),
            pltpu.VMEM((rows, key_columns), bf16),
            pltpu.VMEM((rank, width + 2 * rows), bf16),
            pltpu.SemaphoreType.DMA(blocks[:3]),
            pltpu.SemaphoreType.DMA((2 * wide,)),
            pltpu.SemaphoreType.DMA((2,)),
        ],
        compiler_params=params(58),
        cost_estimate=pl.CostEstimate(
            flops=4 * rows * depth * key_columns,
            bytes_accessed=2 * depth * key_columns + 4 * rows * width,
            transcendentals=0,
        ),
        name="base",
    )(place, tokens, cotangent, *halves, *others, adapter)
    return keys, token_gradient, jnp.swapaxes(grads, 1, 2)


def solution(mesh):
    groups, shards = mesh.devices.shape
    cores = 2
    deep = 8
    mesh = Mesh(
        mesh.devices.reshape(groups, shards // (cores * deep), deep, cores),
        ("grp", "y", "z", "core"),
    )
    every = ("grp",) + SEQ
    placed = (
        P(every, None),
        P(every, None),
        P(SEQ, None),
        P("grp", SEQ, None),
        P(),
        P(),
    )
    return jax.shard_map(
        on_device,
        mesh=mesh,
        in_specs=placed,
        out_specs=(P(every, None), P(every, None), P("grp", SEQ, None)),
        check_vma=False,
    )
```

```python
import jax
import jax.numpy as jnp
from jax import lax
from jax.experimental import pallas as pl
from jax.experimental.pallas import tpu as pltpu
from jax.sharding import Mesh
from jax.sharding import PartitionSpec as P

SEQ = ("y", "z", "core")
TILE_ROWS = 128
LANES = 128
adapter_scale = 0.5
f32 = jnp.float32
bf16 = jnp.bfloat16
NT = (((1,), (1,)), ((), ()))
TN = (((0,), (0,)), ((), ()))


def params(vmem_mib=32):
    return pltpu.CompilerParams(vmem_limit_bytes=vmem_mib * 1024 * 1024)


def pack_kernel(a_ref, o_ref):
    slots, rank, width = a_ref.shape
    tail = width - LANES
    for s in range(slots):
        o_ref[s, :rank, :] = a_ref[s, :, :LANES]
        rest = a_ref[s, :, LANES:].astype(f32)
        pieces = [rest[8 * b : 8 * b + 8, :] for b in range(LANES // tail)]
        o_ref[s, rank:, :] = jnp.concatenate(pieces, axis=1).astype(o_ref.dtype)


def pick_kernel(group_ref, job_ref, slot_ref, *refs):
    sources, (o_ref, every_ref) = refs[:-2], refs[-2:]
    tiles = o_ref.shape[0]
    count = sources[0].shape[0]
    me = group_ref[0]
    for k, source in enumerate(sources):
        every_ref[pl.ds(lax.rem(me + k, len(sources)) * count, count)] = source[...]

    def step(t, carry):
        o_ref[t] = every_ref[slot_ref[job_ref[me * tiles + t]]]
        return carry

    lax.fori_loop(0, tiles, step, 0, unroll=4)


def sum_kernel(group_ref, job_ref, slot_ref, x_ref, *refs):
    sinks, sum_ref = refs[:-1], refs[-1]
    tiles = x_ref.shape[0]
    count = sinks[0].shape[0]
    me = group_ref[0]
    sum_ref[...] = jnp.zeros_like(sum_ref)

    def step(t, carry):
        s = slot_ref[job_ref[me * tiles + t]]
        sum_ref[s] = sum_ref[s] + x_ref[t].astype(f32)
        return carry

    lax.fori_loop(0, tiles, step, 0, unroll=4)
    for k, sink in enumerate(sinks):
        sink[...] = sum_ref[pl.ds(lax.rem(me + k, len(sinks)) * count, count)].astype(sink.dtype)


def unpack_kernel(x0_ref, x1_ref, x2_ref, x3_ref, o_ref):
    slots, rank, width = o_ref.shape
    tail = width - LANES
    for s in range(slots):
        total = x0_ref[s] + (x1_ref[s].astype(f32) + x2_ref[s].astype(f32)) + x3_ref[s].astype(f32)
        o_ref[s, :, :LANES] = total[:rank]
        rest = total[rank:]
        for b in range(LANES // tail):
            o_ref[s, 8 * b : 8 * b + 8, LANES:] = rest[:, tail * b : tail * (b + 1)]


def tile_kernel(x_ref, tok_ref, cot_ref, terms_ref, at_ref, t_ref):
    shards, _, _ = x_ref.shape
    rank = at_ref.shape[0]
    depth = tok_ref.shape[1]
    width = depth + cot_ref.shape[1]
    tail = width // shards - LANES
    per = LANES // tail
    group = per * (LANES + tail)
    lane = lax.broadcasted_iota(jnp.int32, (rank, LANES), 1)
    lane8 = lax.broadcasted_iota(jnp.int32, (8, LANES), 1)

    def unpack(a, carry):
        before = None
        for j in range(per + 1):
            if j < per:
                block = x_ref[a * per + j].astype(f32)
                main = block[:rank]
                now = main if j == 0 else pltpu.roll(main, tail * j, axis=1)
            else:
                now = None
            if before is None:
                out = now
            else:
                out = jnp.where(lane >= tail * (j - 1), rest, before)
                if now is not None:
                    out = jnp.where(lane >= tail * j, now, out)
            start = pl.multiple_of(a * group + LANES * j, LANES)
            at_ref[:, pl.ds(start, LANES)] = out.astype(at_ref.dtype)
            before = now
            if j < per:
                packed = block[rank:]
                rest = jnp.concatenate(
                    [
                        packed if b == j else pltpu.roll(packed, tail * ((j - b) % per), axis=1)
                        for b in range(per)
                    ],
                    axis=0,
                )
        return carry

    lax.fori_loop(0, shards // per, unpack, 0)

    tok = tok_ref[...]
    cot = cot_ref[...]
    hidden = lax.dot_general(
        at_ref[:, :depth], tok, NT, preferred_element_type=f32
    ).astype(bf16)
    back = lax.dot_general(
        at_ref[:, depth:width], cot, NT, preferred_element_type=f32
    ).astype(bf16)
    at_ref[:, width : width + LANES] = hidden
    at_ref[:, width + LANES :] = back
    t_ref[:, :depth] = adapter_scale * jnp.dot(back, tok, preferred_element_type=f32)
    t_ref[:, depth:] = adapter_scale * jnp.dot(hidden, cot, preferred_element_type=f32)

    def pack(a, carry):
        cols = [
            t_ref[:, pl.ds(pl.multiple_of(a * group + LANES * j, LANES), LANES)]
            for j in range(per + 1)
        ]
        for j in range(per):
            main = jnp.where(lane >= tail * j, cols[j], cols[j + 1])
            if j:
                main = pltpu.roll(main, LANES - tail * j, axis=1)
            packed = jnp.zeros((8, LANES), f32)
            for b in range(per):
                piece = cols[j + 1][8 * b : 8 * b + 8]
                if b != j:
                    piece = pltpu.roll(piece, tail * ((b - j) % per), axis=1)
                packed = jnp.where(lane8 // tail == b, piece, packed)
            terms_ref[a * per + j] = jnp.concatenate([main, packed], axis=0).astype(
                terms_ref.dtype
            )
        return carry

    lax.fori_loop(0, shards // per, pack, 0)


def join_kernel(x0, x1, x2, x3, o_ref, sems):
    copies = [
        pltpu.make_async_copy(x, o_ref.at[k], sems.at[k]) for k, x in enumerate((x0, x1, x2, x3))
    ]
    for copy in copies:
        copy.start()
    for copy in copies:
        copy.wait()


def base_kernel(
    place_ref, tok_ref, cot_in, s0, s1, s2, s3, t0, t1, t2, t3, adapter_in, keys_ref, out_ref,
    w_ref, grad_ref, acc_ref, cot_ref, adapter_ref, sems, out_sems, in_sems,
):
    wide, cores, groups, deep, _, key_columns = w_ref.shape
    rows, depth = tok_ref.shape
    width = depth + key_columns
    core = place_ref[2]
    inputs = [
        pltpu.make_async_copy(cot_in, cot_ref, in_sems.at[0]),
        pltpu.make_async_copy(adapter_in, adapter_ref, in_sems.at[1]),
    ]
    for copy in inputs:
        copy.start()

    def fetch(source, back, c, k):
        g = lax.rem(place_ref[0] - k + groups, groups)
        pltpu.make_async_copy(source, w_ref.at[back, c, g], sems.at[back, c, g]).start()

    def fetch_all(along_y_first, along_y_second):
        for back in range(wide):
            for k in range(groups):
                fetch(along_y_first[k].at[back], back, 0, k)
                fetch(along_y_second[back].at[k], back, 1, k)

    @pl.when(core == 0)
    def _():
        fetch_all((s0, s1, s2, s3), (t0, t1, t2, t3))

    @pl.when(core == 1)
    def _():
        fetch_all((t0, t1, t2, t3), (s0, s1, s2, s3))

    for copy in inputs:
        copy.wait()
    hidden = adapter_ref[:, width : width + rows]
    back = adapter_ref[:, width + rows :]
    up = adapter_ref[:, depth:width]
    acc_ref[...] = adapter_scale * lax.dot_general(hidden, up, TN, preferred_element_type=f32)
    halves = 2
    span = depth // (wide * halves)
    stores = []
    for step in range(wide):
        y = lax.rem(place_ref[1] - step + wide, wide)
        for c in range(cores):
            for g in range(groups):
                pltpu.make_async_copy(s0.at[0], w_ref.at[step, c, g], sems.at[step, c, g]).wait()
        for h in range(halves):
            at = pl.ds(pl.multiple_of((y * halves + h) * span, span), span)
            weight = jnp.concatenate(
                [
                    w_ref[step, c, g, z]
                    for z in range(h * deep // halves, (h + 1) * deep // halves)
                    for c in range(cores)
                    for g in range(groups)
                ],
                axis=0,
            )
            acc_ref[...] += jnp.dot(tok_ref[:, at], weight, preferred_element_type=f32)
            grad = lax.dot_general(cot_ref[...], weight, NT, preferred_element_type=f32)
            grad += adapter_scale * lax.dot_general(
                back, adapter_ref[:, at], TN, preferred_element_type=f32
            )
            grad_ref[:, at] = grad.astype(grad_ref.dtype)
            store = pltpu.make_async_copy(
                grad_ref.at[:, at], out_ref.at[:, at], out_sems.at[step * halves + h]
            )
            store.start()
            stores.append(store)
    keys_ref[...] = acc_ref[...].astype(keys_ref.dtype)
    for store in stores:
        store.wait()


def shift(x, by, groups):
    return lax.ppermute(x, "grp", [(i, (i + by) % groups) for i in range(groups)])


def route(x, by, groups, wide, first):
    pairs = []
    for g in range(groups):
        for y in range(wide):
            for c in range(2):
                along_y = (c == 0) == first
                to = (g, (y + by) % wide) if along_y else ((g + by) % groups, y)
                pairs.append(((g * wide + y) * 2 + c, (to[0] * wide + to[1]) * 2 + c))
    return lax.ppermute(x, ("grp", "y", "core"), pairs)


def whole(memory=pltpu.VMEM):
    return pl.BlockSpec(memory_space=memory)


def on_device(tokens, cotangent, frozen_weight, adapters, tile_job, job_slot):
    rows, depth = tokens.shape
    key_columns = cotangent.shape[1]
    slot_count, row_count, rank = adapters.shape
    groups = lax.axis_size("grp")
    shards = lax.axis_size(SEQ)
    packed_rows = row_count * rank // LANES
    width = depth + key_columns
    group = lax.axis_index("grp").reshape(1).astype(jnp.int32)
    place = jnp.stack([lax.axis_index("grp"), lax.axis_index("y"), lax.axis_index("core")])
    place = place.astype(jnp.int32)
    jobs = tile_job.reshape(-1)

    quarter = TILE_ROWS // groups
    wide, deep = lax.axis_size("y"), lax.axis_size("z")
    mine = lax.dynamic_slice_in_dim(frozen_weight, lax.axis_index("grp") * quarter, quarter, 0)
    column = lax.all_to_all(
        jnp.broadcast_to(mine, (deep,) + mine.shape), "z", split_axis=0, concat_axis=0, tiled=True
    )
    line = pl.pallas_call(
        join_kernel,
        out_shape=jax.ShapeDtypeStruct((wide,) + column.shape, bf16),
        in_specs=[whole()] * wide,
        out_specs=whole(pltpu.HBM),
        scratch_shapes=[pltpu.SemaphoreType.DMA((wide,))],
        compiler_params=params(),
        name="join",
    )(column, *[route(column, k, groups, wide, True) for k in range(1, wide)])
    halves = [line] + [route(line, k, groups, wide, False) for k in range(1, groups)]
    others = [lax.ppermute(x, "core", [(0, 1), (1, 0)]) for x in halves]

    own = pl.pallas_call(
        pack_kernel,
        out_shape=jax.ShapeDtypeStruct((slot_count, packed_rows, LANES), bf16),
        in_specs=[whole()],
        out_specs=whole(),
        compiler_params=params(),
        name="pack",
    )(jnp.swapaxes(adapters, 1, 2))
    every = (own,) + tuple(shift(own, -k, groups) for k in range(1, groups))
    smem = whole(pltpu.SMEM)
    outgoing = pl.pallas_call(
        pick_kernel,
        out_shape=jax.ShapeDtypeStruct((shards, packed_rows, LANES), bf16),
        in_specs=[smem, smem, smem] + [whole()] * groups,
        out_specs=whole(),
        scratch_shapes=[pltpu.VMEM((groups * slot_count, packed_rows, LANES), bf16)],
        compiler_params=params(),
        name="pick",
    )(group, jobs, job_slot, *every)
    arrived = lax.all_to_all(outgoing, SEQ, split_axis=0, concat_axis=0, tiled=True)
    terms, adapter = pl.pallas_call(
        tile_kernel,
        out_shape=(
            jax.ShapeDtypeStruct((shards, packed_rows, LANES), bf16),
            jax.ShapeDtypeStruct((rank, width + 2 * rows), bf16),
        ),
        in_specs=[whole()] * 3,
        out_specs=(whole(),) * 2,
        scratch_shapes=[pltpu.VMEM((rank, width), f32)],
        compiler_params=params(32),
        name="tile",
    )(arrived, tokens, cotangent)
    incoming = lax.all_to_all(terms, SEQ, split_axis=0, concat_axis=0, tiled=True)
    incoming, others[0] = lax.optimization_barrier((incoming, others[0]))
    sums = pl.pallas_call(
        sum_kernel,
        out_shape=(jax.ShapeDtypeStruct((slot_count, packed_rows, LANES), f32),)
        + (jax.ShapeDtypeStruct((slot_count, packed_rows, LANES), bf16),) * (groups - 1),
        in_specs=[smem, smem, smem, whole()],
        out_specs=(whole(),) * groups,
        scratch_shapes=[pltpu.VMEM((groups * slot_count, packed_rows, LANES), f32)],
        compiler_params=params(),
        name="sum",
    )(group, jobs, job_slot, incoming)
    kept, halves[0] = lax.optimization_barrier((sums[0], halves[0]))
    last, others = lax.optimization_barrier((sums[-1], others))
    sums = (kept,) + tuple(sums[1:-1]) + (last,)
    owned = (sums[0],) + tuple(shift(sums[k], k, groups) for k in range(1, groups))
    grads = pl.pallas_call(
        unpack_kernel,
        out_shape=jax.ShapeDtypeStruct((slot_count, rank, row_count), f32),
        in_specs=[whole()] * groups,
        out_specs=whole(),
        compiler_params=params(),
        name="unpack",
    )(*owned)

    blocks = (wide, 2, groups, deep, quarter, key_columns)
    keys, token_gradient = pl.pallas_call(
        base_kernel,
        out_shape=(
            jax.ShapeDtypeStruct((rows, key_columns), bf16),
            jax.ShapeDtypeStruct((rows, depth), bf16),
        ),
        in_specs=[smem, whole()] + [whole(pltpu.HBM)] * (2 * groups + 2),
        out_specs=(whole(), whole(pltpu.HBM)),
        scratch_shapes=[
            pltpu.VMEM(blocks, bf16),
            pltpu.VMEM((rows, depth), bf16),
            pltpu.VMEM((rows, key_columns), f32),
            pltpu.VMEM((rows, key_columns), bf16),
            pltpu.VMEM((rank, width + 2 * rows), bf16),
            pltpu.SemaphoreType.DMA(blocks[:3]),
            pltpu.SemaphoreType.DMA((2 * wide,)),
            pltpu.SemaphoreType.DMA((2,)),
        ],
        compiler_params=params(58),
        cost_estimate=pl.CostEstimate(
            flops=4 * rows * depth * key_columns,
            bytes_accessed=2 * depth * key_columns + 4 * rows * width,
            transcendentals=0,
        ),
        name="base",
    )(place, tokens, cotangent, *halves, *others, adapter)
    return keys, token_gradient, jnp.swapaxes(grads, 1, 2)


def solution(mesh):
    groups, shards = mesh.devices.shape
    cores = 2
    deep = 8
    mesh = Mesh(
        mesh.devices.reshape(groups, shards // (cores * deep), deep, cores),
        ("grp", "y", "z", "core"),
    )
    every = ("grp",) + SEQ
    placed = (
        P(every, None),
        P(every, None),
        P(SEQ, None),
        P("grp", SEQ, None),
        P(),
        P(),
    )
    return jax.shard_map(
        on_device,
        mesh=mesh,
        in_specs=placed,
        out_specs=(P(every, None), P(every, None), P("grp", SEQ, None)),
        check_vma=False,
    )
```

```python
import jax
import jax.numpy as jnp
from jax import lax
from jax.experimental import pallas as pl
from jax.experimental.pallas import tpu as pltpu
from jax.sharding import Mesh
from jax.sharding import PartitionSpec as P

SEQ = ("y", "z", "core")
TILE_ROWS = 128
LANES = 128
adapter_scale = 0.5
f32 = jnp.float32
bf16 = jnp.bfloat16
NT = (((1,), (1,)), ((), ()))
TN = (((0,), (0,)), ((), ()))


def params(vmem_mib=32):
    return pltpu.CompilerParams(vmem_limit_bytes=vmem_mib * 1024 * 1024)


def pack_kernel(a_ref, o_ref):
    slots, rank, width = a_ref.shape
    tail = width - LANES
    for s in range(slots):
        o_ref[s, :rank, :] = a_ref[s, :, :LANES]
        rest = a_ref[s, :, LANES:].astype(f32)
        pieces = [rest[8 * b : 8 * b + 8, :] for b in range(LANES // tail)]
        o_ref[s, rank:, :] = jnp.concatenate(pieces, axis=1).astype(o_ref.dtype)


def pick_kernel(group_ref, job_ref, slot_ref, *refs):
    sources, (o_ref, every_ref) = refs[:-2], refs[-2:]
    tiles = o_ref.shape[0]
    count = sources[0].shape[0]
    me = group_ref[0]
    for k, source in enumerate(sources):
        every_ref[pl.ds(lax.rem(me + k, len(sources)) * count, count)] = source[...]

    def step(t, carry):
        o_ref[t] = every_ref[slot_ref[job_ref[me * tiles + t]]]
        return carry

    lax.fori_loop(0, tiles, step, 0, unroll=4)


def sum_kernel(group_ref, job_ref, slot_ref, x_ref, *refs):
    sinks, sum_ref = refs[:-1], refs[-1]
    tiles = x_ref.shape[0]
    count = sinks[0].shape[0]
    me = group_ref[0]
    sum_ref[...] = jnp.zeros_like(sum_ref)

    def step(t, carry):
        s = slot_ref[job_ref[me * tiles + t]]
        sum_ref[s] = sum_ref[s] + x_ref[t].astype(f32)
        return carry

    lax.fori_loop(0, tiles, step, 0, unroll=4)
    for k, sink in enumerate(sinks):
        sink[...] = sum_ref[pl.ds(lax.rem(me + k, len(sinks)) * count, count)].astype(sink.dtype)


def unpack_kernel(x0_ref, x1_ref, x2_ref, x3_ref, o_ref):
    slots, rank, width = o_ref.shape
    tail = width - LANES
    for s in range(slots):
        total = x0_ref[s] + (x1_ref[s].astype(f32) + x2_ref[s].astype(f32)) + x3_ref[s].astype(f32)
        o_ref[s, :, :LANES] = total[:rank]
        rest = total[rank:]
        for b in range(LANES // tail):
            o_ref[s, 8 * b : 8 * b + 8, LANES:] = rest[:, tail * b : tail * (b + 1)]


def tile_kernel(x_ref, tok_ref, cot_ref, terms_ref, at_ref, t_ref):
    shards, _, _ = x_ref.shape
    rank = at_ref.shape[0]
    depth = tok_ref.shape[1]
    width = depth + cot_ref.shape[1]
    tail = width // shards - LANES
    per = LANES // tail
    group = per * (LANES + tail)
    lane = lax.broadcasted_iota(jnp.int32, (rank, LANES), 1)
    lane8 = lax.broadcasted_iota(jnp.int32, (8, LANES), 1)

    def unpack(a, carry):
        before = None
        for j in range(per + 1):
            if j < per:
                block = x_ref[a * per + j].astype(f32)
                main = block[:rank]
                now = main if j == 0 else pltpu.roll(main, tail * j, axis=1)
            else:
                now = None
            if before is None:
                out = now
            else:
                out = jnp.where(lane >= tail * (j - 1), rest, before)
                if now is not None:
                    out = jnp.where(lane >= tail * j, now, out)
            start = pl.multiple_of(a * group + LANES * j, LANES)
            at_ref[:, pl.ds(start, LANES)] = out.astype(at_ref.dtype)
            before = now
            if j < per:
                packed = block[rank:]
                rest = jnp.concatenate(
                    [
                        packed if b == j else pltpu.roll(packed, tail * ((j - b) % per), axis=1)
                        for b in range(per)
                    ],
                    axis=0,
                )
        return carry

    lax.fori_loop(0, shards // per, unpack, 0)

    tok = tok_ref[...]
    cot = cot_ref[...]
    hidden = lax.dot_general(
        at_ref[:, :depth], tok, NT, preferred_element_type=f32
    ).astype(bf16)
    back = lax.dot_general(
        at_ref[:, depth:width], cot, NT, preferred_element_type=f32
    ).astype(bf16)
    at_ref[:, width : width + LANES] = hidden
    at_ref[:, width + LANES :] = back
    t_ref[:, :depth] = adapter_scale * jnp.dot(back, tok, preferred_element_type=f32)
    t_ref[:, depth:] = adapter_scale * jnp.dot(hidden, cot, preferred_element_type=f32)

    def pack(a, carry):
        cols = [
            t_ref[:, pl.ds(pl.multiple_of(a * group + LANES * j, LANES), LANES)]
            for j in range(per + 1)
        ]
        for j in range(per):
            main = jnp.where(lane >= tail * j, cols[j], cols[j + 1])
            if j:
                main = pltpu.roll(main, LANES - tail * j, axis=1)
            packed = jnp.zeros((8, LANES), f32)
            for b in range(per):
                piece = cols[j + 1][8 * b : 8 * b + 8]
                if b != j:
                    piece = pltpu.roll(piece, tail * ((b - j) % per), axis=1)
                packed = jnp.where(lane8 // tail == b, piece, packed)
            terms_ref[a * per + j] = jnp.concatenate([main, packed], axis=0).astype(
                terms_ref.dtype
            )
        return carry

    lax.fori_loop(0, shards // per, pack, 0)


def join_kernel(x0, x1, x2, x3, o_ref, sems):
    copies = [
        pltpu.make_async_copy(x, o_ref.at[k], sems.at[k]) for k, x in enumerate((x0, x1, x2, x3))
    ]
    for copy in copies:
        copy.start()
    for copy in copies:
        copy.wait()


def base_kernel(
    place_ref, tok_ref, cot_in, s0, s1, s2, s2b, s3, t0, t1, t2, t2b, t3, adapter_in, keys_ref, out_ref,
    w_ref, grad_ref, acc_ref, cot_ref, adapter_ref, sems, out_sems, in_sems,
):
    wide, cores, groups, deep, _, key_columns = w_ref.shape
    rows, depth = tok_ref.shape
    width = depth + key_columns
    core = place_ref[2]
    inputs = [
        pltpu.make_async_copy(cot_in, cot_ref, in_sems.at[0]),
        pltpu.make_async_copy(adapter_in, adapter_ref, in_sems.at[1]),
    ]
    for copy in inputs:
        copy.start()

    def fetch(source, back, c, k):
        g = lax.rem(place_ref[0] - k + groups, groups)
        pltpu.make_async_copy(source, w_ref.at[back, c, g], sems.at[back, c, g]).start()

    def piece(sources, a, b):
        first, second, low, high, last = sources
        if a == 2:
            cut = low.shape[0]
            return low.at[b] if b < cut else high.at[b - cut]
        return (first, second, None, last)[a].at[b]

    def fetch_all(along_y_first, along_y_second):
        for back in range(wide):
            for k in range(groups):
                fetch(piece(along_y_first, k, back), back, 0, k)
                fetch(piece(along_y_second, back, k), back, 1, k)

    own, swapped = (s0, s1, s2, s2b, s3), (t0, t1, t2, t2b, t3)

    @pl.when(core == 0)
    def _():
        fetch_all(own, swapped)

    @pl.when(core == 1)
    def _():
        fetch_all(swapped, own)

    for copy in inputs:
        copy.wait()
    hidden = adapter_ref[:, width : width + rows]
    back = adapter_ref[:, width + rows :]
    up = adapter_ref[:, depth:width]
    acc_ref[...] = adapter_scale * lax.dot_general(hidden, up, TN, preferred_element_type=f32)
    halves = 2
    span = depth // (wide * halves)
    stores = []
    for step in range(wide):
        y = lax.rem(place_ref[1] - step + wide, wide)
        for c in range(cores):
            for g in range(groups):
                pltpu.make_async_copy(s0.at[0], w_ref.at[step, c, g], sems.at[step, c, g]).wait()
        for h in range(halves):
            at = pl.ds(pl.multiple_of((y * halves + h) * span, span), span)
            weight = jnp.concatenate(
                [
                    w_ref[step, c, g, z]
                    for z in range(h * deep // halves, (h + 1) * deep // halves)
                    for c in range(cores)
                    for g in range(groups)
                ],
                axis=0,
            )
            acc_ref[...] += jnp.dot(tok_ref[:, at], weight, preferred_element_type=f32)
            grad = lax.dot_general(cot_ref[...], weight, NT, preferred_element_type=f32)
            grad += adapter_scale * lax.dot_general(
                back, adapter_ref[:, at], TN, preferred_element_type=f32
            )
            grad_ref[:, at] = grad.astype(grad_ref.dtype)
            store = pltpu.make_async_copy(
                grad_ref.at[:, at], out_ref.at[:, at], out_sems.at[step * halves + h]
            )
            store.start()
            stores.append(store)
    keys_ref[...] = acc_ref[...].astype(keys_ref.dtype)
    for store in stores:
        store.wait()


def shift(x, by, groups):
    return lax.ppermute(x, "grp", [(i, (i + by) % groups) for i in range(groups)])


def route(x, by, groups, wide, first):
    pairs = []
    for g in range(groups):
        for y in range(wide):
            for c in range(2):
                along_y = (c == 0) == first
                to = (g, (y + by) % wide) if along_y else ((g + by) % groups, y)
                pairs.append(((g * wide + y) * 2 + c, (to[0] * wide + to[1]) * 2 + c))
    return lax.ppermute(x, ("grp", "y", "core"), pairs)


def whole(memory=pltpu.VMEM):
    return pl.BlockSpec(memory_space=memory)


def on_device(tokens, cotangent, frozen_weight, adapters, tile_job, job_slot):
    rows, depth = tokens.shape
    key_columns = cotangent.shape[1]
    slot_count, row_count, rank = adapters.shape
    groups = lax.axis_size("grp")
    shards = lax.axis_size(SEQ)
    packed_rows = row_count * rank // LANES
    width = depth + key_columns
    group = lax.axis_index("grp").reshape(1).astype(jnp.int32)
    place = jnp.stack([lax.axis_index("grp"), lax.axis_index("y"), lax.axis_index("core")])
    place = place.astype(jnp.int32)
    jobs = tile_job.reshape(-1)

    quarter = TILE_ROWS // groups
    wide, deep = lax.axis_size("y"), lax.axis_size("z")
    mine = lax.dynamic_slice_in_dim(frozen_weight, lax.axis_index("grp") * quarter, quarter, 0)
    column = lax.all_to_all(
        jnp.broadcast_to(mine, (deep,) + mine.shape), "z", split_axis=0, concat_axis=0, tiled=True
    )
    line = pl.pallas_call(
        join_kernel,
        out_shape=jax.ShapeDtypeStruct((wide,) + column.shape, bf16),
        in_specs=[whole()] * wide,
        out_specs=whole(pltpu.HBM),
        scratch_shapes=[pltpu.SemaphoreType.DMA((wide,))],
        compiler_params=params(),
        name="join",
    )(column, *[route(column, k, groups, wide, True) for k in range(1, wide)])
    before, after = route(line, 1, groups, wide, False), route(line, groups - 1, groups, wide, False)
    cut = wide // 2
    halves = [
        line,
        before,
        route(before[:cut], 1, groups, wide, False),
        route(after[cut:], groups - 1, groups, wide, False),
        after,
    ]
    others = [lax.ppermute(x, "core", [(0, 1), (1, 0)]) for x in halves]

    own = pl.pallas_call(
        pack_kernel,
        out_shape=jax.ShapeDtypeStruct((slot_count, packed_rows, LANES), bf16),
        in_specs=[whole()],
        out_specs=whole(),
        compiler_params=params(),
        name="pack",
    )(jnp.swapaxes(adapters, 1, 2))
    every = (own,) + tuple(shift(own, -k, groups) for k in range(1, groups))
    smem = whole(pltpu.SMEM)
    outgoing = pl.pallas_call(
        pick_kernel,
        out_shape=jax.ShapeDtypeStruct((shards, packed_rows, LANES), bf16),
        in_specs=[smem, smem, smem] + [whole()] * groups,
        out_specs=whole(),
        scratch_shapes=[pltpu.VMEM((groups * slot_count, packed_rows, LANES), bf16)],
        compiler_params=params(),
        name="pick",
    )(group, jobs, job_slot, *every)
    arrived = lax.all_to_all(outgoing, SEQ, split_axis=0, concat_axis=0, tiled=True)
    terms, adapter = pl.pallas_call(
        tile_kernel,
        out_shape=(
            jax.ShapeDtypeStruct((shards, packed_rows, LANES), bf16),
            jax.ShapeDtypeStruct((rank, width + 2 * rows), bf16),
        ),
        in_specs=[whole()] * 3,
        out_specs=(whole(),) * 2,
        scratch_shapes=[pltpu.VMEM((rank, width), f32)],
        compiler_params=params(32),
        name="tile",
    )(arrived, tokens, cotangent)
    incoming = lax.all_to_all(terms, SEQ, split_axis=0, concat_axis=0, tiled=True)
    incoming, others[0] = lax.optimization_barrier((incoming, others[0]))
    sums = pl.pallas_call(
        sum_kernel,
        out_shape=(jax.ShapeDtypeStruct((slot_count, packed_rows, LANES), f32),)
        + (jax.ShapeDtypeStruct((slot_count, packed_rows, LANES), bf16),) * (groups - 1),
        in_specs=[smem, smem, smem, whole()],
        out_specs=(whole(),) * groups,
        scratch_shapes=[pltpu.VMEM((groups * slot_count, packed_rows, LANES), f32)],
        compiler_params=params(),
        name="sum",
    )(group, jobs, job_slot, incoming)
    kept, halves[0] = lax.optimization_barrier((sums[0], halves[0]))
    last, others = lax.optimization_barrier((sums[-1], others))
    sums = (kept,) + tuple(sums[1:-1]) + (last,)
    owned = (sums[0],) + tuple(shift(sums[k], k, groups) for k in range(1, groups))
    grads = pl.pallas_call(
        unpack_kernel,
        out_shape=jax.ShapeDtypeStruct((slot_count, rank, row_count), f32),
        in_specs=[whole()] * groups,
        out_specs=whole(),
        compiler_params=params(),
        name="unpack",
    )(*owned)

    blocks = (wide, 2, groups, deep, quarter, key_columns)
    keys, token_gradient = pl.pallas_call(
        base_kernel,
        out_shape=(
            jax.ShapeDtypeStruct((rows, key_columns), bf16),
            jax.ShapeDtypeStruct((rows, depth), bf16),
        ),
        in_specs=[smem, whole()] + [whole(pltpu.HBM)] * (len(halves) + len(others) + 2),
        out_specs=(whole(), whole(pltpu.HBM)),
        scratch_shapes=[
            pltpu.VMEM(blocks, bf16),
            pltpu.VMEM((rows, depth), bf16),
            pltpu.VMEM((rows, key_columns), f32),
            pltpu.VMEM((rows, key_columns), bf16),
            pltpu.VMEM((rank, width + 2 * rows), bf16),
            pltpu.SemaphoreType.DMA(blocks[:3]),
            pltpu.SemaphoreType.DMA((2 * wide,)),
            pltpu.SemaphoreType.DMA((2,)),
        ],
        compiler_params=params(58),
        cost_estimate=pl.CostEstimate(
            flops=4 * rows * depth * key_columns,
            bytes_accessed=2 * depth * key_columns + 4 * rows * width,
            transcendentals=0,
        ),
        name="base",
    )(place, tokens, cotangent, *halves, *others, adapter)
    return keys, token_gradient, jnp.swapaxes(grads, 1, 2)


def solution(mesh):
    groups, shards = mesh.devices.shape
    cores = 2
    deep = 8
    mesh = Mesh(
        mesh.devices.reshape(groups, shards // (cores * deep), deep, cores),
        ("grp", "y", "z", "core"),
    )
    every = ("grp",) + SEQ
    placed = (
        P(every, None),
        P(every, None),
        P(SEQ, None),
        P("grp", SEQ, None),
        P(),
        P(),
    )
    return jax.shard_map(
        on_device,
        mesh=mesh,
        in_specs=placed,
        out_specs=(P(every, None), P(every, None), P("grp", SEQ, None)),
        check_vma=False,
    )
```

```python
import jax
import jax.numpy as jnp
from jax import lax
from jax.experimental import pallas as pl
from jax.experimental.pallas import tpu as pltpu
from jax.sharding import Mesh
from jax.sharding import PartitionSpec as P

SEQ = ("y", "z", "core")
TILE_ROWS = 128
LANES = 128
adapter_scale = 0.5
f32 = jnp.float32
bf16 = jnp.bfloat16
NT = (((1,), (1,)), ((), ()))
TN = (((0,), (0,)), ((), ()))


def params(vmem_mib=32):
    return pltpu.CompilerParams(vmem_limit_bytes=vmem_mib * 1024 * 1024)


def pack_kernel(a_ref, o_ref):
    slots, rank, width = a_ref.shape
    tail = width - LANES
    for s in range(slots):
        o_ref[s, :rank, :] = a_ref[s, :, :LANES]
        rest = a_ref[s, :, LANES:].astype(f32)
        pieces = [rest[8 * b : 8 * b + 8, :] for b in range(LANES // tail)]
        o_ref[s, rank:, :] = jnp.concatenate(pieces, axis=1).astype(o_ref.dtype)


def pick_kernel(group_ref, job_ref, slot_ref, *refs):
    sources, (o_ref, every_ref) = refs[:-2], refs[-2:]
    tiles = o_ref.shape[0]
    count = sources[0].shape[0]
    me = group_ref[0]
    for k, source in enumerate(sources):
        every_ref[pl.ds(lax.rem(me + k, len(sources)) * count, count)] = source[...]

    def step(t, carry):
        o_ref[t] = every_ref[slot_ref[job_ref[me * tiles + t]]]
        return carry

    lax.fori_loop(0, tiles, step, 0, unroll=4)


def sum_kernel(group_ref, job_ref, slot_ref, x_ref, *refs):
    sinks, sum_ref = refs[:-1], refs[-1]
    tiles = x_ref.shape[0]
    count = sinks[0].shape[0]
    me = group_ref[0]
    sum_ref[...] = jnp.zeros_like(sum_ref)

    def step(t, carry):
        s = slot_ref[job_ref[me * tiles + t]]
        sum_ref[s] = sum_ref[s] + x_ref[t].astype(f32)
        return carry

    lax.fori_loop(0, tiles, step, 0, unroll=4)
    for k, sink in enumerate(sinks):
        sink[...] = sum_ref[pl.ds(lax.rem(me + k, len(sinks)) * count, count)].astype(sink.dtype)


def unpack_kernel(x0_ref, x1_ref, x2_ref, x3_ref, o_ref):
    slots, rank, width = o_ref.shape
    tail = width - LANES
    for s in range(slots):
        total = x0_ref[s] + (x1_ref[s].astype(f32) + x2_ref[s].astype(f32)) + x3_ref[s].astype(f32)
        o_ref[s, :, :LANES] = total[:rank]
        rest = total[rank:]
        for b in range(LANES // tail):
            o_ref[s, 8 * b : 8 * b + 8, LANES:] = rest[:, tail * b : tail * (b + 1)]


def tile_kernel(x_ref, tok_ref, cot_ref, at_ref):
    shards, _, _ = x_ref.shape
    rank = at_ref.shape[0]
    depth = tok_ref.shape[1]
    width = depth + cot_ref.shape[1]
    tail = width // shards - LANES
    per = LANES // tail
    group = per * (LANES + tail)
    lane = lax.broadcasted_iota(jnp.int32, (rank, LANES), 1)

    def unpack(a, carry):
        before = None
        for j in range(per + 1):
            if j < per:
                block = x_ref[a * per + j].astype(f32)
                main = block[:rank]
                now = main if j == 0 else pltpu.roll(main, tail * j, axis=1)
            else:
                now = None
            if before is None:
                out = now
            else:
                out = jnp.where(lane >= tail * (j - 1), rest, before)
                if now is not None:
                    out = jnp.where(lane >= tail * j, now, out)
            start = pl.multiple_of(a * group + LANES * j, LANES)
            at_ref[:, pl.ds(start, LANES)] = out.astype(at_ref.dtype)
            before = now
            if j < per:
                packed = block[rank:]
                rest = jnp.concatenate(
                    [
                        packed if b == j else pltpu.roll(packed, tail * ((j - b) % per), axis=1)
                        for b in range(per)
                    ],
                    axis=0,
                )
        return carry

    lax.fori_loop(0, shards // per, unpack, 0)

    tok = tok_ref[...]
    cot = cot_ref[...]
    hidden = lax.dot_general(
        at_ref[:, :depth], tok, NT, preferred_element_type=f32
    ).astype(bf16)
    back = lax.dot_general(
        at_ref[:, depth:width], cot, NT, preferred_element_type=f32
    ).astype(bf16)
    at_ref[:, width : width + LANES] = hidden
    at_ref[:, width + LANES :] = back


def terms_kernel(at_ref, tok_ref, cot_ref, terms_ref, t_ref):
    shards = terms_ref.shape[0]
    rank, width = t_ref.shape
    depth = tok_ref.shape[1]
    tail = width // shards - LANES
    per = LANES // tail
    group = per * (LANES + tail)
    lane = lax.broadcasted_iota(jnp.int32, (rank, LANES), 1)
    lane8 = lax.broadcasted_iota(jnp.int32, (8, LANES), 1)
    hidden = at_ref[:, width : width + LANES]
    back = at_ref[:, width + LANES :]
    t_ref[:, :depth] = adapter_scale * jnp.dot(back, tok_ref[...], preferred_element_type=f32)
    t_ref[:, depth:] = adapter_scale * jnp.dot(hidden, cot_ref[...], preferred_element_type=f32)

    def pack(a, carry):
        cols = [
            t_ref[:, pl.ds(pl.multiple_of(a * group + LANES * j, LANES), LANES)]
            for j in range(per + 1)
        ]
        for j in range(per):
            main = jnp.where(lane >= tail * j, cols[j], cols[j + 1])
            if j:
                main = pltpu.roll(main, LANES - tail * j, axis=1)
            packed = jnp.zeros((8, LANES), f32)
            for b in range(per):
                piece = cols[j + 1][8 * b : 8 * b + 8]
                if b != j:
                    piece = pltpu.roll(piece, tail * ((b - j) % per), axis=1)
                packed = jnp.where(lane8 // tail == b, piece, packed)
            terms_ref[a * per + j] = jnp.concatenate([main, packed], axis=0).astype(
                terms_ref.dtype
            )
        return carry

    lax.fori_loop(0, shards // per, pack, 0)


def join_kernel(x0, x1, x2, x3, o_ref, sems):
    copies = [
        pltpu.make_async_copy(x, o_ref.at[k], sems.at[k]) for k, x in enumerate((x0, x1, x2, x3))
    ]
    for copy in copies:
        copy.start()
    for copy in copies:
        copy.wait()


def base_kernel(
    place_ref, tok_ref, cot_in, s0, s1, s2, s2b, s3, t0, t1, t2, t2b, t3, adapter_in, keys_ref, out_ref,
    w_ref, grad_ref, acc_ref, cot_ref, adapter_ref, sems, out_sems, in_sems,
):
    wide, cores, groups, deep, _, key_columns = w_ref.shape
    rows, depth = tok_ref.shape
    width = depth + key_columns
    core = place_ref[2]
    inputs = [
        pltpu.make_async_copy(cot_in, cot_ref, in_sems.at[0]),
        pltpu.make_async_copy(adapter_in, adapter_ref, in_sems.at[1]),
    ]
    for copy in inputs:
        copy.start()

    def fetch(source, back, c, k):
        g = lax.rem(place_ref[0] - k + groups, groups)
        pltpu.make_async_copy(source, w_ref.at[back, c, g], sems.at[back, c, g]).start()

    def piece(sources, a, b):
        first, second, low, high, last = sources
        if a == 2:
            cut = low.shape[0]
            return low.at[b] if b < cut else high.at[b - cut]
        return (first, second, None, last)[a].at[b]

    def fetch_all(along_y_first, along_y_second):
        for back in range(wide):
            for k in range(groups):
                fetch(piece(along_y_first, k, back), back, 0, k)
                fetch(piece(along_y_second, back, k), back, 1, k)

    own, swapped = (s0, s1, s2, s2b, s3), (t0, t1, t2, t2b, t3)

    @pl.when(core == 0)
    def _():
        fetch_all(own, swapped)

    @pl.when(core == 1)
    def _():
        fetch_all(swapped, own)

    for copy in inputs:
        copy.wait()
    hidden = adapter_ref[:, width : width + rows]
    back = adapter_ref[:, width + rows :]
    up = adapter_ref[:, depth:width]
    acc_ref[...] = adapter_scale * lax.dot_general(hidden, up, TN, preferred_element_type=f32)
    halves = 2
    span = depth // (wide * halves)
    stores = []
    for step in range(wide):
        y = lax.rem(place_ref[1] - step + wide, wide)
        for c in range(cores):
            for g in range(groups):
                pltpu.make_async_copy(s0.at[0], w_ref.at[step, c, g], sems.at[step, c, g]).wait()
        for h in range(halves):
            at = pl.ds(pl.multiple_of((y * halves + h) * span, span), span)
            weight = jnp.concatenate(
                [
                    w_ref[step, c, g, z]
                    for z in range(h * deep // halves, (h + 1) * deep // halves)
                    for c in range(cores)
                    for g in range(groups)
                ],
                axis=0,
            )
            acc_ref[...] += jnp.dot(tok_ref[:, at], weight, preferred_element_type=f32)
            grad = lax.dot_general(cot_ref[...], weight, NT, preferred_element_type=f32)
            grad += adapter_scale * lax.dot_general(
                back, adapter_ref[:, at], TN, preferred_element_type=f32
            )
            grad_ref[:, at] = grad.astype(grad_ref.dtype)
            store = pltpu.make_async_copy(
                grad_ref.at[:, at], out_ref.at[:, at], out_sems.at[step * halves + h]
            )
            store.start()
            stores.append(store)
    keys_ref[...] = acc_ref[...].astype(keys_ref.dtype)
    for store in stores:
        store.wait()


def shift(x, by, groups):
    return lax.ppermute(x, "grp", [(i, (i + by) % groups) for i in range(groups)])


def route(x, by, groups, wide, first):
    pairs = []
    for g in range(groups):
        for y in range(wide):
            for c in range(2):
                along_y = (c == 0) == first
                to = (g, (y + by) % wide) if along_y else ((g + by) % groups, y)
                pairs.append(((g * wide + y) * 2 + c, (to[0] * wide + to[1]) * 2 + c))
    return lax.ppermute(x, ("grp", "y", "core"), pairs)


def whole(memory=pltpu.VMEM):
    return pl.BlockSpec(memory_space=memory)


def on_device(tokens, cotangent, frozen_weight, adapters, tile_job, job_slot):
    rows, depth = tokens.shape
    key_columns = cotangent.shape[1]
    slot_count, row_count, rank = adapters.shape
    groups = lax.axis_size("grp")
    shards = lax.axis_size(SEQ)
    packed_rows = row_count * rank // LANES
    width = depth + key_columns
    group = lax.axis_index("grp").reshape(1).astype(jnp.int32)
    place = jnp.stack([lax.axis_index("grp"), lax.axis_index("y"), lax.axis_index("core")])
    place = place.astype(jnp.int32)
    jobs = tile_job.reshape(-1)

    quarter = TILE_ROWS // groups
    wide, deep = lax.axis_size("y"), lax.axis_size("z")
    mine = lax.dynamic_slice_in_dim(frozen_weight, lax.axis_index("grp") * quarter, quarter, 0)
    column = lax.all_to_all(
        jnp.broadcast_to(mine, (deep,) + mine.shape), "z", split_axis=0, concat_axis=0, tiled=True
    )
    line = pl.pallas_call(
        join_kernel,
        out_shape=jax.ShapeDtypeStruct((wide,) + column.shape, bf16),
        in_specs=[whole()] * wide,
        out_specs=whole(pltpu.HBM),
        scratch_shapes=[pltpu.SemaphoreType.DMA((wide,))],
        compiler_params=params(),
        name="join",
    )(column, *[route(column, k, groups, wide, True) for k in range(1, wide)])
    before, after = route(line, 1, groups, wide, False), route(line, groups - 1, groups, wide, False)
    cut = wide // 2
    halves = [
        line,
        before,
        route(before[:cut], 1, groups, wide, False),
        route(after[cut:], groups - 1, groups, wide, False),
        after,
    ]
    others = [lax.ppermute(x, "core", [(0, 1), (1, 0)]) for x in halves]

    own = pl.pallas_call(
        pack_kernel,
        out_shape=jax.ShapeDtypeStruct((slot_count, packed_rows, LANES), bf16),
        in_specs=[whole()],
        out_specs=whole(),
        compiler_params=params(),
        name="pack",
    )(jnp.swapaxes(adapters, 1, 2))
    every = (own,) + tuple(shift(own, -k, groups) for k in range(1, groups))
    smem = whole(pltpu.SMEM)
    outgoing = pl.pallas_call(
        pick_kernel,
        out_shape=jax.ShapeDtypeStruct((shards, packed_rows, LANES), bf16),
        in_specs=[smem, smem, smem] + [whole()] * groups,
        out_specs=whole(),
        scratch_shapes=[pltpu.VMEM((groups * slot_count, packed_rows, LANES), bf16)],
        compiler_params=params(),
        name="pick",
    )(group, jobs, job_slot, *every)
    arrived = lax.all_to_all(outgoing, SEQ, split_axis=0, concat_axis=0, tiled=True)
    adapter = pl.pallas_call(
        tile_kernel,
        out_shape=jax.ShapeDtypeStruct((rank, width + 2 * rows), bf16),
        in_specs=[whole()] * 3,
        out_specs=whole(),
        compiler_params=params(),
        name="tile",
    )(arrived, tokens, cotangent)
    terms = pl.pallas_call(
        terms_kernel,
        out_shape=jax.ShapeDtypeStruct((shards, packed_rows, LANES), bf16),
        in_specs=[whole()] * 3,
        out_specs=whole(),
        scratch_shapes=[pltpu.VMEM((rank, width), f32)],
        compiler_params=params(),
        name="terms",
    )(adapter, tokens, cotangent)
    incoming = lax.all_to_all(terms, SEQ, split_axis=0, concat_axis=0, tiled=True)
    incoming, others[0] = lax.optimization_barrier((incoming, others[0]))
    sums = pl.pallas_call(
        sum_kernel,
        out_shape=(jax.ShapeDtypeStruct((slot_count, packed_rows, LANES), f32),)
        + (jax.ShapeDtypeStruct((slot_count, packed_rows, LANES), bf16),) * (groups - 1),
        in_specs=[smem, smem, smem, whole()],
        out_specs=(whole(),) * groups,
        scratch_shapes=[pltpu.VMEM((groups * slot_count, packed_rows, LANES), f32)],
        compiler_params=params(),
        name="sum",
    )(group, jobs, job_slot, incoming)
    kept, halves[0] = lax.optimization_barrier((sums[0], halves[0]))
    last, others = lax.optimization_barrier((sums[-1], others))
    sums = (kept,) + tuple(sums[1:-1]) + (last,)
    owned = (sums[0],) + tuple(shift(sums[k], k, groups) for k in range(1, groups))
    grads = pl.pallas_call(
        unpack_kernel,
        out_shape=jax.ShapeDtypeStruct((slot_count, rank, row_count), f32),
        in_specs=[whole()] * groups,
        out_specs=whole(),
        compiler_params=params(),
        name="unpack",
    )(*owned)

    blocks = (wide, 2, groups, deep, quarter, key_columns)
    keys, token_gradient = pl.pallas_call(
        base_kernel,
        out_shape=(
            jax.ShapeDtypeStruct((rows, key_columns), bf16),
            jax.ShapeDtypeStruct((rows, depth), bf16),
        ),
        in_specs=[smem, whole()] + [whole(pltpu.HBM)] * (len(halves) + len(others) + 2),
        out_specs=(whole(), whole(pltpu.HBM)),
        scratch_shapes=[
            pltpu.VMEM(blocks, bf16),
            pltpu.VMEM((rows, depth), bf16),
            pltpu.VMEM((rows, key_columns), f32),
            pltpu.VMEM((rows, key_columns), bf16),
            pltpu.VMEM((rank, width + 2 * rows), bf16),
            pltpu.SemaphoreType.DMA(blocks[:3]),
            pltpu.SemaphoreType.DMA((2 * wide,)),
            pltpu.SemaphoreType.DMA((2,)),
        ],
        compiler_params=params(58),
        cost_estimate=pl.CostEstimate(
            flops=4 * rows * depth * key_columns,
            bytes_accessed=2 * depth * key_columns + 4 * rows * width,
            transcendentals=0,
        ),
        name="base",
    )(place, tokens, cotangent, *halves, *others, adapter)
    return keys, token_gradient, jnp.swapaxes(grads, 1, 2)


def solution(mesh):
    groups, shards = mesh.devices.shape
    cores = 2
    deep = 8
    mesh = Mesh(
        mesh.devices.reshape(groups, shards // (cores * deep), deep, cores),
        ("grp", "y", "z", "core"),
    )
    every = ("grp",) + SEQ
    placed = (
        P(every, None),
        P(every, None),
        P(SEQ, None),
        P("grp", SEQ, None),
        P(),
        P(),
    )
    return jax.shard_map(
        on_device,
        mesh=mesh,
        in_specs=placed,
        out_specs=(P(every, None), P(every, None), P("grp", SEQ, None)),
        check_vma=False,
    )
```
